256 devices in a mesh: rows: 32 (over x, z_lo, core), marg: 8 (over y, z_hi).
Axes of the slice: x: 4, y: 4, z: 8 (z_hi: 2, z_lo: 4; z = z_hi * 4 + z_lo), core: 2. Of those that a mesh axis runs over, the one named last changes fastest.
Arguments:
- logits: float32 [4096, 2048], P('rows', 'marg'), may hold values from -12 to 320
- first_moment: float32 [4096, 2048], P('rows', 'marg'), may hold values from -3 to 3
- second_moment: float32 [4096, 2048], P('rows', 'marg'), may hold values from 0.002 to 0.016
- targets: float32 [128, 32768], P('marg'), may hold values from 0 to 2
- triples: int32 [128, 3], P('marg'), may hold values from 0 to 63, as said below
Outputs:
- new_logits: float32 [4096, 2048], P('rows', 'marg')
- new_first: float32 [4096, 2048], P('rows', 'marg')
- new_second: float32 [4096, 2048], P('rows', 'marg')
The draws below stay inside these ranges and needn't reach their ends.
Inputs may be any that keep to these rules, and one draw needn't show every extreme that they name: `triples`: the three attributes of a marginal are different.
All inputs are finite; a program needn't handle non-finite values.
Results may differ from the reference program's by a relative error of at most 0.0099.
Values may be sent and summed in bfloat16 or wider, within the bound.
No kernel may reach another device: no remote copies, remote signals or barrier semaphores. Data moves between devices by JAX's collectives and lax.ppermute only.
A program may use at most 64 MiB of HBM per device.

```python
import math
import jax
import jax.numpy as jnp
from jax import lax

V = 32
K = 64
ADAM_STEP = 4
COLS = 2048
CELLS = 32768
ROWS = 4096
MARGS = 128


def draw_logits(key, part):
    key = jax.random.fold_in(key, 5)
    key_base = jax.random.fold_in(key, 0)
    base = jnp.clip(2.0 * jax.random.normal(key_base, (ROWS, COLS), jnp.float32), -12.0, 12.0)
    return base


def draw_triples(key, part):
    key = jax.random.fold_in(key, 11)
    key_first, key_step, key_other = jax.random.split(key, 3)
    first = jax.random.randint(key_first, (MARGS,), 0, K)
    step_one = jax.random.randint(key_step, (MARGS,), 1, K)
    step_two = jax.random.randint(key_other, (MARGS,), 1, K - 1)
    second = (first + step_one) % K
    offset = 1 + (step_one - 1 + step_two) % (K - 1)
    third = (first + offset) % K
    return jnp.stack([first, second, third], axis=1).astype(jnp.int32)


def level_of(own_key, shape, cuts, smallest, high):
    level, own = 1.0, jax.random.fold_in(own_key, 6)
    for position, blocks in cuts:
        draws = jnp.exp(jax.random.uniform(jax.random.fold_in(own, position), (blocks,), jnp.float32, smallest / len(cuts), high / len(cuts)))
        level = level * jnp.repeat(draws, shape[position] // blocks).reshape([-1 if axis == position else 1 for axis in range(len(shape))])
    return level


def normal_values(key, dims, spread, most, cuts=(), kind=jnp.bfloat16):
    factor_of = level_of(key, dims, cuts, -0.22, 0.18) if cuts else 1.0
    result = jax.random.normal(key, dims, jnp.float32) * spread * factor_of
    return jnp.minimum(jnp.maximum(result, -most), most).astype(kind)


def setup_inputs(seed: int = 0) -> dict:
    streams_of = jax.random.split(jax.random.key(seed), 6)
    return {
        "logits": draw_logits(jax.random.fold_in(streams_of[5], 71), 0),
        "first_moment": normal_values(streams_of[1], (ROWS, COLS), 0.5, 3.0, ((0, 32), (1, 8)), jnp.float32),
        "second_moment": jnp.clip(jnp.exp(math.log(0.016) - 2.0794415 * jax.random.uniform(streams_of[2], (ROWS, COLS), jnp.float32) ** level_of(streams_of[2], (ROWS, COLS), ((0, 32), (1, 8)), -0.2, 0.2)), 0.002, 0.016),
        "targets": jnp.clip(2.0 * jax.random.uniform(streams_of[3], (MARGS, CELLS), jnp.float32) ** level_of(streams_of[3], (MARGS, CELLS), ((0, 8),), -0.2, 0.2), 0.0, 2.0),
        "triples": draw_triples(jax.random.fold_in(streams_of[5], 71), 0),
    }


def relax(logits):
    shaped = logits.reshape(logits.shape[0], -1, V)
    top = lax.optimization_barrier(jnp.max(shaped, axis=2, keepdims=True))
    expo = jnp.exp(shaped - top)
    return (expo / lax.optimization_barrier(jnp.sum(expo, axis=2, keepdims=True))).reshape(logits.shape)

def pick(full, index):
    return lax.dynamic_slice_in_dim(full, (index * V).astype(jnp.int32), V, 1)

def pairing(left, right):
    both = left.astype(jnp.float32)[:, :, None] * right.astype(jnp.float32)[:, None, :]
    return both.reshape(left.shape[0], V * V).astype(jnp.bfloat16)

def add_cols(total, index, term):
    start = (index * V).astype(jnp.int32)
    current = lax.dynamic_slice_in_dim(total, start, V, 1)
    return lax.dynamic_update_slice_in_dim(total, current + term, start, 1)

def reference(logits, first_moment, second_moment, targets, triples):
    probs = relax(logits)
    probs_low = probs.astype(jnp.bfloat16)
    scale = CELLS / ROWS

    def answer(carry, triple):
        first_cols = pick(probs_low, triple[0])
        second_cols = pick(probs_low, triple[1])
        third_cols = pick(probs_low, triple[2])
        pairs = pairing(first_cols, second_cols)
        total = lax.dot_general(pairs, third_cols, (((0,), (0,)), ((), ())), preferred_element_type=jnp.float32)
        return (carry, total.reshape(CELLS))
    unused, answers = lax.scan(answer, 0.0, triples)
    resid = (scale * answers - targets).astype(jnp.bfloat16)

    def backward(total, inputs):
        triple, resid_row = inputs
        first_cols = pick(probs_low, triple[0])
        second_cols = pick(probs_low, triple[1])
        third_cols = pick(probs_low, triple[2])
        pairs = pairing(first_cols, second_cols)
        table = resid_row.reshape(V * V, V)
        third_grad = jnp.dot(pairs, table, preferred_element_type=jnp.float32)
        cross = lax.dot_general(third_cols, table, (((1,), (1,)), ((), ())), preferred_element_type=jnp.float32)
        cross = cross.reshape(-1, V, V)
        first_grad = jnp.einsum('rij,rj->ri', cross, second_cols.astype(jnp.float32))
        second_grad = jnp.einsum('rij,ri->rj', cross, first_cols.astype(jnp.float32))
        total = add_cols(total, triple[0], first_grad)
        total = add_cols(total, triple[1], second_grad)
        total = add_cols(total, triple[2], third_grad)
        return (total, 0.0)
    row_grad, unused2 = lax.scan(backward, jnp.zeros(logits.shape, jnp.float32), (triples, resid))
    shaped_p = probs.reshape(ROWS, K, V)
    shaped_h = row_grad.reshape(ROWS, K, V)
    inner = lax.optimization_barrier(jnp.sum(shaped_p * shaped_h, axis=2, keepdims=True))
    grad = (512.0 * shaped_p * (shaped_h - inner)).reshape(ROWS, COLS)
    new_first = 0.9 * first_moment + 0.1 * grad
    new_second = 0.999 * second_moment + 0.001 * grad * grad
    first_hat = new_first / (1.0 - 0.9 ** ADAM_STEP)
    second_hat = new_second / (1.0 - 0.999 ** ADAM_STEP)
    new_logits = logits - 0.5 * first_hat / (jnp.sqrt(second_hat) + 1e-08)
    return (new_logits, new_first, new_second)
```

```python
import jax
import jax.numpy as jnp
from jax import lax
from jax.experimental import pallas as pl
from jax.experimental.pallas import tpu as pltpu
from jax.sharding import Mesh, PartitionSpec as P

V = 32
ADAM_STEP = 4
PARTS = (4, 2, 2, 2, 4, 2)
NAMES = ("x", "u", "w", "c", "y", "h")
ROW_AXES = ("x", "u", "w", "c")
MARG_AXES = ("y", "h")
SHARE_AXES = ("x", "w", "c")
MODS = 4
VMEM = pl.BlockSpec(memory_space=pltpu.VMEM)
SMEM = pl.BlockSpec(memory_space=pltpu.SMEM)
LIMIT = 48 * 1024 * 1024


def call(body, out_shape, operands, specs, scratch=()):
    return pl.pallas_call(
        body,
        out_shape=out_shape,
        in_specs=specs,
        out_specs=jax.tree.map(lambda unused: VMEM, out_shape),
        scratch_shapes=scratch,
        compiler_params=pltpu.CompilerParams(vmem_limit_bytes=LIMIT),
    )(*operands)


def relax_kernel(logits_ref, probs_ref, send_ref):
    flipped = logits_ref[...].T
    copies = send_ref.shape[0]
    for attr in range(probs_ref.shape[0]):
        block = flipped[attr * V : (attr + 1) * V, :]
        top = jnp.max(block, axis=0, keepdims=True)
        expo = jnp.exp(block - top)
        probs = expo / jnp.sum(expo, axis=0, keepdims=True)
        probs_ref[attr] = probs
        low = probs.astype(jnp.bfloat16)
        for copy in range(copies):
            send_ref[copy, attr] = low


def select_kernel(triples_ref, full_ref, send_ref):
    for marg in range(send_ref.shape[0]):
        for which in range(3):
            send_ref[marg, which] = full_ref[triples_ref[marg, which]]


def fill_pairs(src_ref, source, lanes, pairs_ref, first_ref, second_ref):
    first_ref[...] = src_ref[source, 0].astype(jnp.float32)
    second_ref[...] = src_ref[source, 1].astype(jnp.float32)
    first = first_ref[...]
    for mod in range(MODS):
        second = second_ref[pl.ds(mod, V // MODS, stride=MODS), :]
        both = first[:, None, :] * second[None, :, :]
        pairs_ref[mod, :, lanes] = both.reshape(V * V // MODS, both.shape[2]).astype(jnp.bfloat16)


def answer_kernel(src_ref, own_ref, send_ref, pairs_ref, third_ref, first_ref, second_ref):
    sources, unused, unused2, rows = src_ref.shape

    def fill(source, carry):
        lanes = pl.ds(pl.multiple_of(source * rows, rows), rows)
        fill_pairs(src_ref, source, lanes, pairs_ref, first_ref, second_ref)
        third_ref[:, lanes] = src_ref[source, 2]
        return carry

    lax.fori_loop(0, sources, fill, 0)
    for mod in range(MODS):
        part = lax.dot_general(
            third_ref[...], pairs_ref[mod], (((1,), (1,)), ((), ())), preferred_element_type=jnp.float32
        )
        own_ref[mod * V : (mod + 1) * V, :] = part
        send_ref[mod * V : (mod + 1) * V, :] = part.astype(jnp.bfloat16)


def backward_kernel(
    scale, src_ref, own_ref, other_ref, target_ref, out_ref, low_ref, mask_ref, pairs_ref, first_ref, second_ref, cross_ref, grad_ref
):
    sources, unused, unused2, rows = src_ref.shape
    total = own_ref[...] + other_ref[...].astype(jnp.float32)
    resid = scale * total - target_ref[...].T
    low_ref[...] = resid.astype(jnp.bfloat16)
    flipped = resid.T
    lane_mod = lax.broadcasted_iota(jnp.int32, flipped.shape, 1) // V
    for mod in range(MODS):
        mask_ref[mod] = jnp.where(lane_mod == mod, flipped, 0.0).astype(jnp.bfloat16)

    def step(source, carry):
        fill_pairs(src_ref, source, slice(None), pairs_ref, first_ref, second_ref)
        third = src_ref[source, 2]
        stacked = jnp.concatenate([third] * MODS, axis=0)
        third_grad = jnp.zeros(third.shape, jnp.float32)
        first = first_ref[...]
        first_sum = jnp.zeros((V, V // MODS, rows), jnp.float32)
        for mod in range(MODS):
            third_grad += jnp.dot(
                low_ref[mod * V : (mod + 1) * V, :], pairs_ref[mod], preferred_element_type=jnp.float32
            )
            cross = jnp.dot(mask_ref[mod], stacked, preferred_element_type=jnp.float32)
            cross = cross.reshape(V, V // MODS, rows)
            second = second_ref[pl.ds(mod, V // MODS, stride=MODS), :]
            first_sum += cross * second[None, :, :]
            grad_ref[pl.ds(mod, V // MODS, stride=MODS), :] = jnp.sum(cross * first[:, None, :], axis=0)
        cross_ref[...] = first_sum.reshape(V * V // MODS, rows)
        first_grad = jnp.zeros((V, rows), jnp.float32)
        for part in range(V // MODS):
            first_grad += cross_ref[pl.ds(part, V, stride=V // MODS), :]
        out_ref[source, 0] = first_grad.astype(jnp.bfloat16)
        out_ref[source, 1] = grad_ref[...].astype(jnp.bfloat16)
        out_ref[source, 2] = third_grad.astype(jnp.bfloat16)
        return carry

    lax.fori_loop(0, sources, step, 0)


def collect_kernel(triples_ref, grads_ref, send_ref, total_ref):
    total_ref[...] = jnp.zeros(total_ref.shape, jnp.float32)
    for marg in range(grads_ref.shape[0]):
        for which in range(3):
            attr = triples_ref[marg, which]
            total_ref[attr] = total_ref[attr] + grads_ref[marg, which].astype(jnp.float32)
    send_ref[...] = total_ref[...].astype(jnp.bfloat16)


def adam_kernel(
    parts_ref, probs_ref, logits_ref, first_ref, second_ref, out_logits_ref, out_first_ref, out_second_ref
):
    row_grad = parts_ref[0].astype(jnp.float32)
    for part in range(1, parts_ref.shape[0]):
        row_grad += parts_ref[part].astype(jnp.float32)
    probs = probs_ref[...]
    inner = jnp.sum(probs * row_grad, axis=1, keepdims=True)
    grad = 512.0 * probs * (row_grad - inner)
    grad = grad.reshape(grad.shape[0] * V, grad.shape[2]).T
    new_first = 0.9 * first_ref[...] + 0.1 * grad
    new_second = 0.999 * second_ref[...] + 0.001 * grad * grad
    first_hat = new_first / (1.0 - 0.9**ADAM_STEP)
    second_hat = new_second / (1.0 - 0.999**ADAM_STEP)
    out_logits_ref[...] = logits_ref[...] - 0.5 * first_hat / (jnp.sqrt(second_hat) + 1e-08)
    out_first_ref[...] = new_first
    out_second_ref[...] = new_second


def swap(value, axes):
    return lax.all_to_all(value, axes, 0, 0, tiled=True)


def shards(logits, first_moment, second_moment, targets, triples):
    rows, cols = logits.shape
    margs, cells = targets.shape
    attrs = cols // V
    groups = lax.axis_size(MARG_AXES)
    scale = cells / (rows * lax.axis_size(ROW_AXES))
    f32, low = jnp.float32, jnp.bfloat16
    shape = jax.ShapeDtypeStruct
    probs, copies = call(
        relax_kernel,
        (shape((attrs, V, rows), f32), shape((groups, attrs, V, rows), low)),
        (logits,),
        [VMEM],
    )
    full = swap(copies, MARG_AXES).reshape(groups * attrs, V, rows)
    picked = call(select_kernel, shape((margs, 3, V, rows), low), (triples, full), [SMEM, VMEM])
    sources = swap(picked, SHARE_AXES)
    tall, wide = V * V // MODS, V * MODS
    own, send = call(
        answer_kernel,
        (shape((wide, tall), f32), shape((wide, tall), low)),
        (sources,),
        [VMEM],
        [
            pltpu.VMEM((MODS, tall, margs * rows), low),
            pltpu.VMEM((V, margs * rows), low),
            pltpu.VMEM((V, rows), f32),
            pltpu.VMEM((V, rows), f32),
        ],
    )
    other = lax.ppermute(send, "u", [(0, 1), (1, 0)])
    place = lax.axis_index(SHARE_AXES)
    target = lax.dynamic_slice_in_dim(targets, place, 1, 0).reshape(tall, wide)
    grads = call(
        lambda *refs: backward_kernel(scale, *refs),
        shape((margs, 3, V, rows), low),
        (sources, own, other, target),
        [VMEM] * 4,
        [
            pltpu.VMEM((wide, tall), low),
            pltpu.VMEM((MODS, tall, wide), low),
            pltpu.VMEM((MODS, tall, rows), low),
            pltpu.VMEM((V, rows), f32),
            pltpu.VMEM((V, rows), f32),
            pltpu.VMEM((tall, rows), f32),
            pltpu.VMEM((V, rows), f32),
        ],
    )
    returned = swap(grads, SHARE_AXES)
    totals = call(
        collect_kernel,
        shape((groups * attrs, V, rows), low),
        (triples, returned),
        [SMEM, VMEM],
        [pltpu.VMEM((groups * attrs, V, rows), f32)],
    )
    parts = swap(totals.reshape(groups, attrs, V, rows), MARG_AXES)
    return call(
        adam_kernel,
        (shape((rows, cols), f32),) * 3,
        (parts, probs, logits, first_moment, second_moment),
        [VMEM] * 5,
    )


def solution(mesh):
    fine = Mesh(mesh.devices.reshape(PARTS), NAMES)
    table = P(ROW_AXES, MARG_AXES)
    listed = P(MARG_AXES, None)
    return jax.shard_map(
        shards,
        mesh=fine,
        in_specs=(table, table, table, listed, listed),
        out_specs=(table, table, table),
        check_vma=False,
    )
```

```python
import jax
import jax.numpy as jnp
from jax import lax
from jax.experimental import pallas as pl
from jax.experimental.pallas import tpu as pltpu
from jax.sharding import Mesh, PartitionSpec as P

V = 32
ADAM_STEP = 4
PARTS = (4, 2, 2, 2, 4, 2)
NAMES = ("x", "u", "w", "c", "y", "h")
ROW_AXES = ("x", "u", "w", "c")
MARG_AXES = ("y", "h")
SHARE_AXES = ("x", "w", "c")
MODS = 4
VMEM = pl.BlockSpec(memory_space=pltpu.VMEM)
SMEM = pl.BlockSpec(memory_space=pltpu.SMEM)
LIMIT = 48 * 1024 * 1024


def call(body, out_shape, operands, specs, scratch=()):
    return pl.pallas_call(
        body,
        out_shape=out_shape,
        in_specs=specs,
        out_specs=jax.tree.map(lambda leaf: SMEM if leaf.dtype == jnp.int32 else VMEM, out_shape),
        scratch_shapes=scratch,
        compiler_params=pltpu.CompilerParams(vmem_limit_bytes=LIMIT),
    )(*operands)


def relax_kernel(place_ref, logits_ref, probs_ref, send_ref, same_place_ref):
    same_place_ref[0] = place_ref[0]
    flipped = logits_ref[...].T
    copies = send_ref.shape[0]
    for attr in range(probs_ref.shape[0]):
        block = flipped[attr * V : (attr + 1) * V, :]
        top = jnp.max(block, axis=0, keepdims=True)
        expo = jnp.exp(block - top)
        probs = expo / jnp.sum(expo, axis=0, keepdims=True)
        probs_ref[attr] = probs
        low = probs.astype(jnp.bfloat16)
        for copy in range(copies):
            send_ref[copy, attr] = low


def select_kernel(triples_ref, full_ref, send_ref):
    for marg in range(send_ref.shape[0]):
        for which in range(3):
            send_ref[marg, which] = full_ref[triples_ref[which, marg]]


def fill_pairs(src_ref, source, lanes, pairs_ref, first_ref, second_ref):
    first_ref[...] = src_ref[source, 0].astype(jnp.float32)
    second_ref[...] = src_ref[source, 1].astype(jnp.float32)
    first = first_ref[...]
    for mod in range(MODS):
        second = second_ref[pl.ds(mod, V // MODS, stride=MODS), :]
        both = first[:, None, :] * second[None, :, :]
        pairs_ref[mod, :, lanes] = both.reshape(V * V // MODS, both.shape[2]).astype(jnp.bfloat16)


def answer_kernel(
    place_ref, src_ref, own_ref, send_ref, same_place_ref, pairs_ref, third_ref, first_ref, second_ref
):
    same_place_ref[0] = place_ref[0]
    sources, unused, unused2, rows = src_ref.shape

    def fill(source, carry):
        lanes = pl.ds(pl.multiple_of(source * rows, rows), rows)
        fill_pairs(src_ref, source, lanes, pairs_ref, first_ref, second_ref)
        third_ref[:, lanes] = src_ref[source, 2]
        return carry

    lax.fori_loop(0, sources, fill, 0)
    for mod in range(MODS):
        part = lax.dot_general(
            third_ref[...], pairs_ref[mod], (((1,), (1,)), ((), ())), preferred_element_type=jnp.float32
        )
        own_ref[mod * V : (mod + 1) * V, :] = part
        send_ref[mod * V : (mod + 1) * V, :] = part.astype(jnp.bfloat16)


def backward_kernel(
    scale, src_ref, own_ref, other_ref, target_ref, out_ref, low_ref, mask_ref, pairs_ref, first_ref, second_ref, cross_ref, grad_ref
):
    sources, unused, unused2, rows = src_ref.shape
    total = own_ref[...] + other_ref[...].astype(jnp.float32)
    resid = scale * total - target_ref[...].T
    low_ref[...] = resid.astype(jnp.bfloat16)
    flipped = resid.T
    lane_mod = lax.broadcasted_iota(jnp.int32, flipped.shape, 1) // V
    for mod in range(MODS):
        mask_ref[mod] = jnp.where(lane_mod == mod, flipped, 0.0).astype(jnp.bfloat16)

    def step(source, carry):
        fill_pairs(src_ref, source, slice(None), pairs_ref, first_ref, second_ref)
        third = src_ref[source, 2]
        stacked = jnp.concatenate([third] * MODS, axis=0)
        third_grad = jnp.zeros(third.shape, jnp.float32)
        first = first_ref[...]
        first_sum = jnp.zeros((V, V // MODS, rows), jnp.float32)
        for mod in range(MODS):
            third_grad += jnp.dot(
                low_ref[mod * V : (mod + 1) * V, :], pairs_ref[mod], preferred_element_type=jnp.float32
            )
            cross = jnp.dot(mask_ref[mod], stacked, preferred_element_type=jnp.float32)
            cross = cross.reshape(V, V // MODS, rows)
            second = second_ref[pl.ds(mod, V // MODS, stride=MODS), :]
            first_sum += cross * second[None, :, :]
            grad_ref[pl.ds(mod, V // MODS, stride=MODS), :] = jnp.sum(cross * first[:, None, :], axis=0)
        cross_ref[...] = first_sum.reshape(V * V // MODS, rows)
        first_grad = jnp.zeros((V, rows), jnp.float32)
        for part in range(V // MODS):
            first_grad += cross_ref[pl.ds(part, V, stride=V // MODS), :]
        out_ref[source, 0] = first_grad.astype(jnp.bfloat16)
        out_ref[source, 1] = grad_ref[...].astype(jnp.bfloat16)
        out_ref[source, 2] = third_grad.astype(jnp.bfloat16)
        return carry

    lax.fori_loop(0, sources, step, 0)


def collect_kernel(triples_ref, grads_ref, send_ref, total_ref):
    total_ref[...] = jnp.zeros(total_ref.shape, jnp.float32)
    for marg in range(grads_ref.shape[0]):
        for which in range(3):
            attr = triples_ref[which, marg]
            total_ref[attr] = total_ref[attr] + grads_ref[marg, which].astype(jnp.float32)
    send_ref[...] = total_ref[...].astype(jnp.bfloat16)


def adam_kernel(
    parts_ref, probs_ref, logits_ref, first_ref, second_ref, out_logits_ref, out_first_ref, out_second_ref
):
    row_grad = parts_ref[0].astype(jnp.float32)
    for part in range(1, parts_ref.shape[0]):
        row_grad += parts_ref[part].astype(jnp.float32)
    probs = probs_ref[...]
    inner = jnp.sum(probs * row_grad, axis=1, keepdims=True)
    grad = 512.0 * probs * (row_grad - inner)
    grad = grad.reshape(grad.shape[0] * V, grad.shape[2]).T
    new_first = 0.9 * first_ref[...] + 0.1 * grad
    new_second = 0.999 * second_ref[...] + 0.001 * grad * grad
    first_hat = new_first / (1.0 - 0.9**ADAM_STEP)
    second_hat = new_second / (1.0 - 0.999**ADAM_STEP)
    out_logits_ref[...] = logits_ref[...] - 0.5 * first_hat / (jnp.sqrt(second_hat) + 1e-08)
    out_first_ref[...] = new_first
    out_second_ref[...] = new_second


def swap(value, axes):
    return lax.all_to_all(value, axes, 0, 0, tiled=True)


def shards(logits, first_moment, second_moment, targets, triples):
    rows, cols = logits.shape
    margs, cells = targets.shape
    attrs = cols // V
    groups = lax.axis_size(MARG_AXES)
    scale = cells / (rows * lax.axis_size(ROW_AXES))
    f32, low = jnp.float32, jnp.bfloat16
    shape = jax.ShapeDtypeStruct
    attributes = triples.T
    place = lax.axis_index(SHARE_AXES).astype(jnp.int32).reshape(1)
    scalar = shape((1,), jnp.int32)
    probs, copies, place = call(
        relax_kernel,
        (shape((attrs, V, rows), f32), shape((groups, attrs, V, rows), low), scalar),
        (place, logits),
        [SMEM, VMEM],
    )
    full = swap(copies, MARG_AXES).reshape(groups * attrs, V, rows)
    picked = call(select_kernel, shape((margs, 3, V, rows), low), (attributes, full), [SMEM, VMEM])
    sources = swap(picked, SHARE_AXES)
    tall, wide = V * V // MODS, V * MODS
    own, send, place = call(
        answer_kernel,
        (shape((wide, tall), f32), shape((wide, tall), low), scalar),
        (place, sources),
        [SMEM, VMEM],
        [
            pltpu.VMEM((MODS, tall, margs * rows), low),
            pltpu.VMEM((V, margs * rows), low),
            pltpu.VMEM((V, rows), f32),
            pltpu.VMEM((V, rows), f32),
        ],
    )
    other = lax.ppermute(send, "u", [(0, 1), (1, 0)])
    target = lax.dynamic_slice_in_dim(targets, place[0], 1, 0).reshape(tall, wide)
    grads = call(
        lambda *refs: backward_kernel(scale, *refs),
        shape((margs, 3, V, rows), low),
        (sources, own, other, target),
        [VMEM] * 4,
        [
            pltpu.VMEM((wide, tall), low),
            pltpu.VMEM((MODS, tall, wide), low),
            pltpu.VMEM((MODS, tall, rows), low),
            pltpu.VMEM((V, rows), f32),
            pltpu.VMEM((V, rows), f32),
            pltpu.VMEM((tall, rows), f32),
            pltpu.VMEM((V, rows), f32),
        ],
    )
    returned = swap(grads, SHARE_AXES)
    totals = call(
        collect_kernel,
        shape((groups * attrs, V, rows), low),
        (attributes, returned),
        [SMEM, VMEM],
        [pltpu.VMEM((groups * attrs, V, rows), f32)],
    )
    parts = swap(totals.reshape(groups, attrs, V, rows), MARG_AXES)
    return call(
        adam_kernel,
        (shape((rows, cols), f32),) * 3,
        (parts, probs, logits, first_moment, second_moment),
        [VMEM] * 5,
    )


def solution(mesh):
    fine = Mesh(mesh.devices.reshape(PARTS), NAMES)
    table = P(ROW_AXES, MARG_AXES)
    listed = P(MARG_AXES, None)
    return jax.shard_map(
        shards,
        mesh=fine,
        in_specs=(table, table, table, listed, listed),
        out_specs=(table, table, table),
        check_vma=False,
    )
```

```python
import jax
import jax.numpy as jnp
from jax import lax
from jax.experimental import pallas as pl
from jax.experimental.pallas import tpu as pltpu
from jax.sharding import Mesh, PartitionSpec as P

V = 32
ADAM_STEP = 4
PARTS = (4, 2, 2, 2, 4, 2)
NAMES = ("x", "u", "w", "c", "y", "h")
ROW_AXES = ("x", "u", "w", "c")
MARG_AXES = ("y", "h")
PLACE_AXES = ("x", "w", "c")
SHARE_AXES = ("x", "w", "c", "y")
CHUNKS = 4
CHUNK = 32
LANES = CHUNKS * CHUNK
SUB = V // CHUNKS
MODS = 4
VMEM = pl.BlockSpec(memory_space=pltpu.VMEM)
SMEM = pl.BlockSpec(memory_space=pltpu.SMEM)
ANY = pl.BlockSpec(memory_space=pl.ANY)
LIMIT = 40 * 1024 * 1024
F32 = jnp.float32
LOW = jnp.bfloat16


def call(body, out_shape, operands, specs, scratch=()):
    return pl.pallas_call(
        body,
        out_shape=out_shape,
        in_specs=specs,
        out_specs=jax.tree.map(lambda unused: VMEM, out_shape),
        scratch_shapes=scratch,
        compiler_params=pltpu.CompilerParams(vmem_limit_bytes=LIMIT),
    )(*operands)


def exchange(blocks):
    lane = lax.broadcasted_iota(jnp.int32, blocks[0].shape, 1)
    blocks = list(blocks)
    for width, pairs in ((2 * CHUNK, ((0, 2), (1, 3))), (CHUNK, ((0, 1), (2, 3)))):
        low_part = (lane // width) % 2 == 0
        for a, b in pairs:
            left, right = blocks[a], blocks[b]
            blocks[a] = jnp.where(low_part, left, pltpu.roll(right, width, 1))
            blocks[b] = jnp.where(low_part, pltpu.roll(left, LANES - width, 1), right)
    return blocks


def relax_kernel(side_ref, triples_ref, logits_ref, target_ref, probs_ref, send_ref, triple_ref):
    flipped = logits_ref[...].T
    attrs = probs_ref.shape[0]
    halves = send_ref.shape[0] // CHUNKS
    for attr in range(attrs):
        block = flipped[attr * V : (attr + 1) * V, :]
        top = jnp.max(block, axis=0, keepdims=True)
        expo = jnp.exp(block - top)
        probs = expo / jnp.sum(expo, axis=0, keepdims=True)
        probs_ref[attr] = probs
        chunks = exchange([probs[part * SUB : (part + 1) * SUB, :] for part in range(CHUNKS)])
        for chunk in range(CHUNKS):
            low = chunks[chunk].astype(LOW)
            for half in range(halves):
                send_ref[chunk * halves + half, attr] = low
    triple_ref[...] = jnp.zeros(triple_ref.shape, F32)
    triple_ref[0:3, 0 : triples_ref.shape[1]] = triples_ref[...].astype(F32)
    for half in range(halves):
        mine = jnp.where(side_ref[0] == half, 1.0, 0.0)
        tile = (triple_ref[...] * mine).astype(LOW)
        for chunk in range(CHUNKS):
            send_ref[chunk * halves + half, attrs] = tile


def select_kernel(full_ref, send_ref, triples_ref, scalar_ref, sem):
    groups, slots = full_ref.shape[0], full_ref.shape[1]
    attrs = slots - 1
    halves = groups // CHUNKS
    for chunk in range(CHUNKS):
        tile = full_ref[chunk * halves, attrs].astype(F32)
        for half in range(1, halves):
            tile += full_ref[chunk * halves + half, attrs].astype(F32)
        triples_ref[chunk] = tile.astype(jnp.int32)
    copy = pltpu.make_async_copy(triples_ref, scalar_ref, sem)
    copy.start()
    copy.wait()

    def pick(place, carry):
        for chunk in range(CHUNKS):
            for which in range(3):
                attr = scalar_ref[chunk, which, place]
                send_ref[place * CHUNKS + chunk, which] = full_ref[attr // attrs, attr % attrs]
        return carry

    lax.fori_loop(0, send_ref.shape[0] // CHUNKS, pick, 0, unroll=4)


def unpack(src_ref, shard):
    packed = [src_ref[shard * CHUNKS + chunk].astype(F32).reshape(3 * SUB, LANES) for chunk in range(CHUNKS)]
    parts = exchange(packed)
    return [
        jnp.concatenate([part[which * SUB : (which + 1) * SUB, :] for part in parts], axis=0) for which in range(3)
    ]


def answer_kernel(src_ref, own_ref, send_ref, table_ref, pairs_ref):
    shards = table_ref.shape[0]

    def fill(step):
        for part in range(2):
            shard = 2 * step + part
            first, second, third = [value.astype(LOW) for value in unpack(src_ref, shard)]
            table_ref[shard, 0] = first
            table_ref[shard, 1] = second
            table_ref[shard, 2] = third
            for value in range(V):
                row = jnp.broadcast_to(second[value : value + 1, :], first.shape)
                mod, rest = value % MODS, value // MODS
                pairs_ref[step, mod, rest * V : (rest + 1) * V, part * LANES : (part + 1) * LANES] = first * row

    def add(step):
        third = jnp.concatenate([table_ref[2 * step, 2], table_ref[2 * step + 1, 2]], axis=1)
        for mod in range(MODS):
            own_ref[mod * V : (mod + 1) * V, :] += lax.dot_general(
                third, pairs_ref[step, mod], (((1,), (1,)), ((), ())), preferred_element_type=F32
            )

    own_ref[...] = jnp.zeros(own_ref.shape, F32)
    fill(0)

    def both(step, carry):
        add(step - 1)
        fill(step)
        return carry

    lax.fori_loop(1, shards // 2, both, 0)
    add(shards // 2 - 1)
    send_ref[...] = own_ref[...].astype(LOW)


def base_kernel(scale, own_ref, target_ref, base_ref):
    rows = [target_ref[pl.ds(rest, V, stride=SUB), :] for rest in range(SUB)]
    base_ref[...] = scale * own_ref[...] - jnp.concatenate(rows, axis=0).T


def backward_kernel(scale, table_ref, pairs_ref, base_ref, other_ref, out_ref, low_ref, mask_ref, row_ref, sum_ref):
    steps = pairs_ref.shape[0]
    wide = 2 * LANES
    resid = base_ref[...] + scale * other_ref[...].astype(F32)
    low_ref[...] = resid.astype(LOW)
    flipped = resid.T
    lane_mod = lax.broadcasted_iota(jnp.int32, flipped.shape, 1) // V
    for mod in range(MODS):
        mask_ref[mod] = jnp.where(lane_mod == mod, flipped, 0.0).astype(LOW)

    def step(index, carry):
        pair = [
            jnp.concatenate([table_ref[2 * index, which], table_ref[2 * index + 1, which]], axis=1)
            for which in range(3)
        ]
        first = pair[0].astype(F32)
        row_ref[...] = pair[1].astype(F32)
        stacked = jnp.concatenate([pair[2]] * MODS, axis=0)
        third_grad = jnp.zeros((V, wide), F32)
        first_grad = jnp.zeros((V, wide), F32)
        for mod in range(MODS):
            third_grad += jnp.dot(
                low_ref[mod * V : (mod + 1) * V, :], pairs_ref[index, mod], preferred_element_type=F32
            )
            cross = jnp.dot(mask_ref[mod], stacked, preferred_element_type=F32)
            for rest in range(SUB):
                value = rest * MODS + mod
                block = cross[rest * V : (rest + 1) * V, :]
                first_grad += block * row_ref[pl.ds(value, 1), :]
                product = block * first
                partial = product[0:8]
                for part in range(1, V // 8):
                    partial += product[8 * part : 8 * part + 8]
                for half in range(2):
                    sum_ref[half, value * 8 : value * 8 + 8, :] = partial[:, half * LANES : (half + 1) * LANES]
        for half in range(2):
            lanes = slice(half * LANES, (half + 1) * LANES)
            second_grad = jnp.zeros((V, LANES), F32)
            for part in range(8):
                second_grad += sum_ref[half, pl.ds(part, V, stride=8), :]
            grads = (first_grad[:, lanes], second_grad, third_grad[:, lanes])
            parts = [
                jnp.concatenate([grad[part * SUB : (part + 1) * SUB, :] for grad in grads], axis=0)
                for part in range(CHUNKS)
            ]
            for chunk, packed in enumerate(exchange(parts)):
                place = (2 * index + half) * CHUNKS + chunk
                out_ref[place] = packed.reshape(3, SUB, LANES).astype(LOW)
        return carry

    lax.fori_loop(0, steps, step, 0)


def collect_kernel(triples_ref, grads_ref, send_ref, total_ref):
    groups, attrs = send_ref.shape[0], send_ref.shape[1]
    total_ref[...] = jnp.zeros(total_ref.shape, F32)

    def add(place, carry):
        for chunk in range(CHUNKS):
            for which in range(3):
                attr = triples_ref[chunk, which, place]
                term = grads_ref[place * CHUNKS + chunk, which].astype(F32)
                total_ref[which, attr] = total_ref[which, attr] + term
        return carry

    lax.fori_loop(0, grads_ref.shape[0] // CHUNKS, add, 0, unroll=4)
    total = total_ref[0] + total_ref[1] + total_ref[2]
    send_ref[...] = total.reshape(groups, attrs, SUB, LANES).astype(LOW)


def adam_kernel(
    parts_ref, probs_ref, logits_ref, first_ref, second_ref, out_logits_ref, out_first_ref, out_second_ref, grad_ref
):
    groups, attrs = parts_ref.shape[0], parts_ref.shape[1]
    halves = groups // CHUNKS
    chunks = []
    for chunk in range(CHUNKS):
        total = parts_ref[chunk * halves].astype(F32)
        for half in range(1, halves):
            total += parts_ref[chunk * halves + half].astype(F32)
        chunks.append(total.reshape(attrs * SUB, LANES))
    parts = exchange(chunks)
    for attr in range(attrs):
        row_grad = jnp.concatenate([part[attr * SUB : (attr + 1) * SUB, :] for part in parts], axis=0)
        probs = probs_ref[attr]
        inner = jnp.sum(probs * row_grad, axis=0, keepdims=True)
        grad_ref[attr * V : (attr + 1) * V, :] = 512.0 * probs * (row_grad - inner)
    grad = grad_ref[...].T
    new_first = 0.9 * first_ref[...] + 0.1 * grad
    new_second = 0.999 * second_ref[...] + 0.001 * grad * grad
    first_hat = new_first / (1.0 - 0.9**ADAM_STEP)
    second_hat = new_second / (1.0 - 0.999**ADAM_STEP)
    out_logits_ref[...] = logits_ref[...] - 0.5 * first_hat / (jnp.sqrt(second_hat) + 1e-08)
    out_first_ref[...] = new_first
    out_second_ref[...] = new_second


def swap(value, axes):
    return lax.all_to_all(value, axes, 0, 0, tiled=True)


def answers(src):
    shape = jax.ShapeDtypeStruct
    shards = src.shape[0] // CHUNKS
    tall, wide = V * V // MODS, V * MODS
    return call(
        answer_kernel,
        (
            shape((wide, tall), F32),
            shape((wide, tall), LOW),
            shape((shards, 3, V, LANES), LOW),
            shape((shards // 2, MODS, tall, 2 * LANES), LOW),
        ),
        (src,),
        [VMEM],
    )


def backward(scale, table, pairs, base, other):
    shards = table.shape[0]
    tall, wide = V * V // MODS, V * MODS
    return call(
        lambda *refs: backward_kernel(scale, *refs),
        jax.ShapeDtypeStruct((shards * CHUNKS, 3, SUB, LANES), LOW),
        (table, pairs, base, other),
        [VMEM] * 4,
        [
            pltpu.VMEM((wide, tall), LOW),
            pltpu.VMEM((MODS, tall, wide), LOW),
            pltpu.VMEM((V, 2 * LANES), F32),
            pltpu.VMEM((2, 8 * V, LANES), F32),
        ],
    )


def shards(logits, first_moment, second_moment, targets, triples):
    rows, cols = logits.shape
    margs, cells = targets.shape
    attrs = cols // V
    groups = lax.axis_size(MARG_AXES)
    scale = cells / (rows * lax.axis_size(ROW_AXES))
    shape = jax.ShapeDtypeStruct
    tall, wide = V * V // MODS, V * MODS
    place = lax.axis_index(PLACE_AXES)
    target = lax.dynamic_slice_in_dim(targets, place, 1, 0).reshape(tall, wide)
    side = lax.axis_index("h").astype(jnp.int32).reshape(1)
    probs, copies = call(
        relax_kernel,
        (shape((attrs, V, rows), F32), shape((groups, attrs + 1, SUB, LANES), LOW)),
        (side, triples.T, logits, target),
        [SMEM, VMEM, VMEM, ANY],
        [pltpu.VMEM((SUB, LANES), F32)],
    )
    full = swap(copies, MARG_AXES)
    picked, attributes = call(
        select_kernel,
        (shape((margs * CHUNKS, 3, SUB, LANES), LOW), shape((CHUNKS, SUB, LANES), jnp.int32)),
        (full,),
        [VMEM],
        [pltpu.SMEM((CHUNKS, SUB, LANES), jnp.int32), pltpu.SemaphoreType.DMA],
    )
    own, send, table, pairs = answers(swap(picked, SHARE_AXES))
    other = lax.ppermute(send, "u", [(0, 1), (1, 0)])
    base = call(lambda *refs: base_kernel(scale, *refs), shape((wide, tall), F32), (own, target), [VMEM] * 2)
    returned = swap(backward(scale, table, pairs, base, other), SHARE_AXES)
    totals = call(
        collect_kernel,
        shape((groups, attrs, SUB, LANES), LOW),
        (attributes, returned),
        [SMEM, VMEM],
        [pltpu.VMEM((3, groups * attrs, SUB, LANES), F32)],
    )
    return call(
        adam_kernel,
        (shape((rows, cols), F32),) * 3,
        (swap(totals, MARG_AXES), probs, logits, first_moment, second_moment),
        [VMEM] * 5,
        [pltpu.VMEM((cols, rows), F32)],
    )


def solution(mesh):
    fine = Mesh(mesh.devices.reshape(PARTS), NAMES)
    table = P(ROW_AXES, MARG_AXES)
    listed = P(MARG_AXES, None)
    return jax.shard_map(
        shards,
        mesh=fine,
        in_specs=(table, table, table, listed, listed),
        out_specs=(table, table, table),
        check_vma=False,
    )
```

```python
import jax
import jax.numpy as jnp
from jax import lax
from jax.experimental import pallas as pl
from jax.experimental.pallas import tpu as pltpu
from jax.sharding import Mesh, PartitionSpec as P

V = 32
ADAM_STEP = 4
PARTS = (4, 2, 2, 2, 4, 2)
NAMES = ("x", "u", "w", "c", "y", "h")
ROW_AXES = ("x", "u", "w", "c")
MARG_AXES = ("y", "h")
PLACE_AXES = ("x", "w", "c")
SHARE_AXES = ("x", "w", "c", "y")
CHUNKS = 4
CHUNK = 32
LANES = CHUNKS * CHUNK
SUB = V // CHUNKS
MODS = 4
VMEM = pl.BlockSpec(memory_space=pltpu.VMEM)
SMEM = pl.BlockSpec(memory_space=pltpu.SMEM)
ANY = pl.BlockSpec(memory_space=pl.ANY)
LIMIT = 40 * 1024 * 1024
HIGH_LIMIT = 60 * 1024 * 1024
F32 = jnp.float32
LOW = jnp.bfloat16


def call(body, out_shape, operands, specs, scratch=(), limit=LIMIT):
    return pl.pallas_call(
        body,
        out_shape=out_shape,
        in_specs=specs,
        out_specs=jax.tree.map(lambda unused: VMEM, out_shape),
        scratch_shapes=scratch,
        compiler_params=pltpu.CompilerParams(vmem_limit_bytes=limit),
    )(*operands)


def exchange(blocks):
    lane = lax.broadcasted_iota(jnp.int32, blocks[0].shape, 1)
    blocks = list(blocks)
    for width, pairs in ((2 * CHUNK, ((0, 2), (1, 3))), (CHUNK, ((0, 1), (2, 3)))):
        low_part = (lane // width) % 2 == 0
        for a, b in pairs:
            left, right = blocks[a], blocks[b]
            blocks[a] = jnp.where(low_part, left, pltpu.roll(right, width, 1))
            blocks[b] = jnp.where(low_part, pltpu.roll(left, LANES - width, 1), right)
    return blocks


def relax_kernel(
    place_ref, triples_any, logits_any, probs_ref, send_ref, triple_ref, triples_ref, logits_ref, triples_sem, logits_sem
):
    triples_copy = pltpu.make_async_copy(triples_any, triples_ref, triples_sem)
    logits_copy = pltpu.make_async_copy(logits_any, logits_ref, logits_sem)
    logits_copy.start()
    triples_copy.start()
    logits_copy.wait()
    triples_copy.wait()
    flipped = logits_ref[...].T
    attrs = probs_ref.shape[0]
    halves = send_ref.shape[0] // CHUNKS
    for attr in range(attrs):
        block = flipped[attr * V : (attr + 1) * V, :]
        top = jnp.max(block, axis=0, keepdims=True)
        expo = jnp.exp(block - top)
        probs = expo / jnp.sum(expo, axis=0, keepdims=True)
        probs_ref[attr] = probs
        chunks = exchange([probs[part * SUB : (part + 1) * SUB, :] for part in range(CHUNKS)])
        for chunk in range(CHUNKS):
            low = chunks[chunk].astype(LOW)
            for half in range(halves):
                send_ref[chunk * halves + half, attr] = low
    triple_ref[...] = jnp.zeros(triple_ref.shape, F32)
    triple_ref[0:3, 0 : triples_ref.shape[1]] = triples_ref[...].astype(F32)
    for half in range(halves):
        mine = jnp.where(place_ref[1] == half, 1.0, 0.0)
        tile = (triple_ref[...] * mine).astype(LOW)
        for chunk in range(CHUNKS):
            send_ref[chunk * halves + half, attrs] = tile


def select_kernel(full_ref, send_ref, triples_ref, index_ref, scalar_ref, sem):
    slots = full_ref.shape[0] // (2 * CHUNKS)
    places = send_ref.shape[0] // CHUNKS
    triples = jnp.zeros(triples_ref.shape, F32)
    for chunk in range(CHUNKS):
        tile = full_ref[2 * chunk * slots + slots - 1].astype(F32) + full_ref[(2 * chunk + 2) * slots - 1].astype(F32)
        triples += pltpu.roll(tile, chunk * places, 1) if chunk else tile
    attrs = triples.astype(jnp.int32)
    triples_ref[...] = attrs
    index_ref[...] = attrs + attrs // (slots - 1)
    copy = pltpu.make_async_copy(index_ref, scalar_ref, sem)
    copy.start()
    copy.wait()
    for place in range(places):
        for chunk in range(CHUNKS):
            for which in range(3):
                send_ref[place * CHUNKS + chunk, which] = full_ref[scalar_ref[which, chunk * places + place]]


def unpack(src_ref, shard):
    packed = [src_ref[shard * CHUNKS + chunk].astype(F32).reshape(3 * SUB, LANES) for chunk in range(CHUNKS)]
    parts = exchange(packed)
    return [
        jnp.concatenate([part[which * SUB : (which + 1) * SUB, :] for part in parts], axis=0) for which in range(3)
    ]


def answer_kernel(src_ref, own_ref, send_ref, table_ref, pairs_ref):
    shards = table_ref.shape[0]

    def fill(step):
        for part in range(2):
            shard = 2 * step + part
            first, second, third = [value.astype(LOW) for value in unpack(src_ref, shard)]
            table_ref[shard, 0] = first
            table_ref[shard, 1] = second
            table_ref[shard, 2] = third
            for value in range(V):
                row = jnp.broadcast_to(second[value : value + 1, :], first.shape)
                mod, rest = value % MODS, value // MODS
                pairs_ref[step, mod, rest * V : (rest + 1) * V, part * LANES : (part + 1) * LANES] = first * row

    def add(step):
        third = jnp.concatenate([table_ref[2 * step, 2], table_ref[2 * step + 1, 2]], axis=1)
        for mod in range(MODS):
            own_ref[mod * V : (mod + 1) * V, :] += lax.dot_general(
                third, pairs_ref[step, mod], (((1,), (1,)), ((), ())), preferred_element_type=F32
            )

    own_ref[...] = jnp.zeros(own_ref.shape, F32)
    fill(0)

    def both(step, carry):
        add(step - 1)
        fill(step)
        return carry

    lax.fori_loop(1, shards // 2, both, 0, unroll=shards // 2 - 1)
    add(shards // 2 - 1)
    send_ref[...] = own_ref[...].astype(LOW)


def base_kernel(scale, place_ref, own_ref, targets_any, base_ref, block_ref, target_ref, sem):
    place = place_ref[0]
    start = pl.multiple_of(place // 8 * 8, 8)
    copy = pltpu.make_async_copy(targets_any.at[pl.ds(start, 8), :], block_ref, sem)
    copy.start()
    copy.wait()
    mine = lax.broadcasted_iota(jnp.int32, (8, LANES), 0) == lax.rem(place, 8)
    for rest in range(SUB):
        for value in range(V):
            tile = block_ref[:, pl.ds((value * SUB + rest) * LANES, LANES)]
            row = jnp.sum(jnp.where(mine, tile, 0.0), axis=0, keepdims=True)
            target_ref[pl.ds(rest * V + value, 1), :] = row
    base_ref[...] = scale * own_ref[...] - target_ref[...].T


def backward_kernel(scale, table_ref, pairs_ref, base_ref, other_ref, out_ref, low_ref, mask_ref, row_ref, sum_ref):
    steps = pairs_ref.shape[0]
    wide = 2 * LANES
    resid = base_ref[...] + scale * other_ref[...].astype(F32)
    low_ref[...] = resid.astype(LOW)
    flipped = resid.T
    lane_mod = lax.broadcasted_iota(jnp.int32, flipped.shape, 1) // V
    for mod in range(MODS):
        mask_ref[mod] = jnp.where(lane_mod == mod, flipped, 0.0).astype(LOW)

    def step(index, carry):
        pair = [
            jnp.concatenate([table_ref[2 * index, which], table_ref[2 * index + 1, which]], axis=1)
            for which in range(3)
        ]
        first = pair[0].astype(F32)
        row_ref[...] = pair[1].astype(F32)
        stacked = jnp.concatenate([pair[2]] * MODS, axis=0)
        third_grad = jnp.zeros((V, wide), F32)
        first_grad = jnp.zeros((V, wide), F32)
        for mod in range(MODS):
            third_grad += jnp.dot(
                low_ref[mod * V : (mod + 1) * V, :], pairs_ref[index, mod], preferred_element_type=F32
            )
            cross = jnp.dot(mask_ref[mod], stacked, preferred_element_type=F32)
            for rest in range(SUB):
                value = rest * MODS + mod
                block = cross[rest * V : (rest + 1) * V, :]
                first_grad += block * row_ref[pl.ds(value, 1), :]
                product = block * first
                partial = product[0:8]
                for part in range(1, V // 8):
                    partial += product[8 * part : 8 * part + 8]
                for half in range(2):
                    sum_ref[half, value * 8 : value * 8 + 8, :] = partial[:, half * LANES : (half + 1) * LANES]
        for half in range(2):
            lanes = slice(half * LANES, (half + 1) * LANES)
            second_grad = jnp.zeros((V, LANES), F32)
            for part in range(8):
                second_grad += sum_ref[half, pl.ds(part, V, stride=8), :]
            grads = (first_grad[:, lanes], second_grad, third_grad[:, lanes])
            parts = [
                jnp.concatenate([grad[part * SUB : (part + 1) * SUB, :] for grad in grads], axis=0)
                for part in range(CHUNKS)
            ]
            for chunk, packed in enumerate(exchange(parts)):
                place = (2 * index + half) * CHUNKS + chunk
                out_ref[place] = packed.reshape(3, SUB, LANES).astype(LOW)
        return carry

    lax.fori_loop(0, steps, step, 0, unroll=steps)


def collect_kernel(triples_ref, grads_ref, send_ref, *total_refs):
    groups, attrs = send_ref.shape[0], send_ref.shape[1]
    places = grads_ref.shape[0] // CHUNKS
    for total_ref in total_refs:
        total_ref[...] = jnp.zeros(total_ref.shape, F32)
    for place in range(places):
        for chunk in range(CHUNKS):
            for which, total_ref in enumerate(total_refs):
                attr = triples_ref[which, chunk * places + place]
                total_ref[attr] = total_ref[attr] + grads_ref[place * CHUNKS + chunk, which].astype(F32)
    total = total_refs[0][...] + total_refs[1][...] + total_refs[2][...]
    send_ref[...] = total.reshape(groups, attrs, SUB, LANES).astype(LOW)


def adam_kernel(
    parts_ref, probs_ref, logits_ref, first_ref, second_ref, out_logits_ref, out_first_ref, out_second_ref, grad_ref
):
    groups, attrs = parts_ref.shape[0], parts_ref.shape[1]
    halves = groups // CHUNKS
    chunks = []
    for chunk in range(CHUNKS):
        total = parts_ref[chunk * halves].astype(F32)
        for half in range(1, halves):
            total += parts_ref[chunk * halves + half].astype(F32)
        chunks.append(total.reshape(attrs * SUB, LANES))
    parts = exchange(chunks)
    for attr in range(attrs):
        row_grad = jnp.concatenate([part[attr * SUB : (attr + 1) * SUB, :] for part in parts], axis=0)
        probs = probs_ref[attr]
        inner = jnp.sum(probs * row_grad, axis=0, keepdims=True)
        grad_ref[attr * V : (attr + 1) * V, :] = 512.0 * probs * (row_grad - inner)
    grad = grad_ref[...].T
    new_first = 0.9 * first_ref[...] + 0.1 * grad
    new_second = 0.999 * second_ref[...] + 0.001 * grad * grad
    first_hat = new_first / (1.0 - 0.9**ADAM_STEP)
    second_hat = new_second / (1.0 - 0.999**ADAM_STEP)
    out_logits_ref[...] = logits_ref[...] - 0.5 * first_hat / (jnp.sqrt(second_hat) + 1e-08)
    out_first_ref[...] = new_first
    out_second_ref[...] = new_second


def swap(value, axes):
    return lax.all_to_all(value, axes, 0, 0, tiled=True)


def answers(src):
    shape = jax.ShapeDtypeStruct
    shards = src.shape[0] // CHUNKS
    tall, wide = V * V // MODS, V * MODS
    return call(
        answer_kernel,
        (
            shape((wide, tall), F32),
            shape((wide, tall), LOW),
            shape((shards, 3, V, LANES), LOW),
            shape((shards // 2, MODS, tall, 2 * LANES), LOW),
        ),
        (src,),
        [VMEM],
    )


def backward(scale, table, pairs, base, other):
    shards = table.shape[0]
    tall, wide = V * V // MODS, V * MODS
    return call(
        lambda *refs: backward_kernel(scale, *refs),
        jax.ShapeDtypeStruct((shards * CHUNKS, 3, SUB, LANES), LOW),
        (table, pairs, base, other),
        [VMEM] * 4,
        [
            pltpu.VMEM((wide, tall), LOW),
            pltpu.VMEM((MODS, tall, wide), LOW),
            pltpu.VMEM((V, 2 * LANES), F32),
            pltpu.VMEM((2, 8 * V, LANES), F32),
        ],
    )


def shards(logits, first_moment, second_moment, targets, triples):
    rows, cols = logits.shape
    margs, cells = targets.shape
    attrs = cols // V
    groups = lax.axis_size(MARG_AXES)
    scale = cells / (rows * lax.axis_size(ROW_AXES))
    shape = jax.ShapeDtypeStruct
    tall, wide = V * V // MODS, V * MODS
    place = jnp.stack([lax.axis_index(PLACE_AXES), lax.axis_index("h")]).astype(jnp.int32)
    probs, copies = call(
        relax_kernel,
        (shape((attrs, V, rows), F32), shape((groups, attrs + 1, SUB, LANES), LOW)),
        (place, triples.T, logits),
        [SMEM, ANY, ANY],
        [
            pltpu.VMEM((SUB, LANES), F32),
            pltpu.VMEM((3, margs), jnp.int32),
            pltpu.VMEM((rows, cols), F32),
            pltpu.SemaphoreType.DMA,
            pltpu.SemaphoreType.DMA,
        ],
        HIGH_LIMIT,
    )
    full = swap(copies, MARG_AXES)
    picked, attributes = call(
        select_kernel,
        (shape((margs * CHUNKS, 3, SUB, LANES), LOW), shape((SUB, LANES), jnp.int32)),
        (full.reshape(groups * (attrs + 1), SUB, LANES),),
        [VMEM],
        [pltpu.VMEM((SUB, LANES), jnp.int32), pltpu.SMEM((SUB, LANES), jnp.int32), pltpu.SemaphoreType.DMA],
    )
    own, send, table, pairs = answers(swap(picked, SHARE_AXES))
    other = lax.ppermute(send, "u", [(0, 1), (1, 0)])
    base = call(
        lambda *refs: base_kernel(scale, *refs),
        shape((wide, tall), F32),
        (place, own, targets),
        [SMEM, VMEM, ANY],
        [pltpu.VMEM((8, cells), F32), pltpu.VMEM((tall, wide), F32), pltpu.SemaphoreType.DMA],
    )
    returned = swap(backward(scale, table, pairs, base, other), SHARE_AXES)
    totals = call(
        collect_kernel,
        shape((groups, attrs, SUB, LANES), LOW),
        (attributes, returned),
        [SMEM, VMEM],
        [pltpu.VMEM((groups * attrs, SUB, LANES), F32)] * 3,
    )
    return call(
        adam_kernel,
        (shape((rows, cols), F32),) * 3,
        (swap(totals, MARG_AXES), probs, logits, first_moment, second_moment),
        [VMEM] * 5,
        [pltpu.VMEM((cols, rows), F32)],
    )


def solution(mesh):
    fine = Mesh(mesh.devices.reshape(PARTS), NAMES)
    table = P(ROW_AXES, MARG_AXES)
    listed = P(MARG_AXES, None)
    return jax.shard_map(
        shards,
        mesh=fine,
        in_specs=(table, table, table, listed, listed),
        out_specs=(table, table, table),
        check_vma=False,
    )
```

```python
import jax
import jax.numpy as jnp
from jax import lax
from jax.experimental import pallas as pl
from jax.experimental.pallas import tpu as pltpu
from jax.sharding import Mesh, PartitionSpec as P

V = 32
ADAM_STEP = 4
PARTS = (4, 2, 2, 2, 4, 2)
NAMES = ("x", "u", "w", "c", "y", "h")
ROW_AXES = ("x", "u", "w", "c")
MARG_AXES = ("y", "h")
PLACE_AXES = ("x", "w", "c")
SHARE_AXES = ("x", "w", "c", "y")
CHUNKS = 4
CHUNK = 32
LANES = CHUNKS * CHUNK
SUB = V // CHUNKS
MODS = 4
VMEM = pl.BlockSpec(memory_space=pltpu.VMEM)
SMEM = pl.BlockSpec(memory_space=pltpu.SMEM)
ANY = pl.BlockSpec(memory_space=pl.ANY)
LIMIT = 40 * 1024 * 1024
F32 = jnp.float32
LOW = jnp.bfloat16


def call(body, out_shape, operands, specs, scratch=()):
    return pl.pallas_call(
        body,
        out_shape=out_shape,
        in_specs=specs,
        out_specs=jax.tree.map(lambda unused: VMEM, out_shape),
        scratch_shapes=scratch,
        compiler_params=pltpu.CompilerParams(vmem_limit_bytes=LIMIT),
    )(*operands)


def exchange(blocks):
    lane = lax.broadcasted_iota(jnp.int32, blocks[0].shape, 1)
    blocks = list(blocks)
    for width, pairs in ((2 * CHUNK, ((0, 2), (1, 3))), (CHUNK, ((0, 1), (2, 3)))):
        low_part = (lane // width) % 2 == 0
        for a, b in pairs:
            left, right = blocks[a], blocks[b]
            blocks[a] = jnp.where(low_part, left, pltpu.roll(right, width, 1))
            blocks[b] = jnp.where(low_part, pltpu.roll(left, LANES - width, 1), right)
    return blocks


def relax_kernel(side_ref, triples_ref, logits_ref, probs_ref, send_ref, tile_ref):
    flipped = logits_ref[...].T
    attrs = probs_ref.shape[0]
    halves = send_ref.shape[0] // CHUNKS
    for attr in range(attrs):
        block = flipped[attr * V : (attr + 1) * V, :]
        top = jnp.max(block, axis=0, keepdims=True)
        expo = jnp.exp(block - top)
        probs = expo / jnp.sum(expo, axis=0, keepdims=True)
        probs_ref[attr] = probs
        chunks = exchange([probs[part * SUB : (part + 1) * SUB, :] for part in range(CHUNKS)])
        for chunk in range(CHUNKS):
            low = chunks[chunk].astype(LOW)
            for half in range(halves):
                send_ref[chunk * halves + half, attr] = low
    tile_ref[...] = jnp.zeros(tile_ref.shape, F32)
    tile_ref[0:3, 0 : triples_ref.shape[1]] = triples_ref[...].astype(F32)
    for half in range(halves):
        tile = (tile_ref[...] * jnp.where(side_ref[0] == half, 1.0, 0.0)).astype(LOW)
        for chunk in range(CHUNKS):
            send_ref[chunk * halves + half, attrs] = tile


def select_kernel(full_ref, send_ref, triples_ref, index_ref, scalar_ref, sem):
    slots = full_ref.shape[0] // (2 * CHUNKS)
    places = send_ref.shape[0] // CHUNKS
    triples = jnp.zeros(triples_ref.shape, F32)
    for chunk in range(CHUNKS):
        tile = full_ref[2 * chunk * slots + slots - 1].astype(F32) + full_ref[(2 * chunk + 2) * slots - 1].astype(F32)
        triples += pltpu.roll(tile, chunk * places, 1) if chunk else tile
    attrs = triples.astype(jnp.int32)
    triples_ref[...] = attrs
    index_ref[...] = attrs + attrs // (slots - 1)
    copy = pltpu.make_async_copy(index_ref, scalar_ref, sem)
    copy.start()
    copy.wait()
    for place in range(places):
        for chunk in range(CHUNKS):
            for which in range(3):
                send_ref[place * CHUNKS + chunk, which] = full_ref[scalar_ref[which, chunk * places + place]]


def unpack(src_ref, shard):
    packed = [src_ref[shard * CHUNKS + chunk].astype(F32).reshape(3 * SUB, LANES) for chunk in range(CHUNKS)]
    parts = exchange(packed)
    return [
        jnp.concatenate([part[which * SUB : (which + 1) * SUB, :] for part in parts], axis=0) for which in range(3)
    ]


def answer_kernel(src_ref, own_ref, send_ref, table_ref, pairs_ref):
    shards = table_ref.shape[0]

    def fill(step):
        for part in range(2):
            shard = 2 * step + part
            first, second, third = [value.astype(LOW) for value in unpack(src_ref, shard)]
            table_ref[shard, 0] = first
            table_ref[shard, 1] = second
            table_ref[shard, 2] = third
            for value in range(V):
                row = jnp.broadcast_to(second[value : value + 1, :], first.shape)
                mod, rest = value % MODS, value // MODS
                pairs_ref[step, mod, rest * V : (rest + 1) * V, part * LANES : (part + 1) * LANES] = first * row

    def add(step):
        third = jnp.concatenate([table_ref[2 * step, 2], table_ref[2 * step + 1, 2]], axis=1)
        for mod in range(MODS):
            own_ref[mod * V : (mod + 1) * V, :] += lax.dot_general(
                third, pairs_ref[step, mod], (((1,), (1,)), ((), ())), preferred_element_type=F32
            )

    own_ref[...] = jnp.zeros(own_ref.shape, F32)
    fill(0)

    def both(step, carry):
        add(step - 1)
        fill(step)
        return carry

    lax.fori_loop(1, shards // 2, both, 0, unroll=shards // 2 - 1)
    add(shards // 2 - 1)
    send_ref[...] = own_ref[...].astype(LOW)


def base_kernel(scale, place_ref, own_ref, targets_any, base_ref, block_ref, target_ref, sem):
    place = place_ref[0]
    start = pl.multiple_of(place // 8 * 8, 8)
    copy = pltpu.make_async_copy(targets_any.at[pl.ds(start, 8), :], block_ref, sem)
    copy.start()
    copy.wait()
    mine = lax.broadcasted_iota(jnp.int32, (8, LANES), 0) == lax.rem(place, 8)
    for rest in range(SUB):
        for value in range(V):
            tile = block_ref[:, pl.ds((value * SUB + rest) * LANES, LANES)]
            row = jnp.sum(jnp.where(mine, tile, 0.0), axis=0, keepdims=True)
            target_ref[pl.ds(rest * V + value, 1), :] = row
    base_ref[...] = scale * own_ref[...] - target_ref[...].T


def backward_kernel(scale, table_ref, pairs_ref, base_ref, other_ref, out_ref, low_ref, mask_ref, row_ref, sum_ref):
    steps = pairs_ref.shape[0]
    wide = 2 * LANES
    resid = base_ref[...] + scale * other_ref[...].astype(F32)
    low_ref[...] = resid.astype(LOW)
    flipped = resid.T
    lane_mod = lax.broadcasted_iota(jnp.int32, flipped.shape, 1) // V
    for mod in range(MODS):
        mask_ref[mod] = jnp.where(lane_mod == mod, flipped, 0.0).astype(LOW)

    def step(index, carry):
        pair = [
            jnp.concatenate([table_ref[2 * index, which], table_ref[2 * index + 1, which]], axis=1)
            for which in range(3)
        ]
        first = pair[0].astype(F32)
        row_ref[...] = pair[1].astype(F32)
        stacked = jnp.concatenate([pair[2]] * MODS, axis=0)
        third_grad = jnp.zeros((V, wide), F32)
        first_grad = jnp.zeros((V, wide), F32)
        for mod in range(MODS):
            third_grad += jnp.dot(
                low_ref[mod * V : (mod + 1) * V, :], pairs_ref[index, mod], preferred_element_type=F32
            )
            cross = jnp.dot(mask_ref[mod], stacked, preferred_element_type=F32)
            for rest in range(SUB):
                value = rest * MODS + mod
                block = cross[rest * V : (rest + 1) * V, :]
                first_grad += block * row_ref[pl.ds(value, 1), :]
                product = block * first
                partial = product[0:8]
                for part in range(1, V // 8):
                    partial += product[8 * part : 8 * part + 8]
                for half in range(2):
                    sum_ref[half, value * 8 : value * 8 + 8, :] = partial[:, half * LANES : (half + 1) * LANES]
        for half in range(2):
            lanes = slice(half * LANES, (half + 1) * LANES)
            second_grad = jnp.zeros((V, LANES), F32)
            for part in range(8):
                second_grad += sum_ref[half, pl.ds(part, V, stride=8), :]
            grads = (first_grad[:, lanes], second_grad, third_grad[:, lanes])
            parts = [
                jnp.concatenate([grad[part * SUB : (part + 1) * SUB, :] for grad in grads], axis=0)
                for part in range(CHUNKS)
            ]
            for chunk, packed in enumerate(exchange(parts)):
                place = (2 * index + half) * CHUNKS + chunk
                out_ref[place] = packed.reshape(3, SUB, LANES).astype(LOW)
        return carry

    lax.fori_loop(0, steps, step, 0, unroll=steps)


def collect_kernel(triples_ref, grads_ref, send_ref, *total_refs):
    groups, attrs = send_ref.shape[0], send_ref.shape[1]
    places = grads_ref.shape[0] // CHUNKS
    for total_ref in total_refs:
        total_ref[...] = jnp.zeros(total_ref.shape, F32)
    for place in range(places):
        for chunk in range(CHUNKS):
            for which, total_ref in enumerate(total_refs):
                attr = triples_ref[which, chunk * places + place]
                total_ref[attr] = total_ref[attr] + grads_ref[place * CHUNKS + chunk, which].astype(F32)
    total = total_refs[0][...] + total_refs[1][...] + total_refs[2][...]
    send_ref[...] = total.reshape(groups, attrs, SUB, LANES).astype(LOW)


def adam_kernel(
    parts_ref, probs_ref, logits_ref, first_ref, second_ref, out_logits_ref, out_first_ref, out_second_ref, grad_ref
):
    groups, attrs = parts_ref.shape[0], parts_ref.shape[1]
    halves = groups // CHUNKS
    chunks = []
    for chunk in range(CHUNKS):
        total = parts_ref[chunk * halves].astype(F32)
        for half in range(1, halves):
            total += parts_ref[chunk * halves + half].astype(F32)
        chunks.append(total.reshape(attrs * SUB, LANES))
    parts = exchange(chunks)
    for attr in range(attrs):
        row_grad = jnp.concatenate([part[attr * SUB : (attr + 1) * SUB, :] for part in parts], axis=0)
        probs = probs_ref[attr]
        inner = jnp.sum(probs * row_grad, axis=0, keepdims=True)
        grad_ref[attr * V : (attr + 1) * V, :] = 512.0 * probs * (row_grad - inner)
    grad = grad_ref[...].T
    new_first = 0.9 * first_ref[...] + 0.1 * grad
    new_second = 0.999 * second_ref[...] + 0.001 * grad * grad
    first_hat = new_first / (1.0 - 0.9**ADAM_STEP)
    second_hat = new_second / (1.0 - 0.999**ADAM_STEP)
    out_logits_ref[...] = logits_ref[...] - 0.5 * first_hat / (jnp.sqrt(second_hat) + 1e-08)
    out_first_ref[...] = new_first
    out_second_ref[...] = new_second


def swap(value, axes):
    return lax.all_to_all(value, axes, 0, 0, tiled=True)


def answers(src):
    shape = jax.ShapeDtypeStruct
    shards = src.shape[0] // CHUNKS
    tall, wide = V * V // MODS, V * MODS
    return call(
        answer_kernel,
        (
            shape((wide, tall), F32),
            shape((wide, tall), LOW),
            shape((shards, 3, V, LANES), LOW),
            shape((shards // 2, MODS, tall, 2 * LANES), LOW),
        ),
        (src,),
        [VMEM],
    )


def backward(scale, table, pairs, base, other):
    shards = table.shape[0]
    tall, wide = V * V // MODS, V * MODS
    return call(
        lambda *refs: backward_kernel(scale, *refs),
        jax.ShapeDtypeStruct((shards * CHUNKS, 3, SUB, LANES), LOW),
        (table, pairs, base, other),
        [VMEM] * 4,
        [
            pltpu.VMEM((wide, tall), LOW),
            pltpu.VMEM((MODS, tall, wide), LOW),
            pltpu.VMEM((V, 2 * LANES), F32),
            pltpu.VMEM((2, 8 * V, LANES), F32),
        ],
    )


def shards(logits, first_moment, second_moment, targets, triples):
    rows, cols = logits.shape
    margs, cells = targets.shape
    attrs = cols // V
    groups = lax.axis_size(MARG_AXES)
    scale = cells / (rows * lax.axis_size(ROW_AXES))
    shape = jax.ShapeDtypeStruct
    tall, wide = V * V // MODS, V * MODS
    place = lax.axis_index(PLACE_AXES).astype(jnp.int32).reshape(1)
    side = lax.axis_index("h").astype(jnp.int32).reshape(1)
    probs, copies = call(
        relax_kernel,
        (shape((attrs, V, rows), F32), shape((groups, attrs + 1, SUB, LANES), LOW)),
        (side, triples.T, logits),
        [SMEM, VMEM, VMEM],
        [pltpu.VMEM((SUB, LANES), F32)],
    )
    full = swap(copies, MARG_AXES)
    picked, attributes = call(
        select_kernel,
        (shape((margs * CHUNKS, 3, SUB, LANES), LOW), shape((SUB, LANES), jnp.int32)),
        (full.reshape(groups * (attrs + 1), SUB, LANES),),
        [VMEM],
        [pltpu.VMEM((SUB, LANES), jnp.int32), pltpu.SMEM((SUB, LANES), jnp.int32), pltpu.SemaphoreType.DMA],
    )
    own, send, table, pairs = answers(swap(picked, SHARE_AXES))
    other = lax.ppermute(send, "u", [(0, 1), (1, 0)])
    base = call(
        lambda *refs: base_kernel(scale, *refs),
        shape((wide, tall), F32),
        (place, own, targets),
        [SMEM, VMEM, ANY],
        [pltpu.VMEM((8, cells), F32), pltpu.VMEM((tall, wide), F32), pltpu.SemaphoreType.DMA],
    )
    returned = swap(backward(scale, table, pairs, base, other), SHARE_AXES)
    totals = call(
        collect_kernel,
        shape((groups, attrs, SUB, LANES), LOW),
        (attributes, returned),
        [SMEM, VMEM],
        [pltpu.VMEM((groups * attrs, SUB, LANES), F32)] * 3,
    )
    return call(
        adam_kernel,
        (shape((rows, cols), F32),) * 3,
        (swap(totals, MARG_AXES), probs, logits, first_moment, second_moment),
        [VMEM] * 5,
        [pltpu.VMEM((cols, rows), F32)],
    )


def solution(mesh):
    fine = Mesh(mesh.devices.reshape(PARTS), NAMES)
    table = P(ROW_AXES, MARG_AXES)
    listed = P(MARG_AXES, None)
    return jax.shard_map(
        shards,
        mesh=fine,
        in_specs=(table, table, table, listed, listed),
        out_specs=(table, table, table),
        check_vma=False,
    )
```

```python
import jax
import jax.numpy as jnp
from jax import lax
from jax.experimental import pallas as pl
from jax.experimental.pallas import tpu as pltpu
from jax.sharding import Mesh, PartitionSpec as P

V = 32
ADAM_STEP = 4
PARTS = (4, 2, 2, 2, 4, 2)
NAMES = ("x", "u", "w", "c", "y", "h")
ROW_AXES = ("x", "u", "w", "c")
MARG_AXES = ("y", "h")
PLACE_AXES = ("x", "w", "c")
SHARE_AXES = ("x", "w", "c", "y")
CHUNKS = 4
CHUNK = 32
LANES = CHUNKS * CHUNK
SUB = V // CHUNKS
MODS = 4
VMEM = pl.BlockSpec(memory_space=pltpu.VMEM)
SMEM = pl.BlockSpec(memory_space=pltpu.SMEM)
ANY = pl.BlockSpec(memory_space=pl.ANY)
LIMIT = 20 * 1024 * 1024
F32 = jnp.float32
LOW = jnp.bfloat16


def call(body, out_shape, operands, specs, scratch=()):
    return pl.pallas_call(
        body,
        out_shape=out_shape,
        in_specs=specs,
        out_specs=jax.tree.map(lambda unused: VMEM, out_shape),
        scratch_shapes=scratch,
        compiler_params=pltpu.CompilerParams(vmem_limit_bytes=LIMIT),
    )(*operands)


def exchange(blocks):
    lane = lax.broadcasted_iota(jnp.int32, blocks[0].shape, 1)
    blocks = list(blocks)
    for width, pairs in ((2 * CHUNK, ((0, 2), (1, 3))), (CHUNK, ((0, 1), (2, 3)))):
        low_part = (lane // width) % 2 == 0
        for a, b in pairs:
            left, right = blocks[a], blocks[b]
            blocks[a] = jnp.where(low_part, left, pltpu.roll(right, width, 1))
            blocks[b] = jnp.where(low_part, pltpu.roll(left, LANES - width, 1), right)
    return blocks


def relax_kernel(side_ref, triples_ref, logits_ref, probs_ref, send_ref, tile_ref):
    flipped = logits_ref[...].T
    attrs = probs_ref.shape[0]
    halves = send_ref.shape[0] // CHUNKS
    for attr in range(attrs):
        block = flipped[attr * V : (attr + 1) * V, :]
        top = jnp.max(block, axis=0, keepdims=True)
        expo = jnp.exp(block - top)
        probs = expo / jnp.sum(expo, axis=0, keepdims=True)
        probs_ref[attr] = probs
        chunks = exchange([probs[part * SUB : (part + 1) * SUB, :] for part in range(CHUNKS)])
        for chunk in range(CHUNKS):
            low = chunks[chunk].astype(LOW)
            for half in range(halves):
                send_ref[chunk * halves + half, attr] = low
    tile_ref[...] = jnp.zeros(tile_ref.shape, F32)
    tile_ref[0:3, 0 : triples_ref.shape[1]] = triples_ref[...].astype(F32)
    for half in range(halves):
        tile = (tile_ref[...] * jnp.where(side_ref[0] == half, 1.0, 0.0)).astype(LOW)
        for chunk in range(CHUNKS):
            send_ref[chunk * halves + half, attrs] = tile


def select_kernel(full_ref, send_ref, triples_ref, index_ref, scalar_ref, sem):
    slots = full_ref.shape[0] // (2 * CHUNKS)
    places = send_ref.shape[0] // CHUNKS
    triples = jnp.zeros(triples_ref.shape, F32)
    for chunk in range(CHUNKS):
        tile = full_ref[2 * chunk * slots + slots - 1].astype(F32) + full_ref[(2 * chunk + 2) * slots - 1].astype(F32)
        triples += pltpu.roll(tile, chunk * places, 1) if chunk else tile
    attrs = triples.astype(jnp.int32)
    triples_ref[...] = attrs
    index_ref[...] = attrs + attrs // (slots - 1)
    copy = pltpu.make_async_copy(index_ref, scalar_ref, sem)
    copy.start()
    copy.wait()
    for place in range(places):
        for chunk in range(CHUNKS):
            for which in range(3):
                send_ref[place * CHUNKS + chunk, which] = full_ref[scalar_ref[which, chunk * places + place]]


def unpack(src_ref, shard):
    packed = [src_ref[shard * CHUNKS + chunk].astype(F32).reshape(3 * SUB, LANES) for chunk in range(CHUNKS)]
    parts = exchange(packed)
    return [
        jnp.concatenate([part[which * SUB : (which + 1) * SUB, :] for part in parts], axis=0) for which in range(3)
    ]


def answer_kernel(src_ref, own_ref, send_ref, table_ref, pairs_ref):
    shards = table_ref.shape[0]

    def fill(step):
        for part in range(2):
            shard = 2 * step + part
            first, second, third = [value.astype(LOW) for value in unpack(src_ref, shard)]
            table_ref[shard, 0] = first
            table_ref[shard, 1] = second
            table_ref[shard, 2] = third
            for value in range(V):
                row = jnp.broadcast_to(second[value : value + 1, :], first.shape)
                mod, rest = value % MODS, value // MODS
                pairs_ref[step, mod, rest * V : (rest + 1) * V, part * LANES : (part + 1) * LANES] = first * row

    def add(step):
        third = jnp.concatenate([table_ref[2 * step, 2], table_ref[2 * step + 1, 2]], axis=1)
        for mod in range(MODS):
            own_ref[mod * V : (mod + 1) * V, :] += lax.dot_general(
                third, pairs_ref[step, mod], (((1,), (1,)), ((), ())), preferred_element_type=F32
            )

    own_ref[...] = jnp.zeros(own_ref.shape, F32)
    fill(0)

    def both(step, carry):
        add(step - 1)
        fill(step)
        return carry

    lax.fori_loop(1, shards // 2, both, 0, unroll=shards // 2 - 1)
    add(shards // 2 - 1)
    send_ref[...] = own_ref[...].astype(LOW)


def base_kernel(scale, place_ref, own_ref, targets_any, base_ref, block_ref, target_ref, sem):
    place = place_ref[0]
    start = pl.multiple_of(place // 8 * 8, 8)
    copy = pltpu.make_async_copy(targets_any.at[pl.ds(start, 8), :], block_ref, sem)
    copy.start()
    copy.wait()
    mine = lax.broadcasted_iota(jnp.int32, (8, LANES), 0) == lax.rem(place, 8)
    for rest in range(SUB):
        for value in range(V):
            tile = block_ref[:, pl.ds((value * SUB + rest) * LANES, LANES)]
            row = jnp.sum(jnp.where(mine, tile, 0.0), axis=0, keepdims=True)
            target_ref[pl.ds(rest * V + value, 1), :] = row
    base_ref[...] = scale * own_ref[...] - target_ref[...].T


def backward_kernel(scale, table_ref, pairs_ref, base_ref, other_ref, out_ref, low_ref, mask_ref, row_ref, sum_ref):
    steps = pairs_ref.shape[0]
    wide = 2 * LANES
    resid = base_ref[...] + scale * other_ref[...].astype(F32)
    low_ref[...] = resid.astype(LOW)
    flipped = resid.T
    lane_mod = lax.broadcasted_iota(jnp.int32, flipped.shape, 1) // V
    for mod in range(MODS):
        mask_ref[mod] = jnp.where(lane_mod == mod, flipped, 0.0).astype(LOW)

    def step(index, carry):
        pair = [
            jnp.concatenate([table_ref[2 * index, which], table_ref[2 * index + 1, which]], axis=1)
            for which in range(3)
        ]
        first = pair[0].astype(F32)
        row_ref[...] = pair[1].astype(F32)
        stacked = jnp.concatenate([pair[2]] * MODS, axis=0)
        third_grad = jnp.zeros((V, wide), F32)
        first_grad = jnp.zeros((V, wide), F32)
        for mod in range(MODS):
            third_grad += jnp.dot(
                low_ref[mod * V : (mod + 1) * V, :], pairs_ref[index, mod], preferred_element_type=F32
            )
            cross = jnp.dot(mask_ref[mod], stacked, preferred_element_type=F32)
            for rest in range(SUB):
                value = rest * MODS + mod
                block = cross[rest * V : (rest + 1) * V, :]
                first_grad += block * row_ref[pl.ds(value, 1), :]
                product = block * first
                partial = product[0:8]
                for part in range(1, V // 8):
                    partial += product[8 * part : 8 * part + 8]
                for half in range(2):
                    sum_ref[half, value * 8 : value * 8 + 8, :] = partial[:, half * LANES : (half + 1) * LANES]
        for half in range(2):
            lanes = slice(half * LANES, (half + 1) * LANES)
            second_grad = jnp.zeros((V, LANES), F32)
            for part in range(8):
                second_grad += sum_ref[half, pl.ds(part, V, stride=8), :]
            grads = (first_grad[:, lanes], second_grad, third_grad[:, lanes])
            parts = [
                jnp.concatenate([grad[part * SUB : (part + 1) * SUB, :] for grad in grads], axis=0)
                for part in range(CHUNKS)
            ]
            for chunk, packed in enumerate(exchange(parts)):
                place = (2 * index + half) * CHUNKS + chunk
                out_ref[place] = packed.reshape(3, SUB, LANES).astype(LOW)
        return carry

    lax.fori_loop(0, steps, step, 0, unroll=steps)


def collect_kernel(triples_ref, grads_ref, send_ref, *total_refs):
    groups, attrs = send_ref.shape[0], send_ref.shape[1]
    places = grads_ref.shape[0] // CHUNKS
    for total_ref in total_refs:
        total_ref[...] = jnp.zeros(total_ref.shape, F32)
    for place in range(places):
        for chunk in range(CHUNKS):
            for which, total_ref in enumerate(total_refs):
                attr = triples_ref[which, chunk * places + place]
                total_ref[attr] = total_ref[attr] + grads_ref[place * CHUNKS + chunk, which].astype(F32)
    total = total_refs[0][...] + total_refs[1][...] + total_refs[2][...]
    send_ref[...] = total.reshape(groups, attrs, SUB, LANES).astype(LOW)


def adam_kernel(
    parts_ref, probs_ref, logits_ref, first_ref, second_ref, out_logits_ref, out_first_ref, out_second_ref, grad_ref
):
    groups, attrs = parts_ref.shape[0], parts_ref.shape[1]
    halves = groups // CHUNKS
    chunks = []
    for chunk in range(CHUNKS):
        total = parts_ref[chunk * halves].astype(F32)
        for half in range(1, halves):
            total += parts_ref[chunk * halves + half].astype(F32)
        chunks.append(total.reshape(attrs * SUB, LANES))
    parts = exchange(chunks)
    for attr in range(attrs):
        row_grad = jnp.concatenate([part[attr * SUB : (attr + 1) * SUB, :] for part in parts], axis=0)
        probs = probs_ref[attr]
        inner = jnp.sum(probs * row_grad, axis=0, keepdims=True)
        grad_ref[attr * V : (attr + 1) * V, :] = 512.0 * probs * (row_grad - inner)
    grad = grad_ref[...].T
    new_first = 0.9 * first_ref[...] + 0.1 * grad
    new_second = 0.999 * second_ref[...] + 0.001 * grad * grad
    first_hat = new_first / (1.0 - 0.9**ADAM_STEP)
    second_hat = new_second / (1.0 - 0.999**ADAM_STEP)
    out_logits_ref[...] = logits_ref[...] - 0.5 * first_hat / (jnp.sqrt(second_hat) + 1e-08)
    out_first_ref[...] = new_first
    out_second_ref[...] = new_second


def swap(value, axes):
    return lax.all_to_all(value, axes, 0, 0, tiled=True)


def answers(src):
    shape = jax.ShapeDtypeStruct
    shards = src.shape[0] // CHUNKS
    tall, wide = V * V // MODS, V * MODS
    return call(
        answer_kernel,
        (
            shape((wide, tall), F32),
            shape((wide, tall), LOW),
            shape((shards, 3, V, LANES), LOW),
            shape((shards // 2, MODS, tall, 2 * LANES), LOW),
        ),
        (src,),
        [VMEM],
    )


def backward(scale, table, pairs, base, other):
    shards = table.shape[0]
    tall, wide = V * V // MODS, V * MODS
    return call(
        lambda *refs: backward_kernel(scale, *refs),
        jax.ShapeDtypeStruct((shards * CHUNKS, 3, SUB, LANES), LOW),
        (table, pairs, base, other),
        [VMEM] * 4,
        [
            pltpu.VMEM((wide, tall), LOW),
            pltpu.VMEM((MODS, tall, wide), LOW),
            pltpu.VMEM((V, 2 * LANES), F32),
            pltpu.VMEM((2, 8 * V, LANES), F32),
        ],
    )


def shards(logits, first_moment, second_moment, targets, triples):
    rows, cols = logits.shape
    margs, cells = targets.shape
    attrs = cols // V
    groups = lax.axis_size(MARG_AXES)
    scale = cells / (rows * lax.axis_size(ROW_AXES))
    shape = jax.ShapeDtypeStruct
    tall, wide = V * V // MODS, V * MODS
    place = lax.axis_index(PLACE_AXES).astype(jnp.int32).reshape(1)
    side = lax.axis_index("h").astype(jnp.int32).reshape(1)
    probs, copies = call(
        relax_kernel,
        (shape((attrs, V, rows), F32), shape((groups, attrs + 1, SUB, LANES), LOW)),
        (side, triples.T, logits),
        [SMEM, VMEM, VMEM],
        [pltpu.VMEM((SUB, LANES), F32)],
    )
    full = swap(copies, MARG_AXES)
    picked, attributes = call(
        select_kernel,
        (shape((margs * CHUNKS, 3, SUB, LANES), LOW), shape((SUB, LANES), jnp.int32)),
        (full.reshape(groups * (attrs + 1), SUB, LANES),),
        [VMEM],
        [pltpu.VMEM((SUB, LANES), jnp.int32), pltpu.SMEM((SUB, LANES), jnp.int32), pltpu.SemaphoreType.DMA],
    )
    own, send, table, pairs = answers(swap(picked, SHARE_AXES))
    other = lax.ppermute(send, "u", [(0, 1), (1, 0)])
    base = call(
        lambda *refs: base_kernel(scale, *refs),
        shape((wide, tall), F32),
        (place, own, targets),
        [SMEM, VMEM, ANY],
        [pltpu.VMEM((8, cells), F32), pltpu.VMEM((tall, wide), F32), pltpu.SemaphoreType.DMA],
    )
    returned = swap(backward(scale, table, pairs, base, other), SHARE_AXES)
    totals = call(
        collect_kernel,
        shape((groups, attrs, SUB, LANES), LOW),
        (attributes, returned),
        [SMEM, VMEM],
        [pltpu.VMEM((groups * attrs, SUB, LANES), F32)] * 3,
    )
    return call(
        adam_kernel,
        (shape((rows, cols), F32),) * 3,
        (swap(totals, MARG_AXES), probs, logits, first_moment, second_moment),
        [VMEM] * 5,
        [pltpu.VMEM((cols, rows), F32)],
    )


def solution(mesh):
    fine = Mesh(mesh.devices.reshape(PARTS), NAMES)
    table = P(ROW_AXES, MARG_AXES)
    listed = P(MARG_AXES, None)
    return jax.shard_map(
        shards,
        mesh=fine,
        in_specs=(table, table, table, listed, listed),
        out_specs=(table, table, table),
        check_vma=False,
    )
```

```python
import jax
import jax.numpy as jnp
from jax import lax
from jax.experimental import pallas as pl
from jax.experimental.pallas import tpu as pltpu
from jax.sharding import Mesh, PartitionSpec as P

V = 32
ADAM_STEP = 4
PARTS = (4, 2, 2, 2, 4, 2)
NAMES = ("x", "u", "w", "c", "y", "h")
ROW_AXES = ("x", "u", "w", "c")
MARG_AXES = ("y", "h")
PLACE_AXES = ("x", "w", "c")
SHARE_AXES = ("x", "w", "c", "y")
CHUNKS = 4
CHUNK = 32
LANES = CHUNKS * CHUNK
SUB = V // CHUNKS
MODS = 4
VMEM = pl.BlockSpec(memory_space=pltpu.VMEM)
SMEM = pl.BlockSpec(memory_space=pltpu.SMEM)
ANY = pl.BlockSpec(memory_space=pl.ANY)
LIMIT = 20 * 1024 * 1024
F32 = jnp.float32
LOW = jnp.bfloat16


def call(body, out_shape, operands, specs, scratch=()):
    return pl.pallas_call(
        body,
        out_shape=out_shape,
        in_specs=specs,
        out_specs=jax.tree.map(lambda unused: VMEM, out_shape),
        scratch_shapes=scratch,
        compiler_params=pltpu.CompilerParams(vmem_limit_bytes=LIMIT),
    )(*operands)


def exchange(blocks):
    lane = lax.broadcasted_iota(jnp.int32, blocks[0].shape, 1)
    blocks = list(blocks)
    for width, pairs in ((2 * CHUNK, ((0, 2), (1, 3))), (CHUNK, ((0, 1), (2, 3)))):
        low_part = (lane // width) % 2 == 0
        for a, b in pairs:
            left, right = blocks[a], blocks[b]
            blocks[a] = jnp.where(low_part, left, pltpu.roll(right, width, 1))
            blocks[b] = jnp.where(low_part, pltpu.roll(left, LANES - width, 1), right)
    return blocks


def relax_kernel(side_ref, place_ref, triples_ref, logits_ref, probs_ref, send_ref, tile_ref):
    flipped = logits_ref[...].T
    attrs = probs_ref.shape[0]
    halves = send_ref.shape[0] // CHUNKS
    for attr in range(attrs):
        block = flipped[attr * V : (attr + 1) * V, :]
        top = jnp.max(block, axis=0, keepdims=True)
        expo = jnp.exp(block - top)
        probs = expo / jnp.sum(expo, axis=0, keepdims=True)
        probs_ref[attr] = probs
        chunks = exchange([probs[part * SUB : (part + 1) * SUB, :] for part in range(CHUNKS)])
        for chunk in range(CHUNKS):
            low = chunks[chunk].astype(LOW)
            for half in range(halves):
                send_ref[chunk * halves + half, attr] = low
    tile_ref[...] = jnp.zeros(tile_ref.shape, F32)
    tile_ref[0:3, 0 : triples_ref.shape[1]] = triples_ref[...].astype(F32)
    for half in range(halves):
        tile = (tile_ref[...] * jnp.where(side_ref[0] == half, 1.0, 0.0)).astype(LOW)
        for chunk in range(CHUNKS):
            send_ref[chunk * halves + half, attrs] = tile


def select_kernel(full_ref, send_ref, triples_ref, index_ref, scalar_ref, sem):
    slots = full_ref.shape[0] // (2 * CHUNKS)
    places = send_ref.shape[0] // CHUNKS
    triples = jnp.zeros(triples_ref.shape, F32)
    for chunk in range(CHUNKS):
        tile = full_ref[2 * chunk * slots + slots - 1].astype(F32) + full_ref[(2 * chunk + 2) * slots - 1].astype(F32)
        triples += pltpu.roll(tile, chunk * places, 1) if chunk else tile
    attrs = triples.astype(jnp.int32)
    triples_ref[...] = attrs
    index_ref[...] = attrs + attrs // (slots - 1)
    copy = pltpu.make_async_copy(index_ref, scalar_ref, sem)
    copy.start()
    copy.wait()
    for place in range(places):
        for chunk in range(CHUNKS):
            for which in range(3):
                send_ref[place * CHUNKS + chunk, which] = full_ref[scalar_ref[which, chunk * places + place]]


def unpack(src_ref, shard):
    packed = [src_ref[shard * CHUNKS + chunk].astype(F32).reshape(3 * SUB, LANES) for chunk in range(CHUNKS)]
    parts = exchange(packed)
    return [
        jnp.concatenate([part[which * SUB : (which + 1) * SUB, :] for part in parts], axis=0) for which in range(3)
    ]


def answer_kernel(src_ref, own_ref, send_ref, table_ref, pairs_ref):
    shards = table_ref.shape[0]

    def fill(step):
        for part in range(2):
            shard = 2 * step + part
            first, second, third = [value.astype(LOW) for value in unpack(src_ref, shard)]
            table_ref[shard, 0] = first
            table_ref[shard, 1] = second
            table_ref[shard, 2] = third
            for value in range(V):
                row = jnp.broadcast_to(second[value : value + 1, :], first.shape)
                mod, rest = value % MODS, value // MODS
                pairs_ref[step, mod, rest * V : (rest + 1) * V, part * LANES : (part + 1) * LANES] = first * row

    def add(step):
        third = jnp.concatenate([table_ref[2 * step, 2], table_ref[2 * step + 1, 2]], axis=1)
        for mod in range(MODS):
            own_ref[mod * V : (mod + 1) * V, :] += lax.dot_general(
                third, pairs_ref[step, mod], (((1,), (1,)), ((), ())), preferred_element_type=F32
            )

    own_ref[...] = jnp.zeros(own_ref.shape, F32)
    fill(0)

    def both(step, carry):
        add(step - 1)
        fill(step)
        return carry

    lax.fori_loop(1, shards // 2, both, 0, unroll=shards // 2 - 1)
    add(shards // 2 - 1)
    send_ref[...] = own_ref[...].astype(LOW)


def base_kernel(scale, place_ref, own_ref, targets_any, base_ref, block_ref, target_ref, sem):
    place = place_ref[0]
    start = pl.multiple_of(place // 8 * 8, 8)
    copy = pltpu.make_async_copy(targets_any.at[pl.ds(start, 8), :], block_ref, sem)
    copy.start()
    copy.wait()
    mine = lax.broadcasted_iota(jnp.int32, (8, LANES), 0) == lax.rem(place, 8)
    for rest in range(SUB):
        for value in range(V):
            tile = block_ref[:, pl.ds((value * SUB + rest) * LANES, LANES)]
            row = jnp.sum(jnp.where(mine, tile, 0.0), axis=0, keepdims=True)
            target_ref[pl.ds(rest * V + value, 1), :] = row
    base_ref[...] = scale * own_ref[...] - target_ref[...].T


def backward_kernel(scale, table_ref, pairs_ref, base_ref, other_ref, out_ref, low_ref, mask_ref, row_ref, sum_ref):
    steps = pairs_ref.shape[0]
    wide = 2 * LANES
    resid = base_ref[...] + scale * other_ref[...].astype(F32)
    low_ref[...] = resid.astype(LOW)
    flipped = resid.T
    lane_mod = lax.broadcasted_iota(jnp.int32, flipped.shape, 1) // V
    for mod in range(MODS):
        mask_ref[mod] = jnp.where(lane_mod == mod, flipped, 0.0).astype(LOW)

    def step(index, carry):
        pair = [
            jnp.concatenate([table_ref[2 * index, which], table_ref[2 * index + 1, which]], axis=1)
            for which in range(3)
        ]
        first = pair[0].astype(F32)
        row_ref[...] = pair[1].astype(F32)
        stacked = jnp.concatenate([pair[2]] * MODS, axis=0)
        third_grad = jnp.zeros((V, wide), F32)
        first_grad = jnp.zeros((V, wide), F32)
        for mod in range(MODS):
            third_grad += jnp.dot(
                low_ref[mod * V : (mod + 1) * V, :], pairs_ref[index, mod], preferred_element_type=F32
            )
            cross = jnp.dot(mask_ref[mod], stacked, preferred_element_type=F32)
            for rest in range(SUB):
                value = rest * MODS + mod
                block = cross[rest * V : (rest + 1) * V, :]
                first_grad += block * row_ref[pl.ds(value, 1), :]
                product = block * first
                partial = product[0:8]
                for part in range(1, V // 8):
                    partial += product[8 * part : 8 * part + 8]
                for half in range(2):
                    sum_ref[half, value * 8 : value * 8 + 8, :] = partial[:, half * LANES : (half + 1) * LANES]
        for half in range(2):
            lanes = slice(half * LANES, (half + 1) * LANES)
            second_grad = jnp.zeros((V, LANES), F32)
            for part in range(8):
                second_grad += sum_ref[half, pl.ds(part, V, stride=8), :]
            grads = (first_grad[:, lanes], second_grad, third_grad[:, lanes])
            parts = [
                jnp.concatenate([grad[part * SUB : (part + 1) * SUB, :] for grad in grads], axis=0)
                for part in range(CHUNKS)
            ]
            for chunk, packed in enumerate(exchange(parts)):
                place = (2 * index + half) * CHUNKS + chunk
                out_ref[place] = packed.reshape(3, SUB, LANES).astype(LOW)
        return carry

    lax.fori_loop(0, steps, step, 0, unroll=steps)


def collect_kernel(triples_ref, grads_ref, send_ref, *total_refs):
    groups, attrs = send_ref.shape[0], send_ref.shape[1]
    places = grads_ref.shape[0] // CHUNKS
    for total_ref in total_refs:
        total_ref[...] = jnp.zeros(total_ref.shape, F32)
    for place in range(places):
        for chunk in range(CHUNKS):
            for which, total_ref in enumerate(total_refs):
                attr = triples_ref[which, chunk * places + place]
                total_ref[attr] = total_ref[attr] + grads_ref[place * CHUNKS + chunk, which].astype(F32)
    total = total_refs[0][...] + total_refs[1][...] + total_refs[2][...]
    send_ref[...] = total.reshape(groups, attrs, SUB, LANES).astype(LOW)


def adam_kernel(
    parts_ref, probs_ref, logits_ref, first_ref, second_ref, out_logits_ref, out_first_ref, out_second_ref, grad_ref
):
    groups, attrs = parts_ref.shape[0], parts_ref.shape[1]
    halves = groups // CHUNKS
    chunks = []
    for chunk in range(CHUNKS):
        total = parts_ref[chunk * halves].astype(F32)
        for half in range(1, halves):
            total += parts_ref[chunk * halves + half].astype(F32)
        chunks.append(total.reshape(attrs * SUB, LANES))
    parts = exchange(chunks)
    for attr in range(attrs):
        row_grad = jnp.concatenate([part[attr * SUB : (attr + 1) * SUB, :] for part in parts], axis=0)
        probs = probs_ref[attr]
        inner = jnp.sum(probs * row_grad, axis=0, keepdims=True)
        grad_ref[attr * V : (attr + 1) * V, :] = 512.0 * probs * (row_grad - inner)
    grad = grad_ref[...].T
    new_first = 0.9 * first_ref[...] + 0.1 * grad
    new_second = 0.999 * second_ref[...] + 0.001 * grad * grad
    first_hat = new_first / (1.0 - 0.9**ADAM_STEP)
    second_hat = new_second / (1.0 - 0.999**ADAM_STEP)
    out_logits_ref[...] = logits_ref[...] - 0.5 * first_hat / (jnp.sqrt(second_hat) + 1e-08)
    out_first_ref[...] = new_first
    out_second_ref[...] = new_second


def swap(value, axes):
    return lax.all_to_all(value, axes, 0, 0, tiled=True)


def answers(src):
    shape = jax.ShapeDtypeStruct
    shards = src.shape[0] // CHUNKS
    tall, wide = V * V // MODS, V * MODS
    return call(
        answer_kernel,
        (
            shape((wide, tall), F32),
            shape((wide, tall), LOW),
            shape((shards, 3, V, LANES), LOW),
            shape((shards // 2, MODS, tall, 2 * LANES), LOW),
        ),
        (src,),
        [VMEM],
    )


def backward(scale, table, pairs, base, other):
    shards = table.shape[0]
    tall, wide = V * V // MODS, V * MODS
    return call(
        lambda *refs: backward_kernel(scale, *refs),
        jax.ShapeDtypeStruct((shards * CHUNKS, 3, SUB, LANES), LOW),
        (table, pairs, base, other),
        [VMEM] * 4,
        [
            pltpu.VMEM((wide, tall), LOW),
            pltpu.VMEM((MODS, tall, wide), LOW),
            pltpu.VMEM((V, 2 * LANES), F32),
            pltpu.VMEM((2, 8 * V, LANES), F32),
        ],
    )


def shards(logits, first_moment, second_moment, targets, triples):
    rows, cols = logits.shape
    margs, cells = targets.shape
    attrs = cols // V
    groups = lax.axis_size(MARG_AXES)
    scale = cells / (rows * lax.axis_size(ROW_AXES))
    shape = jax.ShapeDtypeStruct
    tall, wide = V * V // MODS, V * MODS
    place = lax.axis_index(PLACE_AXES).astype(jnp.int32).reshape(1)
    side = lax.axis_index("h").astype(jnp.int32).reshape(1)
    probs, copies = call(
        relax_kernel,
        (shape((attrs, V, rows), F32), shape((groups, attrs + 1, SUB, LANES), LOW)),
        (side, place, triples.T, logits),
        [SMEM, SMEM, VMEM, VMEM],
        [pltpu.VMEM((SUB, LANES), F32)],
    )
    full = swap(copies, MARG_AXES)
    picked, attributes = call(
        select_kernel,
        (shape((margs * CHUNKS, 3, SUB, LANES), LOW), shape((SUB, LANES), jnp.int32)),
        (full.reshape(groups * (attrs + 1), SUB, LANES),),
        [VMEM],
        [pltpu.VMEM((SUB, LANES), jnp.int32), pltpu.SMEM((SUB, LANES), jnp.int32), pltpu.SemaphoreType.DMA],
    )
    own, send, table, pairs = answers(swap(picked, SHARE_AXES))
    other = lax.ppermute(send, "u", [(0, 1), (1, 0)])
    base = call(
        lambda *refs: base_kernel(scale, *refs),
        shape((wide, tall), F32),
        (place, own, targets),
        [SMEM, VMEM, ANY],
        [pltpu.VMEM((8, cells), F32), pltpu.VMEM((tall, wide), F32), pltpu.SemaphoreType.DMA],
    )
    returned = swap(backward(scale, table, pairs, base, other), SHARE_AXES)
    totals = call(
        collect_kernel,
        shape((groups, attrs, SUB, LANES), LOW),
        (attributes, returned),
        [SMEM, VMEM],
        [pltpu.VMEM((groups * attrs, SUB, LANES), F32)] * 3,
    )
    return call(
        adam_kernel,
        (shape((rows, cols), F32),) * 3,
        (swap(totals, MARG_AXES), probs, logits, first_moment, second_moment),
        [VMEM] * 5,
        [pltpu.VMEM((cols, rows), F32)],
    )


def solution(mesh):
    fine = Mesh(mesh.devices.reshape(PARTS), NAMES)
    table = P(ROW_AXES, MARG_AXES)
    listed = P(MARG_AXES, None)
    return jax.shard_map(
        shards,
        mesh=fine,
        in_specs=(table, table, table, listed, listed),
        out_specs=(table, table, table),
        check_vma=False,
    )
```

```python
import jax
import jax.numpy as jnp
from jax import lax
from jax.experimental import pallas as pl
from jax.experimental.pallas import tpu as pltpu
from jax.sharding import Mesh, PartitionSpec as P

V = 32
ADAM_STEP = 4
PARTS = (4, 2, 2, 2, 4, 2)
NAMES = ("x", "u", "w", "c", "y", "h")
ROW_AXES = ("x", "u", "w", "c")
MARG_AXES = ("y", "h")
PLACE_AXES = ("x", "w", "c")
SHARE_AXES = ("x", "w", "c", "y")
CHUNKS = 4
CHUNK = 32
LANES = CHUNKS * CHUNK
SUB = V // CHUNKS
MODS = 4
VMEM = pl.BlockSpec(memory_space=pltpu.VMEM)
SMEM = pl.BlockSpec(memory_space=pltpu.SMEM)
ANY = pl.BlockSpec(memory_space=pl.ANY)
LIMIT = 20 * 1024 * 1024
F32 = jnp.float32
LOW = jnp.bfloat16


def call(body, out_shape, operands, specs, scratch=()):
    return pl.pallas_call(
        body,
        out_shape=out_shape,
        in_specs=specs,
        out_specs=jax.tree.map(lambda unused: VMEM, out_shape),
        scratch_shapes=scratch,
        compiler_params=pltpu.CompilerParams(vmem_limit_bytes=LIMIT),
    )(*operands)


def exchange(blocks):
    lane = lax.broadcasted_iota(jnp.int32, blocks[0].shape, 1)
    blocks = list(blocks)
    for width, pairs in ((2 * CHUNK, ((0, 2), (1, 3))), (CHUNK, ((0, 1), (2, 3)))):
        low_part = (lane // width) % 2 == 0
        for a, b in pairs:
            left, right = blocks[a], blocks[b]
            blocks[a] = jnp.where(low_part, left, pltpu.roll(right, width, 1))
            blocks[b] = jnp.where(low_part, pltpu.roll(left, LANES - width, 1), right)
    return blocks


def stay(value):
    return pltpu.with_memory_space_constraint(value, pltpu.HBM)


def relax_kernel(
    side_ref, place_ref, triples_hbm, logits_hbm, probs_ref, send_ref, tile_ref, triples_ref, logits_ref, sems
):
    logits_copy = pltpu.make_async_copy(logits_hbm, logits_ref, sems.at[0])
    triples_copy = pltpu.make_async_copy(triples_hbm, triples_ref, sems.at[1])
    logits_copy.start()
    triples_copy.start()
    logits_copy.wait()
    flipped = logits_ref[...].T
    attrs = probs_ref.shape[0]
    halves = send_ref.shape[0] // CHUNKS
    for attr in range(attrs):
        block = flipped[attr * V : (attr + 1) * V, :]
        top = jnp.max(block, axis=0, keepdims=True)
        expo = jnp.exp(block - top)
        probs = expo / jnp.sum(expo, axis=0, keepdims=True)
        probs_ref[attr] = probs
        chunks = exchange([probs[part * SUB : (part + 1) * SUB, :] for part in range(CHUNKS)])
        for chunk in range(CHUNKS):
            low = chunks[chunk].astype(LOW)
            for half in range(halves):
                send_ref[chunk * halves + half, attr] = low
    triples_copy.wait()
    tile_ref[...] = jnp.zeros(tile_ref.shape, F32)
    tile_ref[0:3, 0 : triples_ref.shape[1]] = triples_ref[...].astype(F32)
    for half in range(halves):
        tile = (tile_ref[...] * jnp.where(side_ref[0] == half, 1.0, 0.0)).astype(LOW)
        for chunk in range(CHUNKS):
            send_ref[chunk * halves + half, attrs] = tile


def select_kernel(full_ref, send_ref, triples_ref, index_ref, scalar_ref, sem):
    slots = full_ref.shape[0] // (2 * CHUNKS)
    places = send_ref.shape[0] // CHUNKS
    triples = jnp.zeros(triples_ref.shape, F32)
    for chunk in range(CHUNKS):
        tile = full_ref[2 * chunk * slots + slots - 1].astype(F32) + full_ref[(2 * chunk + 2) * slots - 1].astype(F32)
        triples += pltpu.roll(tile, chunk * places, 1) if chunk else tile
    attrs = triples.astype(jnp.int32)
    triples_ref[...] = attrs
    index_ref[...] = attrs + attrs // (slots - 1)
    copy = pltpu.make_async_copy(index_ref, scalar_ref, sem)
    copy.start()
    copy.wait()
    for place in range(places):
        for chunk in range(CHUNKS):
            for which in range(3):
                send_ref[place * CHUNKS + chunk, which] = full_ref[scalar_ref[which, chunk * places + place]]


def unpack(src_ref, shard):
    packed = [src_ref[shard * CHUNKS + chunk].astype(F32).reshape(3 * SUB, LANES) for chunk in range(CHUNKS)]
    parts = exchange(packed)
    return [
        jnp.concatenate([part[which * SUB : (which + 1) * SUB, :] for part in parts], axis=0) for which in range(3)
    ]


def answer_kernel(src_ref, own_ref, send_ref, table_ref, pairs_ref):
    shards = table_ref.shape[0]

    def fill(step):
        for part in range(2):
            shard = 2 * step + part
            first, second, third = [value.astype(LOW) for value in unpack(src_ref, shard)]
            table_ref[shard, 0] = first
            table_ref[shard, 1] = second
            table_ref[shard, 2] = third
            for value in range(V):
                row = jnp.broadcast_to(second[value : value + 1, :], first.shape)
                mod, rest = value % MODS, value // MODS
                pairs_ref[step, mod, rest * V : (rest + 1) * V, part * LANES : (part + 1) * LANES] = first * row

    def add(step):
        third = jnp.concatenate([table_ref[2 * step, 2], table_ref[2 * step + 1, 2]], axis=1)
        for mod in range(MODS):
            own_ref[mod * V : (mod + 1) * V, :] += lax.dot_general(
                third, pairs_ref[step, mod], (((1,), (1,)), ((), ())), preferred_element_type=F32
            )

    own_ref[...] = jnp.zeros(own_ref.shape, F32)
    fill(0)

    def both(step, carry):
        add(step - 1)
        fill(step)
        return carry

    lax.fori_loop(1, shards // 2, both, 0, unroll=shards // 2 - 1)
    add(shards // 2 - 1)
    send_ref[...] = own_ref[...].astype(LOW)


def base_kernel(scale, place_ref, own_ref, targets_any, base_ref, block_ref, target_ref, sem):
    place = place_ref[0]
    start = pl.multiple_of(place // 8 * 8, 8)
    copy = pltpu.make_async_copy(targets_any.at[pl.ds(start, 8), :], block_ref, sem)
    copy.start()
    copy.wait()
    mine = lax.broadcasted_iota(jnp.int32, (8, LANES), 0) == lax.rem(place, 8)
    for rest in range(SUB):
        for value in range(V):
            tile = block_ref[:, pl.ds((value * SUB + rest) * LANES, LANES)]
            row = jnp.sum(jnp.where(mine, tile, 0.0), axis=0, keepdims=True)
            target_ref[pl.ds(rest * V + value, 1), :] = row
    base_ref[...] = scale * own_ref[...] - target_ref[...].T


def backward_kernel(scale, table_ref, pairs_ref, base_ref, other_ref, out_ref, low_ref, mask_ref, row_ref, sum_ref):
    steps = pairs_ref.shape[0]
    wide = 2 * LANES
    resid = base_ref[...] + scale * other_ref[...].astype(F32)
    low_ref[...] = resid.astype(LOW)
    flipped = resid.T
    lane_mod = lax.broadcasted_iota(jnp.int32, flipped.shape, 1) // V
    for mod in range(MODS):
        mask_ref[mod] = jnp.where(lane_mod == mod, flipped, 0.0).astype(LOW)

    def step(index, carry):
        pair = [
            jnp.concatenate([table_ref[2 * index, which], table_ref[2 * index + 1, which]], axis=1)
            for which in range(3)
        ]
        first = pair[0].astype(F32)
        row_ref[...] = pair[1].astype(F32)
        stacked = jnp.concatenate([pair[2]] * MODS, axis=0)
        third_grad = jnp.zeros((V, wide), F32)
        first_grad = jnp.zeros((V, wide), F32)
        for mod in range(MODS):
            third_grad += jnp.dot(
                low_ref[mod * V : (mod + 1) * V, :], pairs_ref[index, mod], preferred_element_type=F32
            )
            cross = jnp.dot(mask_ref[mod], stacked, preferred_element_type=F32)
            for rest in range(SUB):
                value = rest * MODS + mod
                block = cross[rest * V : (rest + 1) * V, :]
                first_grad += block * row_ref[pl.ds(value, 1), :]
                product = block * first
                partial = product[0:8]
                for part in range(1, V // 8):
                    partial += product[8 * part : 8 * part + 8]
                for half in range(2):
                    sum_ref[half, value * 8 : value * 8 + 8, :] = partial[:, half * LANES : (half + 1) * LANES]
        for half in range(2):
            lanes = slice(half * LANES, (half + 1) * LANES)
            second_grad = jnp.zeros((V, LANES), F32)
            for part in range(8):
                second_grad += sum_ref[half, pl.ds(part, V, stride=8), :]
            grads = (first_grad[:, lanes], second_grad, third_grad[:, lanes])
            parts = [
                jnp.concatenate([grad[part * SUB : (part + 1) * SUB, :] for grad in grads], axis=0)
                for part in range(CHUNKS)
            ]
            for chunk, packed in enumerate(exchange(parts)):
                place = (2 * index + half) * CHUNKS + chunk
                out_ref[place] = packed.reshape(3, SUB, LANES).astype(LOW)
        return carry

    lax.fori_loop(0, steps, step, 0, unroll=steps)


def collect_kernel(triples_ref, grads_ref, send_ref, *total_refs):
    groups, attrs = send_ref.shape[0], send_ref.shape[1]
    places = grads_ref.shape[0] // CHUNKS
    for total_ref in total_refs:
        total_ref[...] = jnp.zeros(total_ref.shape, F32)
    for place in range(places):
        for chunk in range(CHUNKS):
            for which, total_ref in enumerate(total_refs):
                attr = triples_ref[which, chunk * places + place]
                total_ref[attr] = total_ref[attr] + grads_ref[place * CHUNKS + chunk, which].astype(F32)
    total = total_refs[0][...] + total_refs[1][...] + total_refs[2][...]
    send_ref[...] = total.reshape(groups, attrs, SUB, LANES).astype(LOW)


def adam_kernel(
    parts_ref, probs_ref, logits_ref, first_ref, second_ref, out_logits_ref, out_first_ref, out_second_ref, grad_ref
):
    groups, attrs = parts_ref.shape[0], parts_ref.shape[1]
    halves = groups // CHUNKS
    chunks = []
    for chunk in range(CHUNKS):
        total = parts_ref[chunk * halves].astype(F32)
        for half in range(1, halves):
            total += parts_ref[chunk * halves + half].astype(F32)
        chunks.append(total.reshape(attrs * SUB, LANES))
    parts = exchange(chunks)
    for attr in range(attrs):
        row_grad = jnp.concatenate([part[attr * SUB : (attr + 1) * SUB, :] for part in parts], axis=0)
        probs = probs_ref[attr]
        inner = jnp.sum(probs * row_grad, axis=0, keepdims=True)
        grad_ref[attr * V : (attr + 1) * V, :] = 512.0 * probs * (row_grad - inner)
    grad = grad_ref[...].T
    new_first = 0.9 * first_ref[...] + 0.1 * grad
    new_second = 0.999 * second_ref[...] + 0.001 * grad * grad
    first_hat = new_first / (1.0 - 0.9**ADAM_STEP)
    second_hat = new_second / (1.0 - 0.999**ADAM_STEP)
    out_logits_ref[...] = logits_ref[...] - 0.5 * first_hat / (jnp.sqrt(second_hat) + 1e-08)
    out_first_ref[...] = new_first
    out_second_ref[...] = new_second


def swap(value, axes):
    return lax.all_to_all(value, axes, 0, 0, tiled=True)


def answers(src):
    shape = jax.ShapeDtypeStruct
    shards = src.shape[0] // CHUNKS
    tall, wide = V * V // MODS, V * MODS
    return call(
        answer_kernel,
        (
            shape((wide, tall), F32),
            shape((wide, tall), LOW),
            shape((shards, 3, V, LANES), LOW),
            shape((shards // 2, MODS, tall, 2 * LANES), LOW),
        ),
        (src,),
        [VMEM],
    )


def backward(scale, table, pairs, base, other):
    shards = table.shape[0]
    tall, wide = V * V // MODS, V * MODS
    return call(
        lambda *refs: backward_kernel(scale, *refs),
        jax.ShapeDtypeStruct((shards * CHUNKS, 3, SUB, LANES), LOW),
        (table, pairs, base, other),
        [VMEM] * 4,
        [
            pltpu.VMEM((wide, tall), LOW),
            pltpu.VMEM((MODS, tall, wide), LOW),
            pltpu.VMEM((V, 2 * LANES), F32),
            pltpu.VMEM((2, 8 * V, LANES), F32),
        ],
    )


def shards(logits, first_moment, second_moment, targets, triples):
    rows, cols = logits.shape
    margs, cells = targets.shape
    attrs = cols // V
    groups = lax.axis_size(MARG_AXES)
    scale = cells / (rows * lax.axis_size(ROW_AXES))
    shape = jax.ShapeDtypeStruct
    tall, wide = V * V // MODS, V * MODS
    place = lax.axis_index(PLACE_AXES).astype(jnp.int32).reshape(1)
    side = lax.axis_index("h").astype(jnp.int32).reshape(1)
    probs, copies = call(
        relax_kernel,
        (shape((attrs, V, rows), F32), shape((groups, attrs + 1, SUB, LANES), LOW)),
        (side, place, stay(triples.T), stay(logits)),
        [SMEM, SMEM, ANY, ANY],
        [
            pltpu.VMEM((SUB, LANES), F32),
            pltpu.VMEM((3, margs), jnp.int32),
            pltpu.VMEM((rows, cols), F32),
            pltpu.SemaphoreType.DMA((2,)),
        ],
    )
    full = swap(copies, MARG_AXES)
    picked, attributes = call(
        select_kernel,
        (shape((margs * CHUNKS, 3, SUB, LANES), LOW), shape((SUB, LANES), jnp.int32)),
        (full.reshape(groups * (attrs + 1), SUB, LANES),),
        [VMEM],
        [pltpu.VMEM((SUB, LANES), jnp.int32), pltpu.SMEM((SUB, LANES), jnp.int32), pltpu.SemaphoreType.DMA],
    )
    own, send, table, pairs = answers(swap(picked, SHARE_AXES))
    other = lax.ppermute(send, "u", [(0, 1), (1, 0)])
    base = call(
        lambda *refs: base_kernel(scale, *refs),
        shape((wide, tall), F32),
        (place, own, stay(targets)),
        [SMEM, VMEM, ANY],
        [pltpu.VMEM((8, cells), F32), pltpu.VMEM((tall, wide), F32), pltpu.SemaphoreType.DMA],
    )
    returned = swap(backward(scale, table, pairs, base, other), SHARE_AXES)
    totals = call(
        collect_kernel,
        shape((groups, attrs, SUB, LANES), LOW),
        (attributes, returned),
        [SMEM, VMEM],
        [pltpu.VMEM((groups * attrs, SUB, LANES), F32)] * 3,
    )
    return call(
        adam_kernel,
        (shape((rows, cols), F32),) * 3,
        (swap(totals, MARG_AXES), probs, logits, first_moment, second_moment),
        [VMEM] * 5,
        [pltpu.VMEM((cols, rows), F32)],
    )


def solution(mesh):
    fine = Mesh(mesh.devices.reshape(PARTS), NAMES)
    table = P(ROW_AXES, MARG_AXES)
    listed = P(MARG_AXES, None)
    return jax.shard_map(
        shards,
        mesh=fine,
        in_specs=(table, table, table, listed, listed),
        out_specs=(table, table, table),
        check_vma=False,
    )
```

```python
import jax
import jax.numpy as jnp
from jax import lax
from jax.experimental import pallas as pl
from jax.experimental.pallas import tpu as pltpu
from jax.sharding import Mesh, PartitionSpec as P

V = 32
ADAM_STEP = 4
PARTS = (4, 2, 2, 2, 2, 2, 2)
NAMES = ("x", "u", "w", "c", "v", "y", "h")
ROW_AXES = ("x", "u", "w", "c")
MARG_AXES = ("v", "y", "h")
SIDE_AXES = ("v", "h")
PLACE_AXES = ("x", "w", "c")
SHARE_AXES = ("x", "w", "c", "y")
CHUNKS = 2
CHUNK = 64
LANES = CHUNKS * CHUNK
SUB = V // CHUNKS
TILE = 8
MODS = 4
REST = V // MODS
VMEM = pl.BlockSpec(memory_space=pltpu.VMEM)
SMEM = pl.BlockSpec(memory_space=pltpu.SMEM)
ANY = pl.BlockSpec(memory_space=pl.ANY)
LIMIT = 20 * 1024 * 1024
F32 = jnp.float32
LOW = jnp.bfloat16


def call(body, out_shape, operands, specs, scratch=()):
    return pl.pallas_call(
        body,
        out_shape=out_shape,
        in_specs=specs,
        out_specs=jax.tree.map(lambda unused: VMEM, out_shape),
        scratch_shapes=scratch,
        compiler_params=pltpu.CompilerParams(vmem_limit_bytes=LIMIT),
    )(*operands)


def exchange(blocks):
    left, right = blocks
    first = lax.broadcasted_iota(jnp.int32, left.shape, 1) < CHUNK
    return [
        jnp.where(first, left, pltpu.roll(right, CHUNK, 1)),
        jnp.where(first, pltpu.roll(left, CHUNK, 1), right),
    ]


def members(chunk, groups):
    return [index for index in range(groups) if (index // 2) % CHUNKS == chunk]


def stay(value):
    return pltpu.with_memory_space_constraint(value, pltpu.HBM)


def relax_kernel(
    side_ref, place_ref, triples_hbm, logits_hbm, probs_ref, send_ref, tile_ref, triples_ref, logits_ref, sems
):
    logits_copy = pltpu.make_async_copy(logits_hbm, logits_ref, sems.at[0])
    triples_copy = pltpu.make_async_copy(triples_hbm, triples_ref, sems.at[1])
    logits_copy.start()
    triples_copy.start()
    logits_copy.wait()
    flipped = logits_ref[...].T
    attrs = probs_ref.shape[0]
    groups = send_ref.shape[0]
    for attr in range(attrs):
        block = flipped[attr * V : (attr + 1) * V, :]
        top = jnp.max(block, axis=0, keepdims=True)
        expo = jnp.exp(block - top)
        probs = expo / jnp.sum(expo, axis=0, keepdims=True)
        probs_ref[attr] = probs
        for chunk, packed in enumerate(exchange([probs[part * SUB : (part + 1) * SUB, :] for part in range(CHUNKS)])):
            low = packed.astype(LOW)
            for index in members(chunk, groups):
                send_ref[index, attr] = low
    triples_copy.wait()
    tile_ref[...] = jnp.zeros(tile_ref.shape, F32)
    tile_ref[0:3, 0 : triples_ref.shape[1]] = triples_ref[...].astype(F32)
    for side in range(groups // CHUNKS):
        tile = (tile_ref[...] * jnp.where(side_ref[0] == side, 1.0, 0.0)).astype(LOW)
        for chunk in range(CHUNKS):
            send_ref[members(chunk, groups)[side], attrs] = tile


def select_kernel(full_ref, send_ref, triples_ref, index_ref, scalar_ref, sem):
    slots = full_ref.shape[1]
    places = send_ref.shape[0] // CHUNKS
    triples = jnp.zeros(triples_ref.shape, F32)
    for chunk in range(CHUNKS):
        tile = jnp.zeros((SUB, LANES), F32)
        for index in members(chunk, full_ref.shape[0]):
            tile += full_ref[index, slots - 1].astype(F32)
        triples += pltpu.roll(tile[0:TILE, :], chunk * places, 1) if chunk else tile[0:TILE, :]
    attrs = triples.astype(jnp.int32)
    triples_ref[...] = attrs
    index_ref[...] = attrs + attrs // (slots - 1)
    copy = pltpu.make_async_copy(index_ref, scalar_ref, sem)
    copy.start()
    copy.wait()
    flat_ref = full_ref.reshape(full_ref.shape[0] * slots, SUB, LANES)
    for place in range(places):
        for chunk in range(CHUNKS):
            for which in range(3):
                send_ref[place * CHUNKS + chunk, which] = flat_ref[scalar_ref[which, chunk * places + place]]


def unpack(src_ref, shard):
    packed = [src_ref[shard * CHUNKS + chunk].astype(F32).reshape(3 * SUB, LANES) for chunk in range(CHUNKS)]
    parts = exchange(packed)
    return [
        jnp.concatenate([part[which * SUB : (which + 1) * SUB, :] for part in parts], axis=0) for which in range(3)
    ]


def answer_kernel(src_ref, own_ref, send_ref, table_ref, pairs_ref):
    shards = table_ref.shape[0]

    def fill(step):
        for part in range(2):
            shard = 2 * step + part
            first, second, third = [value.astype(LOW) for value in unpack(src_ref, shard)]
            table_ref[shard, 0] = first
            table_ref[shard, 1] = second
            table_ref[shard, 2] = third
            for value in range(V):
                row = jnp.broadcast_to(second[value : value + 1, :], first.shape)
                mod, rest = value % MODS, value // MODS
                pairs_ref[step, mod, rest * V : (rest + 1) * V, part * LANES : (part + 1) * LANES] = first * row

    def add(step):
        third = jnp.concatenate([table_ref[2 * step, 2], table_ref[2 * step + 1, 2]], axis=1)
        for mod in range(MODS):
            own_ref[mod * V : (mod + 1) * V, :] += lax.dot_general(
                third, pairs_ref[step, mod], (((1,), (1,)), ((), ())), preferred_element_type=F32
            )

    own_ref[...] = jnp.zeros(own_ref.shape, F32)
    fill(0)

    def both(step, carry):
        add(step - 1)
        fill(step)
        return carry

    lax.fori_loop(1, shards // 2, both, 0, unroll=shards // 2 - 1)
    add(shards // 2 - 1)
    send_ref[...] = own_ref[...].astype(LOW)


def base_kernel(scale, place_ref, own_ref, targets_any, base_ref, block_ref, target_ref, sem):
    place = place_ref[0]
    start = pl.multiple_of(place // TILE * TILE, TILE)
    copy = pltpu.make_async_copy(targets_any.at[pl.ds(start, TILE), :], block_ref, sem)
    copy.start()
    copy.wait()
    mine = lax.broadcasted_iota(jnp.int32, (TILE, LANES), 0) == lax.rem(place, TILE)
    for rest in range(REST):
        for value in range(V):
            tile = block_ref[:, pl.ds((value * REST + rest) * LANES, LANES)]
            row = jnp.sum(jnp.where(mine, tile, 0.0), axis=0, keepdims=True)
            target_ref[pl.ds(rest * V + value, 1), :] = row
    base_ref[...] = scale * own_ref[...] - target_ref[...].T


def backward_kernel(scale, table_ref, pairs_ref, base_ref, other_ref, out_ref, low_ref, mask_ref, row_ref, sum_ref):
    steps = pairs_ref.shape[0]
    wide = 2 * LANES
    resid = base_ref[...] + scale * other_ref[...].astype(F32)
    low_ref[...] = resid.astype(LOW)
    flipped = resid.T
    lane_mod = lax.broadcasted_iota(jnp.int32, flipped.shape, 1) // V
    for mod in range(MODS):
        mask_ref[mod] = jnp.where(lane_mod == mod, flipped, 0.0).astype(LOW)

    def step(index, carry):
        pair = [
            jnp.concatenate([table_ref[2 * index, which], table_ref[2 * index + 1, which]], axis=1)
            for which in range(3)
        ]
        first = pair[0].astype(F32)
        row_ref[...] = pair[1].astype(F32)
        stacked = jnp.concatenate([pair[2]] * MODS, axis=0)
        third_grad = jnp.zeros((V, wide), F32)
        first_grad = jnp.zeros((V, wide), F32)
        for mod in range(MODS):
            third_grad += jnp.dot(
                low_ref[mod * V : (mod + 1) * V, :], pairs_ref[index, mod], preferred_element_type=F32
            )
            cross = jnp.dot(mask_ref[mod], stacked, preferred_element_type=F32)
            for rest in range(REST):
                value = rest * MODS + mod
                block = cross[rest * V : (rest + 1) * V, :]
                first_grad += block * row_ref[pl.ds(value, 1), :]
                product = block * first
                partial = product[0:8]
                for part in range(1, V // 8):
                    partial += product[8 * part : 8 * part + 8]
                for half in range(2):
                    sum_ref[half, value * 8 : value * 8 + 8, :] = partial[:, half * LANES : (half + 1) * LANES]
        for half in range(2):
            lanes = slice(half * LANES, (half + 1) * LANES)
            second_grad = jnp.zeros((V, LANES), F32)
            for part in range(8):
                second_grad += sum_ref[half, pl.ds(part, V, stride=8), :]
            grads = (first_grad[:, lanes], second_grad, third_grad[:, lanes])
            parts = [
                jnp.concatenate([grad[part * SUB : (part + 1) * SUB, :] for grad in grads], axis=0)
                for part in range(CHUNKS)
            ]
            for chunk, packed in enumerate(exchange(parts)):
                place = (2 * index + half) * CHUNKS + chunk
                out_ref[place] = packed.reshape(3, SUB, LANES).astype(LOW)
        return carry

    lax.fori_loop(0, steps, step, 0, unroll=steps)


def collect_kernel(triples_ref, grads_ref, send_ref, *total_refs):
    groups, attrs = send_ref.shape[0], send_ref.shape[1]
    places = grads_ref.shape[0] // CHUNKS
    for total_ref in total_refs:
        total_ref[...] = jnp.zeros(total_ref.shape, F32)
    for place in range(places):
        for chunk in range(CHUNKS):
            for which, total_ref in enumerate(total_refs):
                attr = triples_ref[which, chunk * places + place]
                total_ref[attr] = total_ref[attr] + grads_ref[place * CHUNKS + chunk, which].astype(F32)
    total = total_refs[0][...] + total_refs[1][...] + total_refs[2][...]
    send_ref[...] = total.reshape(groups, attrs, SUB, LANES).astype(LOW)


def adam_kernel(
    parts_ref, probs_ref, logits_ref, first_ref, second_ref, out_logits_ref, out_first_ref, out_second_ref, grad_ref
):
    groups, attrs = parts_ref.shape[0], parts_ref.shape[1]
    chunks = []
    for chunk in range(CHUNKS):
        total = jnp.zeros((attrs, SUB, LANES), F32)
        for index in members(chunk, groups):
            total += parts_ref[index].astype(F32)
        chunks.append(total.reshape(attrs * SUB, LANES))
    parts = exchange(chunks)
    for attr in range(attrs):
        row_grad = jnp.concatenate([part[attr * SUB : (attr + 1) * SUB, :] for part in parts], axis=0)
        probs = probs_ref[attr]
        inner = jnp.sum(probs * row_grad, axis=0, keepdims=True)
        grad_ref[attr * V : (attr + 1) * V, :] = 512.0 * probs * (row_grad - inner)
    grad = grad_ref[...].T
    new_first = 0.9 * first_ref[...] + 0.1 * grad
    new_second = 0.999 * second_ref[...] + 0.001 * grad * grad
    first_hat = new_first / (1.0 - 0.9**ADAM_STEP)
    second_hat = new_second / (1.0 - 0.999**ADAM_STEP)
    out_logits_ref[...] = logits_ref[...] - 0.5 * first_hat / (jnp.sqrt(second_hat) + 1e-08)
    out_first_ref[...] = new_first
    out_second_ref[...] = new_second


def swap(value, axes):
    return lax.all_to_all(value, axes, 0, 0, tiled=True)


def answers(src):
    shape = jax.ShapeDtypeStruct
    shards = src.shape[0] // CHUNKS
    tall, wide = V * V // MODS, V * MODS
    return call(
        answer_kernel,
        (
            shape((wide, tall), F32),
            shape((wide, tall), LOW),
            shape((shards, 3, V, LANES), LOW),
            shape((shards // 2, MODS, tall, 2 * LANES), LOW),
        ),
        (src,),
        [VMEM],
    )


def backward(scale, table, pairs, base, other):
    shards = table.shape[0]
    tall, wide = V * V // MODS, V * MODS
    return call(
        lambda *refs: backward_kernel(scale, *refs),
        jax.ShapeDtypeStruct((shards * CHUNKS, 3, SUB, LANES), LOW),
        (table, pairs, base, other),
        [VMEM] * 4,
        [
            pltpu.VMEM((wide, tall), LOW),
            pltpu.VMEM((MODS, tall, wide), LOW),
            pltpu.VMEM((V, 2 * LANES), F32),
            pltpu.VMEM((2, 8 * V, LANES), F32),
        ],
    )


def shards(logits, first_moment, second_moment, targets, triples):
    rows, cols = logits.shape
    margs, cells = targets.shape
    attrs = cols // V
    groups = lax.axis_size(MARG_AXES)
    scale = cells / (rows * lax.axis_size(ROW_AXES))
    shape = jax.ShapeDtypeStruct
    tall, wide = V * V // MODS, V * MODS
    place = lax.axis_index(PLACE_AXES).astype(jnp.int32).reshape(1)
    side = lax.axis_index(SIDE_AXES).astype(jnp.int32).reshape(1)
    probs, copies = call(
        relax_kernel,
        (shape((attrs, V, rows), F32), shape((groups, attrs + 1, SUB, LANES), LOW)),
        (side, place, stay(triples.T), stay(logits)),
        [SMEM, SMEM, ANY, ANY],
        [
            pltpu.VMEM((SUB, LANES), F32),
            pltpu.VMEM((3, margs), jnp.int32),
            pltpu.VMEM((rows, cols), F32),
            pltpu.SemaphoreType.DMA((2,)),
        ],
    )
    full = swap(copies, MARG_AXES)
    picked, attributes = call(
        select_kernel,
        (shape((margs * CHUNKS, 3, SUB, LANES), LOW), shape((TILE, LANES), jnp.int32)),
        (full,),
        [VMEM],
        [pltpu.VMEM((TILE, LANES), jnp.int32), pltpu.SMEM((TILE, LANES), jnp.int32), pltpu.SemaphoreType.DMA],
    )
    own, send, table, pairs = answers(swap(picked, SHARE_AXES))
    other = lax.ppermute(send, "u", [(0, 1), (1, 0)])
    base = call(
        lambda *refs: base_kernel(scale, *refs),
        shape((wide, tall), F32),
        (place, own, stay(targets)),
        [SMEM, VMEM, ANY],
        [pltpu.VMEM((TILE, cells), F32), pltpu.VMEM((tall, wide), F32), pltpu.SemaphoreType.DMA],
    )
    returned = swap(backward(scale, table, pairs, base, other), SHARE_AXES)
    totals = call(
        collect_kernel,
        shape((groups, attrs, SUB, LANES), LOW),
        (attributes, returned),
        [SMEM, VMEM],
        [pltpu.VMEM((groups * attrs, SUB, LANES), F32)] * 3,
    )
    return call(
        adam_kernel,
        (shape((rows, cols), F32),) * 3,
        (swap(totals, MARG_AXES), probs, logits, first_moment, second_moment),
        [VMEM] * 5,
        [pltpu.VMEM((cols, rows), F32)],
    )


def solution(mesh):
    fine = Mesh(mesh.devices.reshape(PARTS), NAMES)
    table = P(ROW_AXES, MARG_AXES)
    listed = P(MARG_AXES, None)
    return jax.shard_map(
        shards,
        mesh=fine,
        in_specs=(table, table, table, listed, listed),
        out_specs=(table, table, table),
        check_vma=False,
    )
```

```python
import jax
import jax.numpy as jnp
from jax import lax
from jax.experimental import pallas as pl
from jax.experimental.pallas import tpu as pltpu
from jax.sharding import Mesh, PartitionSpec as P

V = 32
ADAM_STEP = 4
PARTS = (4, 2, 2, 2, 4, 2)
NAMES = ("x", "u", "w", "c", "y", "h")
ROW_AXES = ("x", "u", "w", "c")
MARG_AXES = ("y", "h")
PLACE_AXES = ("x", "w", "c")
SHARE_AXES = ("x", "w", "c", "y")
CHUNKS = 4
CHUNK = 32
LANES = CHUNKS * CHUNK
SUB = V // CHUNKS
MODS = 4
MARGS = 16
VMEM = pl.BlockSpec(memory_space=pltpu.VMEM)
SMEM = pl.BlockSpec(memory_space=pltpu.SMEM)
ANY = pl.BlockSpec(memory_space=pl.ANY)
LIMIT = 20 * 1024 * 1024
F32 = jnp.float32
LOW = jnp.bfloat16


def call(body, out_shape, operands, specs, scratch=()):
    return pl.pallas_call(
        body,
        out_shape=out_shape,
        in_specs=specs,
        out_specs=jax.tree.map(lambda unused: VMEM, out_shape),
        scratch_shapes=scratch,
        compiler_params=pltpu.CompilerParams(vmem_limit_bytes=LIMIT),
    )(*operands)


def exchange(blocks):
    lane = lax.broadcasted_iota(jnp.int32, blocks[0].shape, 1)
    blocks = list(blocks)
    for width, pairs in ((2 * CHUNK, ((0, 2), (1, 3))), (CHUNK, ((0, 1), (2, 3)))):
        low_part = (lane // width) % 2 == 0
        for a, b in pairs:
            left, right = blocks[a], blocks[b]
            blocks[a] = jnp.where(low_part, left, pltpu.roll(right, width, 1))
            blocks[b] = jnp.where(low_part, pltpu.roll(left, LANES - width, 1), right)
    return blocks


def stay(value):
    return pltpu.with_memory_space_constraint(value, pltpu.HBM)


def relax_kernel(
    side_ref,
    place_ref,
    triples_hbm,
    logits_hbm,
    probs_ref,
    send_ref,
    tile_ref,
    triples_ref,
    logits_ref,
    flipped_ref,
    sems,
):
    logits_copy = pltpu.make_async_copy(logits_hbm, logits_ref, sems.at[0])
    triples_copy = pltpu.make_async_copy(triples_hbm, triples_ref, sems.at[1])
    logits_copy.start()
    triples_copy.start()
    logits_copy.wait()
    flipped_ref[...] = logits_ref[...].T
    attrs = probs_ref.shape[1]
    halves = send_ref.shape[0] // CHUNKS
    values = [flipped_ref[pl.ds(value, attrs, stride=V), :] for value in range(V)]
    top = values[0]
    for value in values[1:]:
        top = jnp.maximum(top, value)
    expos = [jnp.exp(value - top) for value in values]
    total = expos[0]
    for expo in expos[1:]:
        total = total + expo
    probs = [expo / total for expo in expos]
    for value in range(V):
        probs_ref[value] = probs[value]
    for rest in range(SUB):
        for chunk, packed in enumerate(exchange([probs[part * SUB + rest] for part in range(CHUNKS)])):
            low = packed.astype(LOW)
            for half in range(halves):
                send_ref[chunk * halves + half, :, rest * LANES : (rest + 1) * LANES] = low
    triples_copy.wait()
    tile_ref[...] = jnp.zeros(tile_ref.shape, F32)
    tile_ref[0:3, 0 : triples_ref.shape[1]] = triples_ref[...].astype(F32)
    for half in range(halves):
        tile = (tile_ref[...] * jnp.where(side_ref[0] == half, 1.0, 0.0)).astype(LOW)
        for chunk in range(CHUNKS):
            send_ref[chunk * halves + half, :, SUB * LANES :] = tile


def one_hot(triples, which, count):
    width = CHUNKS * MARGS
    row = jnp.broadcast_to(triples[which : which + 1, 0:width], (count, width))
    attr = lax.broadcasted_iota(jnp.int32, (count, width), 0).astype(F32)
    return jnp.where(row == attr, 1.0, 0.0).astype(LOW)


def tile_rows(which, rest):
    step = 3 * SUB
    for chunk in range(CHUNKS):
        for start in range(0, MARGS, SUB):
            rows = pl.ds((start * CHUNKS + chunk) * step + which * SUB + rest, SUB, stride=CHUNKS * step)
            yield rows, chunk * MARGS + start


def select_kernel(full_ref, send_ref, triples_ref, picked_ref):
    groups, attrs = full_ref.shape[0], full_ref.shape[1]
    halves = groups // CHUNKS
    full = [full_ref[index].astype(F32) for index in range(groups)]
    triples = jnp.zeros(triples_ref.shape, F32)
    for chunk in range(CHUNKS):
        tile = full[chunk * halves][:, SUB * LANES :]
        for half in range(1, halves):
            tile += full[chunk * halves + half][:, SUB * LANES :]
        triples += pltpu.roll(tile, chunk * MARGS, 1) if chunk else tile
    triples_ref[...] = triples
    table = jnp.concatenate([value[:, 0 : SUB * LANES] for value in full], axis=0).astype(LOW)
    for which in range(3):
        mine = one_hot(triples, which, groups * attrs)
        picked = lax.dot_general(mine, table, (((0,), (0,)), ((), ())), preferred_element_type=F32)
        for rest in range(SUB):
            for rows, place in tile_rows(which, rest):
                picked_ref[rows, :] = picked[place : place + SUB, rest * LANES : (rest + 1) * LANES]
    send_ref[...] = picked_ref[...].reshape(send_ref.shape).astype(LOW)


def unpack(src_ref, shard):
    packed = [src_ref[shard * CHUNKS + chunk].astype(F32).reshape(3 * SUB, LANES) for chunk in range(CHUNKS)]
    parts = exchange(packed)
    return [
        jnp.concatenate([part[which * SUB : (which + 1) * SUB, :] for part in parts], axis=0) for which in range(3)
    ]


def answer_kernel(src_ref, own_ref, send_ref, table_ref, pairs_ref):
    shards = table_ref.shape[0]

    def fill(step):
        for part in range(2):
            shard = 2 * step + part
            first, second, third = [value.astype(LOW) for value in unpack(src_ref, shard)]
            table_ref[shard, 0] = first
            table_ref[shard, 1] = second
            table_ref[shard, 2] = third
            for value in range(V):
                row = jnp.broadcast_to(second[value : value + 1, :], first.shape)
                mod, rest = value % MODS, value // MODS
                pairs_ref[step, mod, rest * V : (rest + 1) * V, part * LANES : (part + 1) * LANES] = first * row

    def add(step):
        third = jnp.concatenate([table_ref[2 * step, 2], table_ref[2 * step + 1, 2]], axis=1)
        for mod in range(MODS):
            own_ref[mod * V : (mod + 1) * V, :] += lax.dot_general(
                third, pairs_ref[step, mod], (((1,), (1,)), ((), ())), preferred_element_type=F32
            )

    own_ref[...] = jnp.zeros(own_ref.shape, F32)
    fill(0)

    def both(step, carry):
        add(step - 1)
        fill(step)
        return carry

    lax.fori_loop(1, shards // 2, both, 0, unroll=shards // 2 - 1)
    add(shards // 2 - 1)
    send_ref[...] = own_ref[...].astype(LOW)


def base_kernel(scale, place_ref, own_ref, targets_any, base_ref, block_ref, target_ref, sem):
    place = place_ref[0]
    start = pl.multiple_of(place // 8 * 8, 8)
    copy = pltpu.make_async_copy(targets_any.at[pl.ds(start, 8), :], block_ref, sem)
    copy.start()
    copy.wait()
    mine = lax.broadcasted_iota(jnp.int32, (8, LANES), 0) == lax.rem(place, 8)
    for rest in range(SUB):
        for value in range(V):
            tile = block_ref[:, pl.ds((value * SUB + rest) * LANES, LANES)]
            row = jnp.sum(jnp.where(mine, tile, 0.0), axis=0, keepdims=True)
            target_ref[pl.ds(rest * V + value, 1), :] = row
    base_ref[...] = scale * own_ref[...] - target_ref[...].T


def backward_kernel(scale, table_ref, pairs_ref, base_ref, other_ref, out_ref, low_ref, mask_ref, row_ref, sum_ref):
    steps = pairs_ref.shape[0]
    wide = 2 * LANES
    resid = base_ref[...] + scale * other_ref[...].astype(F32)
    low_ref[...] = resid.astype(LOW)
    flipped = resid.T
    lane_mod = lax.broadcasted_iota(jnp.int32, flipped.shape, 1) // V
    for mod in range(MODS):
        mask_ref[mod] = jnp.where(lane_mod == mod, flipped, 0.0).astype(LOW)

    def step(index, carry):
        pair = [
            jnp.concatenate([table_ref[2 * index, which], table_ref[2 * index + 1, which]], axis=1)
            for which in range(3)
        ]
        first = pair[0].astype(F32)
        row_ref[...] = pair[1].astype(F32)
        stacked = jnp.concatenate([pair[2]] * MODS, axis=0)
        third_grad = jnp.zeros((V, wide), F32)
        first_grad = jnp.zeros((V, wide), F32)
        for mod in range(MODS):
            third_grad += jnp.dot(
                low_ref[mod * V : (mod + 1) * V, :], pairs_ref[index, mod], preferred_element_type=F32
            )
            cross = jnp.dot(mask_ref[mod], stacked, preferred_element_type=F32)
            for rest in range(SUB):
                value = rest * MODS + mod
                block = cross[rest * V : (rest + 1) * V, :]
                first_grad += block * row_ref[pl.ds(value, 1), :]
                product = block * first
                partial = product[0:8]
                for part in range(1, V // 8):
                    partial += product[8 * part : 8 * part + 8]
                for half in range(2):
                    sum_ref[half, value * 8 : value * 8 + 8, :] = partial[:, half * LANES : (half + 1) * LANES]
        for half in range(2):
            lanes = slice(half * LANES, (half + 1) * LANES)
            second_grad = jnp.zeros((V, LANES), F32)
            for part in range(8):
                second_grad += sum_ref[half, pl.ds(part, V, stride=8), :]
            grads = (first_grad[:, lanes], second_grad, third_grad[:, lanes])
            parts = [
                jnp.concatenate([grad[part * SUB : (part + 1) * SUB, :] for grad in grads], axis=0)
                for part in range(CHUNKS)
            ]
            for chunk, packed in enumerate(exchange(parts)):
                place = (2 * index + half) * CHUNKS + chunk
                out_ref[place] = packed.reshape(3, SUB, LANES).astype(LOW)
        return carry

    lax.fori_loop(0, steps, step, 0, unroll=steps)


def collect_kernel(triples_ref, grads_ref, send_ref, grad_ref):
    groups, attrs = send_ref.shape[0], send_ref.shape[1]
    triples = triples_ref[...]
    grad_ref[...] = grads_ref[...].astype(F32).reshape(grad_ref.shape)
    total = jnp.zeros((groups * attrs, SUB * LANES), F32)
    for which in range(3):
        parts = []
        for rest in range(SUB):
            tiles = [grad_ref[rows, :] for rows, unused in tile_rows(which, rest)]
            parts.append(jnp.concatenate(tiles, axis=0))
        grads = jnp.concatenate(parts, axis=1).astype(LOW)
        total += jnp.dot(one_hot(triples, which, groups * attrs), grads, preferred_element_type=F32)
    for index in range(groups):
        send_ref[index] = total[index * attrs : (index + 1) * attrs, :].astype(LOW)


def adam_kernel(
    parts_ref, probs_ref, logits_ref, first_ref, second_ref, out_logits_ref, out_first_ref, out_second_ref, grad_ref
):
    groups, attrs = parts_ref.shape[0], parts_ref.shape[1]
    halves = groups // CHUNKS
    chunks = []
    for chunk in range(CHUNKS):
        total = parts_ref[chunk * halves].astype(F32)
        for half in range(1, halves):
            total += parts_ref[chunk * halves + half].astype(F32)
        chunks.append(total)
    row_grad = [None] * V
    for rest in range(SUB):
        blocks = [chunk[:, rest * LANES : (rest + 1) * LANES] for chunk in chunks]
        for part, block in enumerate(exchange(blocks)):
            row_grad[part * SUB + rest] = block
    inner = jnp.zeros((attrs, LANES), F32)
    for value in range(V):
        inner += probs_ref[value] * row_grad[value]
    for value in range(V):
        grad_ref[pl.ds(value, attrs, stride=V), :] = 512.0 * probs_ref[value] * (row_grad[value] - inner)
    grad = grad_ref[...].T
    new_first = 0.9 * first_ref[...] + 0.1 * grad
    new_second = 0.999 * second_ref[...] + 0.001 * grad * grad
    first_hat = new_first / (1.0 - 0.9**ADAM_STEP)
    second_hat = new_second / (1.0 - 0.999**ADAM_STEP)
    out_logits_ref[...] = logits_ref[...] - 0.5 * first_hat / (jnp.sqrt(second_hat) + 1e-08)
    out_first_ref[...] = new_first
    out_second_ref[...] = new_second


def swap(value, axes):
    return lax.all_to_all(value, axes, 0, 0, tiled=True)


def answers(src):
    shape = jax.ShapeDtypeStruct
    shards = src.shape[0] // CHUNKS
    tall, wide = V * V // MODS, V * MODS
    return call(
        answer_kernel,
        (
            shape((wide, tall), F32),
            shape((wide, tall), LOW),
            shape((shards, 3, V, LANES), LOW),
            shape((shards // 2, MODS, tall, 2 * LANES), LOW),
        ),
        (src,),
        [VMEM],
    )


def backward(scale, table, pairs, base, other):
    shards = table.shape[0]
    tall, wide = V * V // MODS, V * MODS
    return call(
        lambda *refs: backward_kernel(scale, *refs),
        jax.ShapeDtypeStruct((shards * CHUNKS, 3, SUB, LANES), LOW),
        (table, pairs, base, other),
        [VMEM] * 4,
        [
            pltpu.VMEM((wide, tall), LOW),
            pltpu.VMEM((MODS, tall, wide), LOW),
            pltpu.VMEM((V, 2 * LANES), F32),
            pltpu.VMEM((2, 8 * V, LANES), F32),
        ],
    )


def shards(logits, first_moment, second_moment, targets, triples):
    rows, cols = logits.shape
    margs, cells = targets.shape
    attrs = cols // V
    groups = lax.axis_size(MARG_AXES)
    scale = cells / (rows * lax.axis_size(ROW_AXES))
    shape = jax.ShapeDtypeStruct
    tall, wide = V * V // MODS, V * MODS
    place = lax.axis_index(PLACE_AXES).astype(jnp.int32).reshape(1)
    side = lax.axis_index("h").astype(jnp.int32).reshape(1)
    probs, copies = call(
        relax_kernel,
        (shape((V, attrs, rows), F32), shape((groups, attrs, (SUB + 1) * LANES), LOW)),
        (side, place, stay(triples.T), stay(logits)),
        [SMEM, SMEM, ANY, ANY],
        [
            pltpu.VMEM((SUB, LANES), F32),
            pltpu.VMEM((3, margs), jnp.int32),
            pltpu.VMEM((rows, cols), F32),
            pltpu.VMEM((cols, rows), F32),
            pltpu.SemaphoreType.DMA((2,)),
        ],
    )
    full = swap(copies, MARG_AXES)
    picked, attributes = call(
        select_kernel,
        (shape((margs * CHUNKS, 3, SUB, LANES), LOW), shape((SUB, LANES), F32)),
        (full,),
        [VMEM],
        [pltpu.VMEM((margs * CHUNKS * 3 * SUB, LANES), F32)],
    )
    own, send, table, pairs = answers(swap(picked, SHARE_AXES))
    other = lax.ppermute(send, "u", [(0, 1), (1, 0)])
    base = call(
        lambda *refs: base_kernel(scale, *refs),
        shape((wide, tall), F32),
        (place, own, stay(targets)),
        [SMEM, VMEM, ANY],
        [pltpu.VMEM((8, cells), F32), pltpu.VMEM((tall, wide), F32), pltpu.SemaphoreType.DMA],
    )
    returned = swap(backward(scale, table, pairs, base, other), SHARE_AXES)
    totals = call(
        collect_kernel,
        shape((groups, attrs, SUB * LANES), LOW),
        (attributes, returned),
        [VMEM, VMEM],
        [pltpu.VMEM((margs * CHUNKS * 3 * SUB, LANES), F32)],
    )
    return call(
        adam_kernel,
        (shape((rows, cols), F32),) * 3,
        (swap(totals, MARG_AXES), probs, logits, first_moment, second_moment),
        [VMEM] * 5,
        [pltpu.VMEM((cols, rows), F32)],
    )


def solution(mesh):
    fine = Mesh(mesh.devices.reshape(PARTS), NAMES)
    table = P(ROW_AXES, MARG_AXES)
    listed = P(MARG_AXES, None)
    return jax.shard_map(
        shards,
        mesh=fine,
        in_specs=(table, table, table, listed, listed),
        out_specs=(table, table, table),
        check_vma=False,
    )
```

```python
import jax
import jax.numpy as jnp
from jax import lax
from jax.experimental import pallas as pl
from jax.experimental.pallas import tpu as pltpu
from jax.sharding import Mesh, PartitionSpec as P

V = 32
ADAM_STEP = 4
PARTS = (4, 2, 2, 2, 4, 2)
NAMES = ("x", "u", "w", "c", "y", "h")
ROW_AXES = ("x", "u", "w", "c")
MARG_AXES = ("y", "h")
PLACE_AXES = ("x", "w", "c")
SHARE_AXES = ("x", "w", "c", "y")
CHUNKS = 4
CHUNK = 32
LANES = CHUNKS * CHUNK
SUB = V // CHUNKS
MODS = 4
MARGS = 16
VMEM = pl.BlockSpec(memory_space=pltpu.VMEM)
SMEM = pl.BlockSpec(memory_space=pltpu.SMEM)
ANY = pl.BlockSpec(memory_space=pl.ANY)
LIMIT = 20 * 1024 * 1024
F32 = jnp.float32
LOW = jnp.bfloat16


def call(body, out_shape, operands, specs, scratch=()):
    return pl.pallas_call(
        body,
        out_shape=out_shape,
        in_specs=specs,
        out_specs=jax.tree.map(lambda unused: VMEM, out_shape),
        scratch_shapes=scratch,
        compiler_params=pltpu.CompilerParams(vmem_limit_bytes=LIMIT),
    )(*operands)


def exchange(blocks):
    lane = lax.broadcasted_iota(jnp.int32, blocks[0].shape, 1)
    blocks = list(blocks)
    for width, pairs in ((2 * CHUNK, ((0, 2), (1, 3))), (CHUNK, ((0, 1), (2, 3)))):
        low_part = (lane // width) % 2 == 0
        for a, b in pairs:
            left, right = blocks[a], blocks[b]
            blocks[a] = jnp.where(low_part, left, pltpu.roll(right, width, 1))
            blocks[b] = jnp.where(low_part, pltpu.roll(left, LANES - width, 1), right)
    return blocks


def stay(value):
    return pltpu.with_memory_space_constraint(value, pltpu.HBM)


def relax_kernel(
    side_ref,
    place_ref,
    triples_hbm,
    logits_hbm,
    probs_ref,
    send_ref,
    tile_ref,
    triples_ref,
    logits_ref,
    flipped_ref,
    sems,
):
    logits_copy = pltpu.make_async_copy(logits_hbm, logits_ref, sems.at[0])
    triples_copy = pltpu.make_async_copy(triples_hbm, triples_ref, sems.at[1])
    logits_copy.start()
    triples_copy.start()
    logits_copy.wait()
    flipped_ref[...] = logits_ref[...].T
    attrs = probs_ref.shape[1]
    halves = send_ref.shape[0] // CHUNKS
    values = [flipped_ref[pl.ds(value, attrs, stride=V), :] for value in range(V)]
    top = values[0]
    for value in values[1:]:
        top = jnp.maximum(top, value)
    expos = [jnp.exp(value - top) for value in values]
    total = expos[0]
    for expo in expos[1:]:
        total = total + expo
    probs = [expo / total for expo in expos]
    for value in range(V):
        probs_ref[value] = probs[value]
    for rest in range(SUB):
        for chunk, packed in enumerate(exchange([probs[part * SUB + rest] for part in range(CHUNKS)])):
            low = packed.astype(LOW)
            for half in range(halves):
                send_ref[chunk * halves + half, :, rest * LANES : (rest + 1) * LANES] = low
    triples_copy.wait()
    tile_ref[...] = jnp.zeros(tile_ref.shape, F32)
    tile_ref[0:3, 0 : triples_ref.shape[1]] = triples_ref[...].astype(F32)
    for half in range(halves):
        tile = (tile_ref[...] * jnp.where(side_ref[0] == half, 1.0, 0.0)).astype(LOW)
        for chunk in range(CHUNKS):
            send_ref[chunk * halves + half, :, SUB * LANES :] = tile


def one_hot(triples, which, count):
    width = CHUNKS * MARGS
    row = jnp.broadcast_to(triples[which : which + 1, 0:width], (count, width))
    attr = lax.broadcasted_iota(jnp.int32, (count, width), 0).astype(F32)
    return jnp.where(row == attr, 1.0, 0.0).astype(LOW)


def tile_rows(which, rest):
    step = 3 * SUB
    for chunk in range(CHUNKS):
        for start in range(0, MARGS, SUB):
            rows = pl.ds((start * CHUNKS + chunk) * step + which * SUB + rest, SUB, stride=CHUNKS * step)
            yield rows, chunk * MARGS + start


def select_kernel(full_ref, send_ref, triples_ref, picked_ref):
    groups, attrs = full_ref.shape[0], full_ref.shape[1]
    halves = groups // CHUNKS
    full = [full_ref[index].astype(F32) for index in range(groups)]
    triples = jnp.zeros(triples_ref.shape, F32)
    for chunk in range(CHUNKS):
        tile = full[chunk * halves][:, SUB * LANES :]
        for half in range(1, halves):
            tile += full[chunk * halves + half][:, SUB * LANES :]
        triples += pltpu.roll(tile, chunk * MARGS, 1) if chunk else tile
    triples_ref[...] = triples
    table = jnp.concatenate([value[:, 0 : SUB * LANES] for value in full], axis=0).astype(LOW)
    for which in range(3):
        mine = one_hot(triples, which, groups * attrs)
        picked = lax.dot_general(mine, table, (((0,), (0,)), ((), ())), preferred_element_type=F32)
        for rest in range(SUB):
            for rows, place in tile_rows(which, rest):
                picked_ref[rows, :] = picked[place : place + SUB, rest * LANES : (rest + 1) * LANES]
    send_ref[...] = picked_ref[...].reshape(send_ref.shape).astype(LOW)


def unpack(src_ref, shard):
    packed = [src_ref[shard * CHUNKS + chunk].astype(F32).reshape(3 * SUB, LANES) for chunk in range(CHUNKS)]
    parts = exchange(packed)
    return [
        jnp.concatenate([part[which * SUB : (which + 1) * SUB, :] for part in parts], axis=0) for which in range(3)
    ]


def answer_kernel(src_ref, own_ref, send_ref, table_ref, pairs_ref):
    shards = table_ref.shape[0]

    def fill(step):
        for part in range(2):
            shard = 2 * step + part
            first, second, third = [value.astype(LOW) for value in unpack(src_ref, shard)]
            table_ref[shard, 0] = first
            table_ref[shard, 1] = second
            table_ref[shard, 2] = third
            for value in range(V):
                row = jnp.broadcast_to(second[value : value + 1, :], first.shape)
                mod, rest = value % MODS, value // MODS
                pairs_ref[step, mod, rest * V : (rest + 1) * V, part * LANES : (part + 1) * LANES] = first * row

    def add(step):
        third = jnp.concatenate([table_ref[2 * step, 2], table_ref[2 * step + 1, 2]], axis=1)
        for mod in range(MODS):
            own_ref[mod * V : (mod + 1) * V, :] += lax.dot_general(
                third, pairs_ref[step, mod], (((1,), (1,)), ((), ())), preferred_element_type=F32
            )

    own_ref[...] = jnp.zeros(own_ref.shape, F32)
    fill(0)

    def both(step, carry):
        add(step - 1)
        fill(step)
        return carry

    lax.fori_loop(1, shards // 2, both, 0, unroll=shards // 2 - 1)
    add(shards // 2 - 1)
    send_ref[...] = own_ref[...].astype(LOW)


def base_kernel(scale, place_ref, own_ref, targets_any, base_ref, block_ref, target_ref, sem):
    place = place_ref[0]
    start = pl.multiple_of(place // 8 * 8, 8)
    copy = pltpu.make_async_copy(targets_any.at[pl.ds(start, 8), :], block_ref, sem)
    copy.start()
    copy.wait()
    mine = lax.broadcasted_iota(jnp.int32, (8, LANES), 0) == lax.rem(place, 8)
    for rest in range(SUB):
        for value in range(V):
            tile = block_ref[:, pl.ds((value * SUB + rest) * LANES, LANES)]
            row = jnp.sum(jnp.where(mine, tile, 0.0), axis=0, keepdims=True)
            target_ref[pl.ds(rest * V + value, 1), :] = row
    base_ref[...] = scale * own_ref[...] - target_ref[...].T


def backward_kernel(scale, table_ref, pairs_ref, base_ref, other_ref, out_ref, low_ref, mask_ref, row_ref, sum_ref):
    steps = pairs_ref.shape[0]
    wide = 2 * LANES
    resid = base_ref[...] + scale * other_ref[...].astype(F32)
    low_ref[...] = resid.astype(LOW)
    flipped = resid.T
    lane_mod = lax.broadcasted_iota(jnp.int32, flipped.shape, 1) // V
    for mod in range(MODS):
        mask_ref[mod] = jnp.where(lane_mod == mod, flipped, 0.0).astype(LOW)

    def step(index, carry):
        pair = [
            jnp.concatenate([table_ref[2 * index, which], table_ref[2 * index + 1, which]], axis=1)
            for which in range(3)
        ]
        first = pair[0].astype(F32)
        row_ref[...] = pair[1].astype(F32)
        stacked = jnp.concatenate([pair[2]] * MODS, axis=0)
        third_grad = jnp.zeros((V, wide), F32)
        first_grad = jnp.zeros((V, wide), F32)
        for mod in range(MODS):
            third_grad += jnp.dot(
                low_ref[mod * V : (mod + 1) * V, :], pairs_ref[index, mod], preferred_element_type=F32
            )
            cross = jnp.dot(mask_ref[mod], stacked, preferred_element_type=F32)
            for rest in range(SUB):
                value = rest * MODS + mod
                block = cross[rest * V : (rest + 1) * V, :]
                first_grad += block * row_ref[pl.ds(value, 1), :]
                product = block * first
                partial = product[0:8]
                for part in range(1, V // 8):
                    partial += product[8 * part : 8 * part + 8]
                for half in range(2):
                    sum_ref[half, value * 8 : value * 8 + 8, :] = partial[:, half * LANES : (half + 1) * LANES]
        mean = jnp.sum(first * first_grad, axis=0, keepdims=True)
        for half in range(2):
            lanes = slice(half * LANES, (half + 1) * LANES)
            second_grad = jnp.zeros((V, LANES), F32)
            for part in range(8):
                second_grad += sum_ref[half, pl.ds(part, V, stride=8), :]
            centre = jnp.broadcast_to(mean[:, lanes], (V, LANES))
            grads = [grad - centre for grad in (first_grad[:, lanes], second_grad, third_grad[:, lanes])]
            parts = [
                jnp.concatenate([grad[part * SUB : (part + 1) * SUB, :] for grad in grads], axis=0)
                for part in range(CHUNKS)
            ]
            for chunk, packed in enumerate(exchange(parts)):
                place = (2 * index + half) * CHUNKS + chunk
                out_ref[place] = packed.reshape(3, SUB, LANES).astype(LOW)
        return carry

    lax.fori_loop(0, steps, step, 0, unroll=steps)


def collect_kernel(triples_ref, grads_ref, send_ref, grad_ref):
    groups, attrs = send_ref.shape[0], send_ref.shape[1]
    triples = triples_ref[...]
    grad_ref[...] = grads_ref[...].astype(F32).reshape(grad_ref.shape)
    total = jnp.zeros((groups * attrs, SUB * LANES), F32)
    for which in range(3):
        parts = []
        for rest in range(SUB):
            tiles = [grad_ref[rows, :] for rows, unused in tile_rows(which, rest)]
            parts.append(jnp.concatenate(tiles, axis=0))
        grads = jnp.concatenate(parts, axis=1).astype(LOW)
        total += jnp.dot(one_hot(triples, which, groups * attrs), grads, preferred_element_type=F32)
    for index in range(groups):
        send_ref[index] = total[index * attrs : (index + 1) * attrs, :].astype(LOW)


def adam_kernel(
    parts_ref, probs_ref, logits_ref, first_ref, second_ref, out_logits_ref, out_first_ref, out_second_ref, grad_ref
):
    groups, attrs = parts_ref.shape[0], parts_ref.shape[1]
    halves = groups // CHUNKS
    chunks = []
    for chunk in range(CHUNKS):
        total = parts_ref[chunk * halves].astype(F32)
        for half in range(1, halves):
            total += parts_ref[chunk * halves + half].astype(F32)
        chunks.append(total)
    row_grad = [None] * V
    for rest in range(SUB):
        blocks = [chunk[:, rest * LANES : (rest + 1) * LANES] for chunk in chunks]
        for part, block in enumerate(exchange(blocks)):
            row_grad[part * SUB + rest] = block
    inner = jnp.zeros((attrs, LANES), F32)
    for value in range(V):
        inner += probs_ref[value] * row_grad[value]
    for value in range(V):
        grad_ref[pl.ds(value, attrs, stride=V), :] = 512.0 * probs_ref[value] * (row_grad[value] - inner)
    grad = grad_ref[...].T
    new_first = 0.9 * first_ref[...] + 0.1 * grad
    new_second = 0.999 * second_ref[...] + 0.001 * grad * grad
    first_hat = new_first / (1.0 - 0.9**ADAM_STEP)
    second_hat = new_second / (1.0 - 0.999**ADAM_STEP)
    out_logits_ref[...] = logits_ref[...] - 0.5 * first_hat / (jnp.sqrt(second_hat) + 1e-08)
    out_first_ref[...] = new_first
    out_second_ref[...] = new_second


def swap(value, axes):
    return lax.all_to_all(value, axes, 0, 0, tiled=True)


def answers(src):
    shape = jax.ShapeDtypeStruct
    shards = src.shape[0] // CHUNKS
    tall, wide = V * V // MODS, V * MODS
    return call(
        answer_kernel,
        (
            shape((wide, tall), F32),
            shape((wide, tall), LOW),
            shape((shards, 3, V, LANES), LOW),
            shape((shards // 2, MODS, tall, 2 * LANES), LOW),
        ),
        (src,),
        [VMEM],
    )


def backward(scale, table, pairs, base, other):
    shards = table.shape[0]
    tall, wide = V * V // MODS, V * MODS
    return call(
        lambda *refs: backward_kernel(scale, *refs),
        jax.ShapeDtypeStruct((shards * CHUNKS, 3, SUB, LANES), LOW),
        (table, pairs, base, other),
        [VMEM] * 4,
        [
            pltpu.VMEM((wide, tall), LOW),
            pltpu.VMEM((MODS, tall, wide), LOW),
            pltpu.VMEM((V, 2 * LANES), F32),
            pltpu.VMEM((2, 8 * V, LANES), F32),
        ],
    )


def shards(logits, first_moment, second_moment, targets, triples):
    rows, cols = logits.shape
    margs, cells = targets.shape
    attrs = cols // V
    groups = lax.axis_size(MARG_AXES)
    scale = cells / (rows * lax.axis_size(ROW_AXES))
    shape = jax.ShapeDtypeStruct
    tall, wide = V * V // MODS, V * MODS
    place = lax.axis_index(PLACE_AXES).astype(jnp.int32).reshape(1)
    side = lax.axis_index("h").astype(jnp.int32).reshape(1)
    probs, copies = call(
        relax_kernel,
        (shape((V, attrs, rows), F32), shape((groups, attrs, (SUB + 1) * LANES), LOW)),
        (side, place, stay(triples.T), stay(logits)),
        [SMEM, SMEM, ANY, ANY],
        [
            pltpu.VMEM((SUB, LANES), F32),
            pltpu.VMEM((3, margs), jnp.int32),
            pltpu.VMEM((rows, cols), F32),
            pltpu.VMEM((cols, rows), F32),
            pltpu.SemaphoreType.DMA((2,)),
        ],
    )
    full = swap(copies, MARG_AXES)
    picked, attributes = call(
        select_kernel,
        (shape((margs * CHUNKS, 3, SUB, LANES), LOW), shape((SUB, LANES), F32)),
        (full,),
        [VMEM],
        [pltpu.VMEM((margs * CHUNKS * 3 * SUB, LANES), F32)],
    )
    own, send, table, pairs = answers(swap(picked, SHARE_AXES))
    other = lax.ppermute(send, "u", [(0, 1), (1, 0)])
    base = call(
        lambda *refs: base_kernel(scale, *refs),
        shape((wide, tall), F32),
        (place, own, stay(targets)),
        [SMEM, VMEM, ANY],
        [pltpu.VMEM((8, cells), F32), pltpu.VMEM((tall, wide), F32), pltpu.SemaphoreType.DMA],
    )
    returned = swap(backward(scale, table, pairs, base, other), SHARE_AXES)
    totals = call(
        collect_kernel,
        shape((groups, attrs, SUB * LANES), LOW),
        (attributes, returned),
        [VMEM, VMEM],
        [pltpu.VMEM((margs * CHUNKS * 3 * SUB, LANES), F32)],
    )
    return call(
        adam_kernel,
        (shape((rows, cols), F32),) * 3,
        (swap(totals, MARG_AXES), probs, logits, first_moment, second_moment),
        [VMEM] * 5,
        [pltpu.VMEM((cols, rows), F32)],
    )


def solution(mesh):
    fine = Mesh(mesh.devices.reshape(PARTS), NAMES)
    table = P(ROW_AXES, MARG_AXES)
    listed = P(MARG_AXES, None)
    return jax.shard_map(
        shards,
        mesh=fine,
        in_specs=(table, table, table, listed, listed),
        out_specs=(table, table, table),
        check_vma=False,
    )
```

```python
import jax
import jax.numpy as jnp
from jax import lax
from jax.experimental import pallas as pl
from jax.experimental.pallas import tpu as pltpu
from jax.sharding import Mesh, PartitionSpec as P

V = 32
ADAM_STEP = 4
PARTS = (4, 2, 2, 2, 4, 2)
NAMES = ("x", "u", "w", "c", "y", "h")
ROW_AXES = ("x", "u", "w", "c")
MARG_AXES = ("y", "h")
PLACE_AXES = ("c", "x", "w")
SHARE_AXES = ("x", "w", "y")
CORES = 2
CHUNKS = 4
CHUNK = 32
LANES = CHUNKS * CHUNK
SUB = V // CHUNKS
MODS = 4
MARGS = 8
VMEM = pl.BlockSpec(memory_space=pltpu.VMEM)
SMEM = pl.BlockSpec(memory_space=pltpu.SMEM)
ANY = pl.BlockSpec(memory_space=pl.ANY)
LIMIT = 20 * 1024 * 1024
F32 = jnp.float32
LOW = jnp.bfloat16


def call(body, out_shape, operands, specs, scratch=()):
    return pl.pallas_call(
        body,
        out_shape=out_shape,
        in_specs=specs,
        out_specs=jax.tree.map(lambda unused: VMEM, out_shape),
        scratch_shapes=scratch,
        compiler_params=pltpu.CompilerParams(vmem_limit_bytes=LIMIT),
    )(*operands)


def exchange(blocks):
    lane = lax.broadcasted_iota(jnp.int32, blocks[0].shape, 1)
    blocks = list(blocks)
    for width, pairs in ((2 * CHUNK, ((0, 2), (1, 3))), (CHUNK, ((0, 1), (2, 3)))):
        low_part = (lane // width) % 2 == 0
        for a, b in pairs:
            left, right = blocks[a], blocks[b]
            blocks[a] = jnp.where(low_part, left, pltpu.roll(right, width, 1))
            blocks[b] = jnp.where(low_part, pltpu.roll(left, LANES - width, 1), right)
    return blocks


def stay(value):
    return pltpu.with_memory_space_constraint(value, pltpu.HBM)


def relax_kernel(
    side_ref,
    place_ref,
    triples_hbm,
    logits_hbm,
    probs_ref,
    send_ref,
    tile_ref,
    triples_ref,
    logits_ref,
    flipped_ref,
    sems,
):
    logits_copy = pltpu.make_async_copy(logits_hbm, logits_ref, sems.at[0])
    triples_copy = pltpu.make_async_copy(triples_hbm, triples_ref, sems.at[1])
    logits_copy.start()
    triples_copy.start()
    logits_copy.wait()
    flipped_ref[...] = logits_ref[...].T
    attrs = probs_ref.shape[1]
    halves = send_ref.shape[0] // CHUNKS
    values = [flipped_ref[pl.ds(value, attrs, stride=V), :] for value in range(V)]
    top = values[0]
    for value in values[1:]:
        top = jnp.maximum(top, value)
    expos = [jnp.exp(value - top) for value in values]
    total = expos[0]
    for expo in expos[1:]:
        total = total + expo
    probs = [expo / total for expo in expos]
    for value in range(V):
        probs_ref[value] = probs[value]
    for rest in range(SUB):
        for chunk, packed in enumerate(exchange([probs[part * SUB + rest] for part in range(CHUNKS)])):
            low = packed.astype(LOW)
            for half in range(halves):
                send_ref[chunk * halves + half, :, rest * LANES : (rest + 1) * LANES] = low
    triples_copy.wait()
    tile_ref[...] = jnp.zeros(tile_ref.shape, F32)
    tile_ref[0:3, 0 : triples_ref.shape[1]] = triples_ref[...].astype(F32)
    both = tile_ref[...]
    first_core = jnp.where(place_ref[0] < MARGS, 1.0, 0.0)
    kept = both * first_core + pltpu.roll(both, LANES - MARGS, 1) * (1.0 - first_core)
    kept = jnp.where(lax.broadcasted_iota(jnp.int32, kept.shape, 1) < MARGS, kept, 0.0)
    for half in range(halves):
        tile = (kept * jnp.where(side_ref[0] == half, 1.0, 0.0)).astype(LOW)
        for chunk in range(CHUNKS):
            send_ref[chunk * halves + half, :, SUB * LANES :] = tile


def one_hot(triples, which, count):
    width = CHUNKS * MARGS
    row = jnp.broadcast_to(triples[which : which + 1, 0:width], (count, width))
    attr = lax.broadcasted_iota(jnp.int32, (count, width), 0).astype(F32)
    return jnp.where(row == attr, 1.0, 0.0).astype(LOW)


def tile_rows(core, which, rest):
    step = CORES * 3 * SUB
    for chunk in range(CHUNKS):
        rows = pl.ds(chunk * step + (core * 3 + which) * SUB + rest, MARGS, stride=CHUNKS * step)
        yield rows, chunk * MARGS


def select_kernel(full_ref, other_ref, send_ref, triples_ref, picked_ref):
    groups, attrs = full_ref.shape[0], full_ref.shape[1]
    halves = groups // CHUNKS
    triples = jnp.zeros(triples_ref.shape, F32)
    for chunk in range(CHUNKS):
        tile = jnp.zeros(triples_ref.shape, F32)
        for half in range(halves):
            tile += full_ref[chunk * halves + half, :, SUB * LANES :].astype(F32)
        triples += pltpu.roll(tile, chunk * MARGS, 1) if chunk else tile
    triples_ref[...] = triples
    hots = [one_hot(triples, which, groups * attrs) for which in range(3)]
    for core, table_ref in enumerate((full_ref, other_ref)):
        parts = [table_ref[index].astype(F32)[:, 0 : SUB * LANES] for index in range(groups)]
        table = jnp.concatenate(parts, axis=0).astype(LOW)
        for which in range(3):
            picked = lax.dot_general(hots[which], table, (((0,), (0,)), ((), ())), preferred_element_type=F32)
            for rest in range(SUB):
                for rows, place in tile_rows(core, which, rest):
                    picked_ref[rows, :] = picked[place : place + MARGS, rest * LANES : (rest + 1) * LANES]
    send_ref[...] = picked_ref[...].reshape(send_ref.shape).astype(LOW)


def unpack(src_ref, place, core):
    packed = [src_ref[place * CHUNKS + chunk, core].astype(F32).reshape(3 * SUB, LANES) for chunk in range(CHUNKS)]
    parts = exchange(packed)
    return [
        jnp.concatenate([part[which * SUB : (which + 1) * SUB, :] for part in parts], axis=0) for which in range(3)
    ]


def answer_kernel(src_ref, own_ref, send_ref, table_ref, pairs_ref):
    shards = table_ref.shape[0]

    def fill(step):
        for part in range(2):
            shard = 2 * step + part
            first, second, third = [value.astype(LOW) for value in unpack(src_ref, step, part)]
            table_ref[shard, 0] = first
            table_ref[shard, 1] = second
            table_ref[shard, 2] = third
            for value in range(V):
                row = jnp.broadcast_to(second[value : value + 1, :], first.shape)
                mod, rest = value % MODS, value // MODS
                pairs_ref[step, mod, rest * V : (rest + 1) * V, part * LANES : (part + 1) * LANES] = first * row

    def add(step):
        third = jnp.concatenate([table_ref[2 * step, 2], table_ref[2 * step + 1, 2]], axis=1)
        for mod in range(MODS):
            own_ref[mod * V : (mod + 1) * V, :] += lax.dot_general(
                third, pairs_ref[step, mod], (((1,), (1,)), ((), ())), preferred_element_type=F32
            )

    own_ref[...] = jnp.zeros(own_ref.shape, F32)
    fill(0)

    def both(step, carry):
        add(step - 1)
        fill(step)
        return carry

    lax.fori_loop(1, shards // 2, both, 0, unroll=shards // 2 - 1)
    add(shards // 2 - 1)
    send_ref[...] = own_ref[...].astype(LOW)


def base_kernel(scale, place_ref, own_ref, targets_any, base_ref, block_ref, target_ref, sem):
    place = place_ref[0]
    start = pl.multiple_of(place // 8 * 8, 8)
    copy = pltpu.make_async_copy(targets_any.at[pl.ds(start, 8), :], block_ref, sem)
    copy.start()
    copy.wait()
    mine = lax.broadcasted_iota(jnp.int32, (8, LANES), 0) == lax.rem(place, 8)
    for rest in range(SUB):
        for value in range(V):
            tile = block_ref[:, pl.ds((value * SUB + rest) * LANES, LANES)]
            row = jnp.sum(jnp.where(mine, tile, 0.0), axis=0, keepdims=True)
            target_ref[pl.ds(rest * V + value, 1), :] = row
    base_ref[...] = scale * own_ref[...] - target_ref[...].T


def backward_kernel(scale, table_ref, pairs_ref, base_ref, other_ref, out_ref, low_ref, mask_ref, row_ref, sum_ref):
    steps = pairs_ref.shape[0]
    wide = 2 * LANES
    resid = base_ref[...] + scale * other_ref[...].astype(F32)
    low_ref[...] = resid.astype(LOW)
    flipped = resid.T
    lane_mod = lax.broadcasted_iota(jnp.int32, flipped.shape, 1) // V
    for mod in range(MODS):
        mask_ref[mod] = jnp.where(lane_mod == mod, flipped, 0.0).astype(LOW)

    def step(index, carry):
        pair = [
            jnp.concatenate([table_ref[2 * index, which], table_ref[2 * index + 1, which]], axis=1)
            for which in range(3)
        ]
        first = pair[0].astype(F32)
        row_ref[...] = pair[1].astype(F32)
        stacked = jnp.concatenate([pair[2]] * MODS, axis=0)
        third_grad = jnp.zeros((V, wide), F32)
        first_grad = jnp.zeros((V, wide), F32)
        for mod in range(MODS):
            third_grad += jnp.dot(
                low_ref[mod * V : (mod + 1) * V, :], pairs_ref[index, mod], preferred_element_type=F32
            )
            cross = jnp.dot(mask_ref[mod], stacked, preferred_element_type=F32)
            for rest in range(SUB):
                value = rest * MODS + mod
                block = cross[rest * V : (rest + 1) * V, :]
                first_grad += block * row_ref[pl.ds(value, 1), :]
                product = block * first
                partial = product[0:8]
                for part in range(1, V // 8):
                    partial += product[8 * part : 8 * part + 8]
                for half in range(2):
                    sum_ref[half, value * 8 : value * 8 + 8, :] = partial[:, half * LANES : (half + 1) * LANES]
        mean = jnp.sum(first * first_grad, axis=0, keepdims=True)
        for half in range(2):
            lanes = slice(half * LANES, (half + 1) * LANES)
            second_grad = jnp.zeros((V, LANES), F32)
            for part in range(8):
                second_grad += sum_ref[half, pl.ds(part, V, stride=8), :]
            centre = jnp.broadcast_to(mean[:, lanes], (V, LANES))
            grads = [grad - centre for grad in (first_grad[:, lanes], second_grad, third_grad[:, lanes])]
            parts = [
                jnp.concatenate([grad[part * SUB : (part + 1) * SUB, :] for grad in grads], axis=0)
                for part in range(CHUNKS)
            ]
            for chunk, packed in enumerate(exchange(parts)):
                out_ref[index * CHUNKS + chunk, half] = packed.reshape(3, SUB, LANES).astype(LOW)
        return carry

    lax.fori_loop(0, steps, step, 0, unroll=steps)


def collect_kernel(triples_ref, grads_ref, own_ref, other_ref, grad_ref):
    attrs = own_ref.shape[0]
    triples = triples_ref[...]
    hots = [one_hot(triples, which, attrs) for which in range(3)]
    grad_ref[...] = grads_ref[...].astype(F32).reshape(grad_ref.shape)
    for core in range(CORES):
        total = jnp.zeros(own_ref.shape, F32)
        for which in range(3):
            parts = []
            for rest in range(SUB):
                tiles = [grad_ref[rows, :] for rows, unused in tile_rows(core, which, rest)]
                parts.append(jnp.concatenate(tiles, axis=0))
            grads = jnp.concatenate(parts, axis=1).astype(LOW)
            total += jnp.dot(hots[which], grads, preferred_element_type=F32)
        if core == 0:
            own_ref[...] = total
        else:
            other_ref[...] = total.astype(LOW)


def join_kernel(own_ref, other_ref, send_ref):
    groups, attrs = send_ref.shape[0], send_ref.shape[1]
    total = own_ref[...] + other_ref[...].astype(F32)
    for index in range(groups):
        send_ref[index] = total[index * attrs : (index + 1) * attrs, :].astype(LOW)


def adam_kernel(
    parts_ref, probs_ref, logits_ref, first_ref, second_ref, out_logits_ref, out_first_ref, out_second_ref, grad_ref
):
    groups, attrs = parts_ref.shape[0], parts_ref.shape[1]
    halves = groups // CHUNKS
    chunks = []
    for chunk in range(CHUNKS):
        total = parts_ref[chunk * halves].astype(F32)
        for half in range(1, halves):
            total += parts_ref[chunk * halves + half].astype(F32)
        chunks.append(total)
    row_grad = [None] * V
    for rest in range(SUB):
        blocks = [chunk[:, rest * LANES : (rest + 1) * LANES] for chunk in chunks]
        for part, block in enumerate(exchange(blocks)):
            row_grad[part * SUB + rest] = block
    inner = jnp.zeros((attrs, LANES), F32)
    for value in range(V):
        inner += probs_ref[value] * row_grad[value]
    for value in range(V):
        grad_ref[pl.ds(value, attrs, stride=V), :] = 512.0 * probs_ref[value] * (row_grad[value] - inner)
    grad = grad_ref[...].T
    new_first = 0.9 * first_ref[...] + 0.1 * grad
    new_second = 0.999 * second_ref[...] + 0.001 * grad * grad
    first_hat = new_first / (1.0 - 0.9**ADAM_STEP)
    second_hat = new_second / (1.0 - 0.999**ADAM_STEP)
    out_logits_ref[...] = logits_ref[...] - 0.5 * first_hat / (jnp.sqrt(second_hat) + 1e-08)
    out_first_ref[...] = new_first
    out_second_ref[...] = new_second


def swap(value, axes):
    return lax.all_to_all(value, axes, 0, 0, tiled=True)


def cross(value, axis):
    return lax.ppermute(value, axis, [(0, 1), (1, 0)])


def answers(src):
    shape = jax.ShapeDtypeStruct
    shards = src.shape[0] // CHUNKS * CORES
    tall, wide = V * V // MODS, V * MODS
    return call(
        answer_kernel,
        (
            shape((wide, tall), F32),
            shape((wide, tall), LOW),
            shape((shards, 3, V, LANES), LOW),
            shape((shards // 2, MODS, tall, 2 * LANES), LOW),
        ),
        (src,),
        [VMEM],
    )


def backward(scale, table, pairs, base, other):
    shards = table.shape[0]
    tall, wide = V * V // MODS, V * MODS
    return call(
        lambda *refs: backward_kernel(scale, *refs),
        jax.ShapeDtypeStruct((shards // CORES * CHUNKS, CORES, 3, SUB, LANES), LOW),
        (table, pairs, base, other),
        [VMEM] * 4,
        [
            pltpu.VMEM((wide, tall), LOW),
            pltpu.VMEM((MODS, tall, wide), LOW),
            pltpu.VMEM((V, 2 * LANES), F32),
            pltpu.VMEM((2, 8 * V, LANES), F32),
        ],
    )


def shards(logits, first_moment, second_moment, targets, triples):
    rows, cols = logits.shape
    margs, cells = targets.shape
    attrs = cols // V
    groups = lax.axis_size(MARG_AXES)
    scale = cells / (rows * lax.axis_size(ROW_AXES))
    shape = jax.ShapeDtypeStruct
    tall, wide = V * V // MODS, V * MODS
    place = lax.axis_index(PLACE_AXES).astype(jnp.int32).reshape(1)
    side = lax.axis_index("h").astype(jnp.int32).reshape(1)
    probs, copies = call(
        relax_kernel,
        (shape((V, attrs, rows), F32), shape((groups, attrs, (SUB + 1) * LANES), LOW)),
        (side, place, stay(triples.T), stay(logits)),
        [SMEM, SMEM, ANY, ANY],
        [
            pltpu.VMEM((SUB, LANES), F32),
            pltpu.VMEM((3, margs), jnp.int32),
            pltpu.VMEM((rows, cols), F32),
            pltpu.VMEM((cols, rows), F32),
            pltpu.SemaphoreType.DMA((2,)),
        ],
    )
    full = swap(copies, MARG_AXES)
    places = margs // CORES * CHUNKS
    lines = places * CORES * 3 * SUB
    picked, attributes = call(
        select_kernel,
        (shape((places, CORES, 3, SUB, LANES), LOW), shape((SUB, LANES), F32)),
        (full, cross(full, "c")),
        [VMEM, VMEM],
        [pltpu.VMEM((lines, LANES), F32)],
    )
    own, send, table, pairs = answers(swap(picked, SHARE_AXES))
    other = cross(send, "u")
    base = call(
        lambda *refs: base_kernel(scale, *refs),
        shape((wide, tall), F32),
        (place, own, stay(targets)),
        [SMEM, VMEM, ANY],
        [pltpu.VMEM((8, cells), F32), pltpu.VMEM((tall, wide), F32), pltpu.SemaphoreType.DMA],
    )
    returned = swap(backward(scale, table, pairs, base, other), SHARE_AXES)
    kept, given = call(
        collect_kernel,
        (shape((groups * attrs, SUB * LANES), F32), shape((groups * attrs, SUB * LANES), LOW)),
        (attributes, returned),
        [VMEM, VMEM],
        [pltpu.VMEM((lines, LANES), F32)],
    )
    totals = call(
        join_kernel, shape((groups, attrs, SUB * LANES), LOW), (kept, cross(given, "c")), [VMEM, VMEM]
    )
    return call(
        adam_kernel,
        (shape((rows, cols), F32),) * 3,
        (swap(totals, MARG_AXES), probs, logits, first_moment, second_moment),
        [VMEM] * 5,
        [pltpu.VMEM((cols, rows), F32)],
    )


def solution(mesh):
    fine = Mesh(mesh.devices.reshape(PARTS), NAMES)
    table = P(ROW_AXES, MARG_AXES)
    listed = P(MARG_AXES, None)
    return jax.shard_map(
        shards,
        mesh=fine,
        in_specs=(table, table, table, listed, listed),
        out_specs=(table, table, table),
        check_vma=False,
    )
```

```python
import jax
import jax.numpy as jnp
from jax import lax
from jax.experimental import pallas as pl
from jax.experimental.pallas import tpu as pltpu
from jax.sharding import Mesh, PartitionSpec as P

V = 32
ADAM_STEP = 4
PARTS = (4, 2, 2, 2, 4, 2)
NAMES = ("x", "u", "w", "c", "y", "h")
ROW_AXES = ("x", "u", "w", "c")
MARG_AXES = ("y", "h")
PLACE_AXES = ("c", "x", "w")
SHARE_AXES = ("x", "w", "y")
CORES = 2
CHUNKS = 4
CHUNK = 32
LANES = CHUNKS * CHUNK
SUB = V // CHUNKS
MODS = 4
MARGS = 8
VMEM = pl.BlockSpec(memory_space=pltpu.VMEM)
SMEM = pl.BlockSpec(memory_space=pltpu.SMEM)
ANY = pl.BlockSpec(memory_space=pl.ANY)
LIMIT = 20 * 1024 * 1024
F32 = jnp.float32
LOW = jnp.bfloat16


def call(body, out_shape, operands, specs, scratch=()):
    return pl.pallas_call(
        body,
        out_shape=out_shape,
        in_specs=specs,
        out_specs=jax.tree.map(lambda unused: VMEM, out_shape),
        scratch_shapes=scratch,
        compiler_params=pltpu.CompilerParams(vmem_limit_bytes=LIMIT),
    )(*operands)


def exchange(blocks):
    lane = lax.broadcasted_iota(jnp.int32, blocks[0].shape, 1)
    blocks = list(blocks)
    for width, pairs in ((2 * CHUNK, ((0, 2), (1, 3))), (CHUNK, ((0, 1), (2, 3)))):
        low_part = (lane // width) % 2 == 0
        for a, b in pairs:
            left, right = blocks[a], blocks[b]
            blocks[a] = jnp.where(low_part, left, pltpu.roll(right, width, 1))
            blocks[b] = jnp.where(low_part, pltpu.roll(left, LANES - width, 1), right)
    return blocks


def stay(value):
    return pltpu.with_memory_space_constraint(value, pltpu.HBM)


def relax_kernel(
    side_ref,
    place_ref,
    triples_hbm,
    logits_hbm,
    probs_ref,
    send_ref,
    tile_ref,
    triples_ref,
    logits_ref,
    flipped_ref,
    sems,
):
    logits_copy = pltpu.make_async_copy(logits_hbm, logits_ref, sems.at[0])
    triples_copy = pltpu.make_async_copy(triples_hbm, triples_ref, sems.at[1])
    logits_copy.start()
    triples_copy.start()
    logits_copy.wait()
    flipped_ref[...] = logits_ref[...].T
    attrs = probs_ref.shape[1]
    halves = send_ref.shape[0] // CHUNKS
    values = [flipped_ref[pl.ds(value, attrs, stride=V), :] for value in range(V)]
    top = values[0]
    for value in values[1:]:
        top = jnp.maximum(top, value)
    expos = [jnp.exp(value - top) for value in values]
    total = expos[0]
    for expo in expos[1:]:
        total = total + expo
    probs = [expo / total for expo in expos]
    for value in range(V):
        probs_ref[value] = probs[value]
    for rest in range(SUB):
        for chunk, packed in enumerate(exchange([probs[part * SUB + rest] for part in range(CHUNKS)])):
            low = packed.astype(LOW)
            for half in range(halves):
                send_ref[chunk * halves + half, :, rest * LANES : (rest + 1) * LANES] = low
    triples_copy.wait()
    tile_ref[...] = jnp.zeros(tile_ref.shape, F32)
    tile_ref[0:3, 0 : triples_ref.shape[1]] = triples_ref[...].astype(F32)
    both = tile_ref[...]
    first_core = jnp.where(place_ref[0] < MARGS, 1.0, 0.0)
    kept = both * first_core + pltpu.roll(both, LANES - MARGS, 1) * (1.0 - first_core)
    kept = jnp.where(lax.broadcasted_iota(jnp.int32, kept.shape, 1) < MARGS, kept, 0.0)
    for half in range(halves):
        tile = (kept * jnp.where(side_ref[0] == half, 1.0, 0.0)).astype(LOW)
        for chunk in range(CHUNKS):
            send_ref[chunk * halves + half, :, SUB * LANES :] = tile


def one_hot(triples, which, count):
    width = CHUNKS * MARGS
    row = jnp.broadcast_to(triples[which : which + 1, 0:width], (count, width))
    attr = lax.broadcasted_iota(jnp.int32, (count, width), 0).astype(F32)
    return jnp.where(row == attr, 1.0, 0.0).astype(LOW)


def tile_rows(which, rest, gap):
    for chunk in range(CHUNKS):
        rows = pl.ds(chunk * gap + which * SUB + rest, MARGS, stride=CHUNKS * gap)
        yield rows, chunk * MARGS


def pick(triples, table_ref, picked_ref):
    groups, attrs = table_ref.shape[0], table_ref.shape[1]
    parts = [table_ref[index].astype(F32)[:, 0 : SUB * LANES] for index in range(groups)]
    table = jnp.concatenate(parts, axis=0).astype(LOW)
    for which in range(3):
        mine = one_hot(triples, which, groups * attrs)
        picked = lax.dot_general(mine, table, (((0,), (0,)), ((), ())), preferred_element_type=F32)
        for rest in range(SUB):
            for rows, place in tile_rows(which, rest, 3 * SUB):
                picked_ref[rows, :] = picked[place : place + MARGS, rest * LANES : (rest + 1) * LANES]
    return picked_ref[...].reshape(CHUNKS * MARGS, 3, SUB, LANES).astype(LOW)


def select_kernel(full_ref, mine_ref, triples_ref, picked_ref):
    halves = full_ref.shape[0] // CHUNKS
    triples = jnp.zeros(triples_ref.shape, F32)
    for chunk in range(CHUNKS):
        tile = jnp.zeros(triples_ref.shape, F32)
        for half in range(halves):
            tile += full_ref[chunk * halves + half, :, SUB * LANES :].astype(F32)
        triples += pltpu.roll(tile, chunk * MARGS, 1) if chunk else tile
    triples_ref[...] = triples
    mine_ref[...] = pick(triples, full_ref, picked_ref)


def merge_kernel(triples_ref, mine_ref, other_ref, send_ref, picked_ref):
    theirs = pick(triples_ref[...], other_ref, picked_ref)
    for place in range(send_ref.shape[0]):
        send_ref[place, 0] = mine_ref[place]
        send_ref[place, 1] = theirs[place]


def unpack(src_ref, place, core):
    packed = [src_ref[place * CHUNKS + chunk, core].astype(F32).reshape(3 * SUB, LANES) for chunk in range(CHUNKS)]
    parts = exchange(packed)
    return [
        jnp.concatenate([part[which * SUB : (which + 1) * SUB, :] for part in parts], axis=0) for which in range(3)
    ]


def answer_kernel(src_ref, own_ref, send_ref, table_ref, pairs_ref):
    shards = table_ref.shape[0]

    def fill(step):
        for part in range(2):
            shard = 2 * step + part
            first, second, third = [value.astype(LOW) for value in unpack(src_ref, step, part)]
            table_ref[shard, 0] = first
            table_ref[shard, 1] = second
            table_ref[shard, 2] = third
            for value in range(V):
                row = jnp.broadcast_to(second[value : value + 1, :], first.shape)
                mod, rest = value % MODS, value // MODS
                pairs_ref[step, mod, rest * V : (rest + 1) * V, part * LANES : (part + 1) * LANES] = first * row

    def add(step):
        third = jnp.concatenate([table_ref[2 * step, 2], table_ref[2 * step + 1, 2]], axis=1)
        for mod in range(MODS):
            own_ref[mod * V : (mod + 1) * V, :] += lax.dot_general(
                third, pairs_ref[step, mod], (((1,), (1,)), ((), ())), preferred_element_type=F32
            )

    own_ref[...] = jnp.zeros(own_ref.shape, F32)
    fill(0)

    def both(step, carry):
        add(step - 1)
        fill(step)
        return carry

    lax.fori_loop(1, shards // 2, both, 0, unroll=shards // 2 - 1)
    add(shards // 2 - 1)
    send_ref[...] = own_ref[...].astype(LOW)


def base_kernel(scale, place_ref, own_ref, targets_any, base_ref, block_ref, target_ref, sem):
    place = place_ref[0]
    start = pl.multiple_of(place // 8 * 8, 8)
    copy = pltpu.make_async_copy(targets_any.at[pl.ds(start, 8), :], block_ref, sem)
    copy.start()
    copy.wait()
    mine = lax.broadcasted_iota(jnp.int32, (8, LANES), 0) == lax.rem(place, 8)
    for rest in range(SUB):
        for value in range(V):
            tile = block_ref[:, pl.ds((value * SUB + rest) * LANES, LANES)]
            row = jnp.sum(jnp.where(mine, tile, 0.0), axis=0, keepdims=True)
            target_ref[pl.ds(rest * V + value, 1), :] = row
    base_ref[...] = scale * own_ref[...] - target_ref[...].T


def backward_kernel(scale, table_ref, pairs_ref, base_ref, other_ref, out_ref, low_ref, mask_ref, row_ref, sum_ref):
    steps = pairs_ref.shape[0]
    wide = 2 * LANES
    resid = base_ref[...] + scale * other_ref[...].astype(F32)
    low_ref[...] = resid.astype(LOW)
    flipped = resid.T
    lane_mod = lax.broadcasted_iota(jnp.int32, flipped.shape, 1) // V
    for mod in range(MODS):
        mask_ref[mod] = jnp.where(lane_mod == mod, flipped, 0.0).astype(LOW)

    def step(index, carry):
        pair = [
            jnp.concatenate([table_ref[2 * index, which], table_ref[2 * index + 1, which]], axis=1)
            for which in range(3)
        ]
        first = pair[0].astype(F32)
        row_ref[...] = pair[1].astype(F32)
        stacked = jnp.concatenate([pair[2]] * MODS, axis=0)
        third_grad = jnp.zeros((V, wide), F32)
        first_grad = jnp.zeros((V, wide), F32)
        for mod in range(MODS):
            third_grad += jnp.dot(
                low_ref[mod * V : (mod + 1) * V, :], pairs_ref[index, mod], preferred_element_type=F32
            )
            cross = jnp.dot(mask_ref[mod], stacked, preferred_element_type=F32)
            for rest in range(SUB):
                value = rest * MODS + mod
                block = cross[rest * V : (rest + 1) * V, :]
                first_grad += block * row_ref[pl.ds(value, 1), :]
                product = block * first
                partial = product[0:8]
                for part in range(1, V // 8):
                    partial += product[8 * part : 8 * part + 8]
                for half in range(2):
                    sum_ref[half, value * 8 : value * 8 + 8, :] = partial[:, half * LANES : (half + 1) * LANES]
        mean = jnp.sum(first * first_grad, axis=0, keepdims=True)
        for half in range(2):
            lanes = slice(half * LANES, (half + 1) * LANES)
            second_grad = jnp.zeros((V, LANES), F32)
            for part in range(8):
                second_grad += sum_ref[half, pl.ds(part, V, stride=8), :]
            centre = jnp.broadcast_to(mean[:, lanes], (V, LANES))
            grads = [grad - centre for grad in (first_grad[:, lanes], second_grad, third_grad[:, lanes])]
            parts = [
                jnp.concatenate([grad[part * SUB : (part + 1) * SUB, :] for grad in grads], axis=0)
                for part in range(CHUNKS)
            ]
            for chunk, packed in enumerate(exchange(parts)):
                out_ref[index * CHUNKS + chunk, half] = packed.reshape(3, SUB, LANES).astype(LOW)
        return carry

    lax.fori_loop(0, steps, step, 0, unroll=steps)


def collect_kernel(core, triples_ref, grads_ref, total_ref, grad_ref):
    attrs = total_ref.shape[0]
    triples = triples_ref[...]
    grad_ref[...] = grads_ref[:, core].astype(F32).reshape(grad_ref.shape)
    total = jnp.zeros(total_ref.shape, F32)
    for which in range(3):
        parts = []
        for rest in range(SUB):
            tiles = [grad_ref[rows, :] for rows, unused in tile_rows(which, rest, 3 * SUB)]
            parts.append(jnp.concatenate(tiles, axis=0))
        grads = jnp.concatenate(parts, axis=1).astype(LOW)
        total += jnp.dot(one_hot(triples, which, attrs), grads, preferred_element_type=F32)
    total_ref[...] = total.astype(total_ref.dtype)


def join_kernel(own_ref, other_ref, send_ref):
    groups, attrs = send_ref.shape[0], send_ref.shape[1]
    total = own_ref[...] + other_ref[...].astype(F32)
    for index in range(groups):
        send_ref[index] = total[index * attrs : (index + 1) * attrs, :].astype(LOW)


def adam_kernel(
    parts_ref, probs_ref, logits_ref, first_ref, second_ref, out_logits_ref, out_first_ref, out_second_ref, grad_ref
):
    groups, attrs = parts_ref.shape[0], parts_ref.shape[1]
    halves = groups // CHUNKS
    chunks = []
    for chunk in range(CHUNKS):
        total = parts_ref[chunk * halves].astype(F32)
        for half in range(1, halves):
            total += parts_ref[chunk * halves + half].astype(F32)
        chunks.append(total)
    row_grad = [None] * V
    for rest in range(SUB):
        blocks = [chunk[:, rest * LANES : (rest + 1) * LANES] for chunk in chunks]
        for part, block in enumerate(exchange(blocks)):
            row_grad[part * SUB + rest] = block
    inner = jnp.zeros((attrs, LANES), F32)
    for value in range(V):
        inner += probs_ref[value] * row_grad[value]
    for value in range(V):
        grad_ref[pl.ds(value, attrs, stride=V), :] = 512.0 * probs_ref[value] * (row_grad[value] - inner)
    grad = grad_ref[...].T
    new_first = 0.9 * first_ref[...] + 0.1 * grad
    new_second = 0.999 * second_ref[...] + 0.001 * grad * grad
    first_hat = new_first / (1.0 - 0.9**ADAM_STEP)
    second_hat = new_second / (1.0 - 0.999**ADAM_STEP)
    out_logits_ref[...] = logits_ref[...] - 0.5 * first_hat / (jnp.sqrt(second_hat) + 1e-08)
    out_first_ref[...] = new_first
    out_second_ref[...] = new_second


def swap(value, axes):
    return lax.all_to_all(value, axes, 0, 0, tiled=True)


def cross(value, axis):
    return lax.ppermute(value, axis, [(0, 1), (1, 0)])


def answers(src):
    shape = jax.ShapeDtypeStruct
    shards = src.shape[0] // CHUNKS * CORES
    tall, wide = V * V // MODS, V * MODS
    return call(
        answer_kernel,
        (
            shape((wide, tall), F32),
            shape((wide, tall), LOW),
            shape((shards, 3, V, LANES), LOW),
            shape((shards // 2, MODS, tall, 2 * LANES), LOW),
        ),
        (src,),
        [VMEM],
    )


def backward(scale, table, pairs, base, other):
    shards = table.shape[0]
    tall, wide = V * V // MODS, V * MODS
    return call(
        lambda *refs: backward_kernel(scale, *refs),
        jax.ShapeDtypeStruct((shards // CORES * CHUNKS, CORES, 3, SUB, LANES), LOW),
        (table, pairs, base, other),
        [VMEM] * 4,
        [
            pltpu.VMEM((wide, tall), LOW),
            pltpu.VMEM((MODS, tall, wide), LOW),
            pltpu.VMEM((V, 2 * LANES), F32),
            pltpu.VMEM((2, 8 * V, LANES), F32),
        ],
    )


def shards(logits, first_moment, second_moment, targets, triples):
    rows, cols = logits.shape
    margs, cells = targets.shape
    attrs = cols // V
    groups = lax.axis_size(MARG_AXES)
    scale = cells / (rows * lax.axis_size(ROW_AXES))
    shape = jax.ShapeDtypeStruct
    tall, wide = V * V // MODS, V * MODS
    place = lax.axis_index(PLACE_AXES).astype(jnp.int32).reshape(1)
    side = lax.axis_index("h").astype(jnp.int32).reshape(1)
    probs, copies = call(
        relax_kernel,
        (shape((V, attrs, rows), F32), shape((groups, attrs, (SUB + 1) * LANES), LOW)),
        (side, place, stay(triples.T), stay(logits)),
        [SMEM, SMEM, ANY, ANY],
        [
            pltpu.VMEM((SUB, LANES), F32),
            pltpu.VMEM((3, margs), jnp.int32),
            pltpu.VMEM((rows, cols), F32),
            pltpu.VMEM((cols, rows), F32),
            pltpu.SemaphoreType.DMA((2,)),
        ],
    )
    full = swap(copies, MARG_AXES)
    places = margs // CORES * CHUNKS
    lines = [pltpu.VMEM((places * 3 * SUB, LANES), F32)]
    other_full = cross(full, "c")
    mine, attributes = call(
        select_kernel,
        (shape((places, 3, SUB, LANES), LOW), shape((SUB, LANES), F32)),
        (full,),
        [VMEM],
        lines,
    )
    picked = call(
        merge_kernel,
        shape((places, CORES, 3, SUB, LANES), LOW),
        (attributes, mine, other_full),
        [VMEM] * 3,
        lines,
    )
    own, send, table, pairs = answers(swap(picked, SHARE_AXES))
    other = cross(send, "u")
    base = call(
        lambda *refs: base_kernel(scale, *refs),
        shape((wide, tall), F32),
        (place, own, stay(targets)),
        [SMEM, VMEM, ANY],
        [pltpu.VMEM((8, cells), F32), pltpu.VMEM((tall, wide), F32), pltpu.SemaphoreType.DMA],
    )
    returned = swap(backward(scale, table, pairs, base, other), SHARE_AXES)
    given, kept = [
        call(
            lambda *refs, core=core: collect_kernel(core, *refs),
            shape((groups * attrs, SUB * LANES), kind),
            (attributes, returned),
            [VMEM, VMEM],
            lines,
        )
        for core, kind in ((1, LOW), (0, F32))
    ]
    totals = call(
        join_kernel, shape((groups, attrs, SUB * LANES), LOW), (kept, cross(given, "c")), [VMEM, VMEM]
    )
    return call(
        adam_kernel,
        (shape((rows, cols), F32),) * 3,
        (swap(totals, MARG_AXES), probs, logits, first_moment, second_moment),
        [VMEM] * 5,
        [pltpu.VMEM((cols, rows), F32)],
    )


def solution(mesh):
    fine = Mesh(mesh.devices.reshape(PARTS), NAMES)
    table = P(ROW_AXES, MARG_AXES)
    listed = P(MARG_AXES, None)
    return jax.shard_map(
        shards,
        mesh=fine,
        in_specs=(table, table, table, listed, listed),
        out_specs=(table, table, table),
        check_vma=False,
    )
```

```python
import jax
import jax.numpy as jnp
from jax import lax
from jax.experimental import pallas as pl
from jax.experimental.pallas import tpu as pltpu
from jax.sharding import Mesh, PartitionSpec as P

V = 32
ADAM_STEP = 4
PARTS = (4, 2, 2, 2, 4, 2)
NAMES = ("x", "u", "w", "c", "y", "h")
ROW_AXES = ("x", "u", "w", "c")
MARG_AXES = ("y", "h")
PLACE_AXES = ("c", "x", "w")
SHARE_AXES = ("x", "w", "y")
CORES = 2
CHUNKS = 4
CHUNK = 32
LANES = CHUNKS * CHUNK
SUB = V // CHUNKS
MODS = 4
MARGS = 8
VMEM = pl.BlockSpec(memory_space=pltpu.VMEM)
SMEM = pl.BlockSpec(memory_space=pltpu.SMEM)
ANY = pl.BlockSpec(memory_space=pl.ANY)
LIMIT = 20 * 1024 * 1024
F32 = jnp.float32
LOW = jnp.bfloat16


def call(body, out_shape, operands, specs, scratch=()):
    return pl.pallas_call(
        body,
        out_shape=out_shape,
        in_specs=specs,
        out_specs=jax.tree.map(lambda unused: VMEM, out_shape),
        scratch_shapes=scratch,
        compiler_params=pltpu.CompilerParams(vmem_limit_bytes=LIMIT),
    )(*operands)


def exchange(blocks):
    lane = lax.broadcasted_iota(jnp.int32, blocks[0].shape, 1)
    blocks = list(blocks)
    for width, pairs in ((2 * CHUNK, ((0, 2), (1, 3))), (CHUNK, ((0, 1), (2, 3)))):
        low_part = (lane // width) % 2 == 0
        for a, b in pairs:
            left, right = blocks[a], blocks[b]
            blocks[a] = jnp.where(low_part, left, pltpu.roll(right, width, 1))
            blocks[b] = jnp.where(low_part, pltpu.roll(left, LANES - width, 1), right)
    return blocks


def stay(value):
    return pltpu.with_memory_space_constraint(value, pltpu.HBM)


def relax_kernel(
    side_ref,
    place_ref,
    triples_hbm,
    logits_hbm,
    probs_ref,
    send_ref,
    tile_ref,
    triples_ref,
    logits_ref,
    flipped_ref,
    sems,
):
    span = logits_ref.shape[0] // 2
    halves_of = [pl.ds(part * span, span) for part in range(2)]
    copies = [
        pltpu.make_async_copy(logits_hbm.at[rows, :], logits_ref.at[rows, :], sems.at[part])
        for part, rows in enumerate(halves_of)
    ]
    triples_copy = pltpu.make_async_copy(triples_hbm, triples_ref, sems.at[2])
    for copy in copies:
        copy.start()
    triples_copy.start()
    for copy, rows in zip(copies, halves_of):
        copy.wait()
        flipped_ref[:, rows] = logits_ref[rows, :].T
    attrs = probs_ref.shape[1]
    halves = send_ref.shape[0] // CHUNKS
    values = [flipped_ref[pl.ds(value, attrs, stride=V), :] for value in range(V)]
    top = values[0]
    for value in values[1:]:
        top = jnp.maximum(top, value)
    expos = [jnp.exp(value - top) for value in values]
    total = expos[0]
    for expo in expos[1:]:
        total = total + expo
    scale = 1.0 / total
    probs = [expo * scale for expo in expos]
    for value in range(V):
        probs_ref[value] = probs[value]
    for rest in range(SUB):
        for chunk, packed in enumerate(exchange([probs[part * SUB + rest] for part in range(CHUNKS)])):
            low = packed.astype(LOW)
            for half in range(halves):
                send_ref[chunk * halves + half, :, rest * LANES : (rest + 1) * LANES] = low
    triples_copy.wait()
    tile_ref[...] = jnp.zeros(tile_ref.shape, F32)
    tile_ref[0:3, 0 : triples_ref.shape[1]] = triples_ref[...].astype(F32)
    both = tile_ref[...]
    first_core = jnp.where(place_ref[0] < MARGS, 1.0, 0.0)
    kept = both * first_core + pltpu.roll(both, LANES - MARGS, 1) * (1.0 - first_core)
    kept = jnp.where(lax.broadcasted_iota(jnp.int32, kept.shape, 1) < MARGS, kept, 0.0)
    for half in range(halves):
        tile = (kept * jnp.where(side_ref[0] == half, 1.0, 0.0)).astype(LOW)
        for chunk in range(CHUNKS):
            send_ref[chunk * halves + half, :, SUB * LANES :] = tile


def one_hot(triples, which, count):
    width = CHUNKS * MARGS
    row = jnp.broadcast_to(triples[which : which + 1, 0:width], (count, width))
    attr = lax.broadcasted_iota(jnp.int32, (count, width), 0).astype(F32)
    return jnp.where(row == attr, 1.0, 0.0).astype(LOW)


def tile_rows(which, rest, gap):
    for chunk in range(CHUNKS):
        rows = pl.ds(chunk * gap + which * SUB + rest, MARGS, stride=CHUNKS * gap)
        yield rows, chunk * MARGS


def pick(triples, table_ref, picked_ref):
    groups, attrs = table_ref.shape[0], table_ref.shape[1]
    parts = [table_ref[index].astype(F32)[:, 0 : SUB * LANES] for index in range(groups)]
    table = jnp.concatenate(parts, axis=0).astype(LOW)
    for which in range(3):
        mine = one_hot(triples, which, groups * attrs)
        picked = lax.dot_general(mine, table, (((0,), (0,)), ((), ())), preferred_element_type=F32)
        for rest in range(SUB):
            for rows, place in tile_rows(which, rest, 3 * SUB):
                picked_ref[rows, :] = picked[place : place + MARGS, rest * LANES : (rest + 1) * LANES]
    return picked_ref[...].reshape(CHUNKS * MARGS, 3, SUB, LANES).astype(LOW)


def select_kernel(full_ref, mine_ref, triples_ref, picked_ref):
    halves = full_ref.shape[0] // CHUNKS
    triples = jnp.zeros(triples_ref.shape, F32)
    for chunk in range(CHUNKS):
        tile = jnp.zeros(triples_ref.shape, F32)
        for half in range(halves):
            tile += full_ref[chunk * halves + half, :, SUB * LANES :].astype(F32)
        triples += pltpu.roll(tile, chunk * MARGS, 1) if chunk else tile
    triples_ref[...] = triples
    mine_ref[...] = pick(triples, full_ref, picked_ref)


def merge_kernel(triples_ref, mine_ref, other_ref, send_ref, picked_ref):
    theirs = pick(triples_ref[...], other_ref, picked_ref)
    for place in range(send_ref.shape[0]):
        send_ref[place, 0] = mine_ref[place]
        send_ref[place, 1] = theirs[place]


def unpack(src_ref, place, core):
    packed = [src_ref[place * CHUNKS + chunk, core].astype(F32).reshape(3 * SUB, LANES) for chunk in range(CHUNKS)]
    parts = exchange(packed)
    return [
        jnp.concatenate([part[which * SUB : (which + 1) * SUB, :] for part in parts], axis=0) for which in range(3)
    ]


def answer_kernel(src_ref, own_ref, send_ref, table_ref, pairs_ref):
    shards = table_ref.shape[0]

    def fill(step):
        for part in range(2):
            shard = 2 * step + part
            first, second, third = [value.astype(LOW) for value in unpack(src_ref, step, part)]
            table_ref[shard, 0] = first
            table_ref[shard, 1] = second
            table_ref[shard, 2] = third
            for value in range(V):
                row = jnp.broadcast_to(second[value : value + 1, :], first.shape)
                mod, rest = value % MODS, value // MODS
                pairs_ref[step, mod, rest * V : (rest + 1) * V, part * LANES : (part + 1) * LANES] = first * row

    def add(step):
        third = jnp.concatenate([table_ref[2 * step, 2], table_ref[2 * step + 1, 2]], axis=1)
        for mod in range(MODS):
            own_ref[mod * V : (mod + 1) * V, :] += lax.dot_general(
                third, pairs_ref[step, mod], (((1,), (1,)), ((), ())), preferred_element_type=F32
            )

    own_ref[...] = jnp.zeros(own_ref.shape, F32)
    fill(0)

    def both(step, carry):
        add(step - 1)
        fill(step)
        return carry

    lax.fori_loop(1, shards // 2, both, 0, unroll=shards // 2 - 1)
    add(shards // 2 - 1)
    send_ref[...] = own_ref[...].astype(LOW)


def base_kernel(scale, place_ref, own_ref, targets_any, base_ref, block_ref, target_ref, sem):
    place = place_ref[0]
    start = pl.multiple_of(place // 8 * 8, 8)
    copy = pltpu.make_async_copy(targets_any.at[pl.ds(start, 8), :], block_ref, sem)
    copy.start()
    copy.wait()
    mine = lax.broadcasted_iota(jnp.int32, (8, LANES), 0) == lax.rem(place, 8)
    for rest in range(SUB):
        for value in range(V):
            tile = block_ref[:, pl.ds((value * SUB + rest) * LANES, LANES)]
            row = jnp.sum(jnp.where(mine, tile, 0.0), axis=0, keepdims=True)
            target_ref[pl.ds(rest * V + value, 1), :] = row
    base_ref[...] = scale * own_ref[...] - target_ref[...].T


def backward_kernel(scale, table_ref, pairs_ref, base_ref, other_ref, out_ref, low_ref, mask_ref, row_ref, sum_ref):
    steps = pairs_ref.shape[0]
    wide = 2 * LANES
    resid = base_ref[...] + scale * other_ref[...].astype(F32)
    low_ref[...] = resid.astype(LOW)
    flipped = resid.T
    lane_mod = lax.broadcasted_iota(jnp.int32, flipped.shape, 1) // V
    for mod in range(MODS):
        mask_ref[mod] = jnp.where(lane_mod == mod, flipped, 0.0).astype(LOW)

    def step(index, carry):
        pair = [
            jnp.concatenate([table_ref[2 * index, which], table_ref[2 * index + 1, which]], axis=1)
            for which in range(3)
        ]
        first = pair[0].astype(F32)
        row_ref[...] = pair[1].astype(F32)
        stacked = jnp.concatenate([pair[2]] * MODS, axis=0)
        third_grad = jnp.zeros((V, wide), F32)
        first_grad = jnp.zeros((V, wide), F32)
        for mod in range(MODS):
            third_grad += jnp.dot(
                low_ref[mod * V : (mod + 1) * V, :], pairs_ref[index, mod], preferred_element_type=F32
            )
            cross = jnp.dot(mask_ref[mod], stacked, preferred_element_type=F32)
            for rest in range(SUB):
                value = rest * MODS + mod
                block = cross[rest * V : (rest + 1) * V, :]
                first_grad += block * row_ref[pl.ds(value, 1), :]
                product = block * first
                partial = product[0:8]
                for part in range(1, V // 8):
                    partial += product[8 * part : 8 * part + 8]
                for half in range(2):
                    sum_ref[half, value * 8 : value * 8 + 8, :] = partial[:, half * LANES : (half + 1) * LANES]
        mean = jnp.sum(first * first_grad, axis=0, keepdims=True)
        for half in range(2):
            lanes = slice(half * LANES, (half + 1) * LANES)
            second_grad = jnp.zeros((V, LANES), F32)
            for part in range(8):
                second_grad += sum_ref[half, pl.ds(part, V, stride=8), :]
            centre = jnp.broadcast_to(mean[:, lanes], (V, LANES))
            grads = [grad - centre for grad in (first_grad[:, lanes], second_grad, third_grad[:, lanes])]
            parts = [
                jnp.concatenate([grad[part * SUB : (part + 1) * SUB, :] for grad in grads], axis=0)
                for part in range(CHUNKS)
            ]
            for chunk, packed in enumerate(exchange(parts)):
                out_ref[index * CHUNKS + chunk, half] = packed.reshape(3, SUB, LANES).astype(LOW)
        return carry

    lax.fori_loop(0, steps, step, 0, unroll=steps)


def collect_kernel(core, triples_ref, grads_ref, total_ref, grad_ref):
    attrs = total_ref.shape[0]
    triples = triples_ref[...]
    grad_ref[...] = grads_ref[:, core].astype(F32).reshape(grad_ref.shape)
    total = jnp.zeros(total_ref.shape, F32)
    for which in range(3):
        parts = []
        for rest in range(SUB):
            tiles = [grad_ref[rows, :] for rows, unused in tile_rows(which, rest, 3 * SUB)]
            parts.append(jnp.concatenate(tiles, axis=0))
        grads = jnp.concatenate(parts, axis=1).astype(LOW)
        total += jnp.dot(one_hot(triples, which, attrs), grads, preferred_element_type=F32)
    total_ref[...] = total.astype(total_ref.dtype)


def join_kernel(own_ref, other_ref, send_ref):
    groups, attrs = send_ref.shape[0], send_ref.shape[1]
    total = own_ref[...] + other_ref[...].astype(F32)
    for index in range(groups):
        send_ref[index] = total[index * attrs : (index + 1) * attrs, :].astype(LOW)


def adam_kernel(
    parts_ref, probs_ref, logits_ref, first_ref, second_ref, out_logits_ref, out_first_ref, out_second_ref, grad_ref
):
    groups, attrs = parts_ref.shape[0], parts_ref.shape[1]
    halves = groups // CHUNKS
    chunks = []
    for chunk in range(CHUNKS):
        total = parts_ref[chunk * halves].astype(F32)
        for half in range(1, halves):
            total += parts_ref[chunk * halves + half].astype(F32)
        chunks.append(total)
    row_grad = [None] * V
    for rest in range(SUB):
        blocks = [chunk[:, rest * LANES : (rest + 1) * LANES] for chunk in chunks]
        for part, block in enumerate(exchange(blocks)):
            row_grad[part * SUB + rest] = block
    inner = jnp.zeros((attrs, LANES), F32)
    for value in range(V):
        inner += probs_ref[value] * row_grad[value]
    for value in range(V):
        grad_ref[pl.ds(value, attrs, stride=V), :] = 512.0 * probs_ref[value] * (row_grad[value] - inner)
    grad = grad_ref[...].T
    new_first = 0.9 * first_ref[...] + 0.1 * grad
    new_second = 0.999 * second_ref[...] + 0.001 * grad * grad
    step = new_first * (0.5 / (1.0 - 0.9**ADAM_STEP))
    second_hat = new_second * (1.0 / (1.0 - 0.999**ADAM_STEP))
    out_logits_ref[...] = logits_ref[...] - step / (jnp.sqrt(second_hat) + 1e-08)
    out_first_ref[...] = new_first
    out_second_ref[...] = new_second


def swap(value, axes):
    return lax.all_to_all(value, axes, 0, 0, tiled=True)


def cross(value, axis):
    return lax.ppermute(value, axis, [(0, 1), (1, 0)])


def answers(src):
    shape = jax.ShapeDtypeStruct
    shards = src.shape[0] // CHUNKS * CORES
    tall, wide = V * V // MODS, V * MODS
    return call(
        answer_kernel,
        (
            shape((wide, tall), F32),
            shape((wide, tall), LOW),
            shape((shards, 3, V, LANES), LOW),
            shape((shards // 2, MODS, tall, 2 * LANES), LOW),
        ),
        (src,),
        [VMEM],
    )


def backward(scale, table, pairs, base, other):
    shards = table.shape[0]
    tall, wide = V * V // MODS, V * MODS
    return call(
        lambda *refs: backward_kernel(scale, *refs),
        jax.ShapeDtypeStruct((shards // CORES * CHUNKS, CORES, 3, SUB, LANES), LOW),
        (table, pairs, base, other),
        [VMEM] * 4,
        [
            pltpu.VMEM((wide, tall), LOW),
            pltpu.VMEM((MODS, tall, wide), LOW),
            pltpu.VMEM((V, 2 * LANES), F32),
            pltpu.VMEM((2, 8 * V, LANES), F32),
        ],
    )


def shards(logits, first_moment, second_moment, targets, triples):
    rows, cols = logits.shape
    margs, cells = targets.shape
    attrs = cols // V
    groups = lax.axis_size(MARG_AXES)
    scale = cells / (rows * lax.axis_size(ROW_AXES))
    shape = jax.ShapeDtypeStruct
    tall, wide = V * V // MODS, V * MODS
    place = lax.axis_index(PLACE_AXES).astype(jnp.int32).reshape(1)
    side = lax.axis_index("h").astype(jnp.int32).reshape(1)
    probs, copies = call(
        relax_kernel,
        (shape((V, attrs, rows), F32), shape((groups, attrs, (SUB + 1) * LANES), LOW)),
        (side, place, stay(triples.T), stay(logits)),
        [SMEM, SMEM, ANY, ANY],
        [
            pltpu.VMEM((SUB, LANES), F32),
            pltpu.VMEM((3, margs), jnp.int32),
            pltpu.VMEM((rows, cols), F32),
            pltpu.VMEM((cols, rows), F32),
            pltpu.SemaphoreType.DMA((3,)),
        ],
    )
    full = swap(copies, MARG_AXES)
    places = margs // CORES * CHUNKS
    lines = [pltpu.VMEM((places * 3 * SUB, LANES), F32)]
    other_full = cross(full, "c")
    mine, attributes = call(
        select_kernel,
        (shape((places, 3, SUB, LANES), LOW), shape((SUB, LANES), F32)),
        (full,),
        [VMEM],
        lines,
    )
    picked = call(
        merge_kernel,
        shape((places, CORES, 3, SUB, LANES), LOW),
        (attributes, mine, other_full),
        [VMEM] * 3,
        lines,
    )
    own, send, table, pairs = answers(swap(picked, SHARE_AXES))
    other = cross(send, "u")
    base = call(
        lambda *refs: base_kernel(scale, *refs),
        shape((wide, tall), F32),
        (place, own, stay(targets)),
        [SMEM, VMEM, ANY],
        [pltpu.VMEM((8, cells), F32), pltpu.VMEM((tall, wide), F32), pltpu.SemaphoreType.DMA],
    )
    returned = swap(backward(scale, table, pairs, base, other), SHARE_AXES)
    given, kept = [
        call(
            lambda *refs, core=core: collect_kernel(core, *refs),
            shape((groups * attrs, SUB * LANES), kind),
            (attributes, returned),
            [VMEM, VMEM],
            lines,
        )
        for core, kind in ((1, LOW), (0, F32))
    ]
    totals = call(
        join_kernel, shape((groups, attrs, SUB * LANES), LOW), (kept, cross(given, "c")), [VMEM, VMEM]
    )
    return call(
        adam_kernel,
        (shape((rows, cols), F32),) * 3,
        (swap(totals, MARG_AXES), probs, logits, first_moment, second_moment),
        [VMEM] * 5,
        [pltpu.VMEM((cols, rows), F32)],
    )


def solution(mesh):
    fine = Mesh(mesh.devices.reshape(PARTS), NAMES)
    table = P(ROW_AXES, MARG_AXES)
    listed = P(MARG_AXES, None)
    return jax.shard_map(
        shards,
        mesh=fine,
        in_specs=(table, table, table, listed, listed),
        out_specs=(table, table, table),
        check_vma=False,
    )
```

```python
import jax
import jax.numpy as jnp
from jax import lax
from jax.experimental import pallas as pl
from jax.experimental.pallas import tpu as pltpu
from jax.sharding import Mesh, PartitionSpec as P

V = 32
ADAM_STEP = 4
PARTS = (4, 2, 2, 2, 4, 2)
NAMES = ("x", "u", "w", "c", "y", "h")
ROW_AXES = ("x", "u", "w", "c")
MARG_AXES = ("y", "h")
PLACE_AXES = ("c", "x", "w")
SHARE_AXES = ("x", "w", "y")
CORES = 2
CHUNKS = 4
CHUNK = 32
LANES = CHUNKS * CHUNK
SUB = V // CHUNKS
MODS = 4
MARGS = 8
VMEM = pl.BlockSpec(memory_space=pltpu.VMEM)
SMEM = pl.BlockSpec(memory_space=pltpu.SMEM)
ANY = pl.BlockSpec(memory_space=pl.ANY)
LIMIT = 20 * 1024 * 1024
F32 = jnp.float32
LOW = jnp.bfloat16


def call(body, out_shape, operands, specs, scratch=()):
    return pl.pallas_call(
        body,
        out_shape=out_shape,
        in_specs=specs,
        out_specs=jax.tree.map(lambda unused: VMEM, out_shape),
        scratch_shapes=scratch,
        compiler_params=pltpu.CompilerParams(vmem_limit_bytes=LIMIT),
    )(*operands)


def exchange(blocks):
    lane = lax.broadcasted_iota(jnp.int32, blocks[0].shape, 1)
    blocks = list(blocks)
    for width, pairs in ((2 * CHUNK, ((0, 2), (1, 3))), (CHUNK, ((0, 1), (2, 3)))):
        low_part = (lane // width) % 2 == 0
        for a, b in pairs:
            left, right = blocks[a], blocks[b]
            blocks[a] = jnp.where(low_part, left, pltpu.roll(right, width, 1))
            blocks[b] = jnp.where(low_part, pltpu.roll(left, LANES - width, 1), right)
    return blocks


def stay(value):
    return pltpu.with_memory_space_constraint(value, pltpu.HBM)


def relax_kernel(
    side_ref,
    place_ref,
    triples_hbm,
    logits_hbm,
    probs_ref,
    send_ref,
    tile_ref,
    triples_ref,
    logits_ref,
    flipped_ref,
    sems,
):
    logits_copy = pltpu.make_async_copy(logits_hbm, logits_ref, sems.at[0])
    triples_copy = pltpu.make_async_copy(triples_hbm, triples_ref, sems.at[1])
    triples_copy.start()
    logits_copy.start()
    attrs = probs_ref.shape[1]
    halves = send_ref.shape[0] // CHUNKS
    triples_copy.wait()
    tile_ref[...] = jnp.zeros(tile_ref.shape, F32)
    tile_ref[0:3, 0 : triples_ref.shape[1]] = triples_ref[...].astype(F32)
    both = tile_ref[...]
    first_core = jnp.where(place_ref[0] < MARGS, 1.0, 0.0)
    kept = both * first_core + pltpu.roll(both, LANES - MARGS, 1) * (1.0 - first_core)
    kept = jnp.where(lax.broadcasted_iota(jnp.int32, kept.shape, 1) < MARGS, kept, 0.0)
    for half in range(halves):
        tile = (kept * jnp.where(side_ref[0] == half, 1.0, 0.0)).astype(LOW)
        for chunk in range(CHUNKS):
            send_ref[chunk * halves + half, :, SUB * LANES :] = tile
    logits_copy.wait()
    flipped_ref[...] = logits_ref[...].T
    values = [flipped_ref[pl.ds(value, attrs, stride=V), :] for value in range(V)]
    top = values[0]
    for value in values[1:]:
        top = jnp.maximum(top, value)
    expos = [jnp.exp(value - top) for value in values]
    total = expos[0]
    for expo in expos[1:]:
        total = total + expo
    scale = 1.0 / total
    probs = [expo * scale for expo in expos]
    for value in range(V):
        probs_ref[value] = probs[value]
    for rest in range(SUB):
        for chunk, packed in enumerate(exchange([probs[part * SUB + rest] for part in range(CHUNKS)])):
            low = packed.astype(LOW)
            for half in range(halves):
                send_ref[chunk * halves + half, :, rest * LANES : (rest + 1) * LANES] = low


def one_hot(triples, which, count):
    width = CHUNKS * MARGS
    row = jnp.broadcast_to(triples[which : which + 1, 0:width], (count, width))
    attr = lax.broadcasted_iota(jnp.int32, (count, width), 0).astype(F32)
    return jnp.where(row == attr, 1.0, 0.0).astype(LOW)


def tile_rows(which, rest, gap):
    for chunk in range(CHUNKS):
        rows = pl.ds(chunk * gap + which * SUB + rest, MARGS, stride=CHUNKS * gap)
        yield rows, chunk * MARGS


def pick(triples, table_ref, picked_ref):
    groups, attrs = table_ref.shape[0], table_ref.shape[1]
    parts = [table_ref[index].astype(F32)[:, 0 : SUB * LANES] for index in range(groups)]
    table = jnp.concatenate(parts, axis=0).astype(LOW)
    for which in range(3):
        mine = one_hot(triples, which, groups * attrs)
        picked = lax.dot_general(mine, table, (((0,), (0,)), ((), ())), preferred_element_type=F32)
        for rest in range(SUB):
            for rows, place in tile_rows(which, rest, 3 * SUB):
                picked_ref[rows, :] = picked[place : place + MARGS, rest * LANES : (rest + 1) * LANES]
    return picked_ref[...].reshape(CHUNKS * MARGS, 3, SUB, LANES).astype(LOW)


def select_kernel(full_ref, mine_ref, triples_ref, picked_ref):
    halves = full_ref.shape[0] // CHUNKS
    triples = jnp.zeros(triples_ref.shape, F32)
    for chunk in range(CHUNKS):
        tile = jnp.zeros(triples_ref.shape, F32)
        for half in range(halves):
            tile += full_ref[chunk * halves + half, :, SUB * LANES :].astype(F32)
        triples += pltpu.roll(tile, chunk * MARGS, 1) if chunk else tile
    triples_ref[...] = triples
    mine_ref[...] = pick(triples, full_ref, picked_ref)


def merge_kernel(triples_ref, mine_ref, other_ref, send_ref, picked_ref):
    theirs = pick(triples_ref[...], other_ref, picked_ref)
    for place in range(send_ref.shape[0]):
        send_ref[place, 0] = mine_ref[place]
        send_ref[place, 1] = theirs[place]


def unpack(src_ref, place, core):
    packed = [src_ref[place * CHUNKS + chunk, core].astype(F32).reshape(3 * SUB, LANES) for chunk in range(CHUNKS)]
    parts = exchange(packed)
    return [
        jnp.concatenate([part[which * SUB : (which + 1) * SUB, :] for part in parts], axis=0) for which in range(3)
    ]


def answer_kernel(src_ref, own_ref, send_ref, table_ref, pairs_ref):
    shards = table_ref.shape[0]

    def fill(step):
        for part in range(2):
            shard = 2 * step + part
            first, second, third = [value.astype(LOW) for value in unpack(src_ref, step, part)]
            table_ref[shard, 0] = first
            table_ref[shard, 1] = second
            table_ref[shard, 2] = third
            for value in range(V):
                row = jnp.broadcast_to(second[value : value + 1, :], first.shape)
                mod, rest = value % MODS, value // MODS
                pairs_ref[step, mod, rest * V : (rest + 1) * V, part * LANES : (part + 1) * LANES] = first * row

    def add(step):
        third = jnp.concatenate([table_ref[2 * step, 2], table_ref[2 * step + 1, 2]], axis=1)
        for mod in range(MODS):
            own_ref[mod * V : (mod + 1) * V, :] += lax.dot_general(
                third, pairs_ref[step, mod], (((1,), (1,)), ((), ())), preferred_element_type=F32
            )

    own_ref[...] = jnp.zeros(own_ref.shape, F32)
    fill(0)

    def both(step, carry):
        add(step - 1)
        fill(step)
        return carry

    lax.fori_loop(1, shards // 2, both, 0, unroll=shards // 2 - 1)
    add(shards // 2 - 1)
    send_ref[...] = own_ref[...].astype(LOW)


def base_kernel(scale, place_ref, own_ref, targets_any, base_ref, block_ref, target_ref, sem):
    place = place_ref[0]
    start = pl.multiple_of(place // 8 * 8, 8)
    copy = pltpu.make_async_copy(targets_any.at[pl.ds(start, 8), :], block_ref, sem)
    copy.start()
    copy.wait()
    mine = lax.broadcasted_iota(jnp.int32, (8, LANES), 0) == lax.rem(place, 8)
    for rest in range(SUB):
        for value in range(V):
            tile = block_ref[:, pl.ds((value * SUB + rest) * LANES, LANES)]
            row = jnp.sum(jnp.where(mine, tile, 0.0), axis=0, keepdims=True)
            target_ref[pl.ds(rest * V + value, 1), :] = row
    base_ref[...] = scale * own_ref[...] - target_ref[...].T


def backward_kernel(scale, table_ref, pairs_ref, base_ref, other_ref, out_ref, low_ref, mask_ref, row_ref, sum_ref):
    steps = pairs_ref.shape[0]
    wide = 2 * LANES
    resid = base_ref[...] + scale * other_ref[...].astype(F32)
    low_ref[...] = resid.astype(LOW)
    flipped = resid.T
    lane_mod = lax.broadcasted_iota(jnp.int32, flipped.shape, 1) // V
    for mod in range(MODS):
        mask_ref[mod] = jnp.where(lane_mod == mod, flipped, 0.0).astype(LOW)

    def step(index, carry):
        pair = [
            jnp.concatenate([table_ref[2 * index, which], table_ref[2 * index + 1, which]], axis=1)
            for which in range(3)
        ]
        first = pair[0].astype(F32)
        row_ref[...] = pair[1].astype(F32)
        stacked = jnp.concatenate([pair[2]] * MODS, axis=0)
        third_grad = jnp.zeros((V, wide), F32)
        first_grad = jnp.zeros((V, wide), F32)
        for mod in range(MODS):
            third_grad += jnp.dot(
                low_ref[mod * V : (mod + 1) * V, :], pairs_ref[index, mod], preferred_element_type=F32
            )
            cross = jnp.dot(mask_ref[mod], stacked, preferred_element_type=F32)
            for rest in range(SUB):
                value = rest * MODS + mod
                block = cross[rest * V : (rest + 1) * V, :]
                first_grad += block * row_ref[pl.ds(value, 1), :]
                product = block * first
                partial = product[0:8]
                for part in range(1, V // 8):
                    partial += product[8 * part : 8 * part + 8]
                for half in range(2):
                    sum_ref[half, value * 8 : value * 8 + 8, :] = partial[:, half * LANES : (half + 1) * LANES]
        mean = jnp.sum(first * first_grad, axis=0, keepdims=True)
        for half in range(2):
            lanes = slice(half * LANES, (half + 1) * LANES)
            second_grad = jnp.zeros((V, LANES), F32)
            for part in range(8):
                second_grad += sum_ref[half, pl.ds(part, V, stride=8), :]
            centre = jnp.broadcast_to(mean[:, lanes], (V, LANES))
            grads = [grad - centre for grad in (first_grad[:, lanes], second_grad, third_grad[:, lanes])]
            parts = [
                jnp.concatenate([grad[part * SUB : (part + 1) * SUB, :] for grad in grads], axis=0)
                for part in range(CHUNKS)
            ]
            for chunk, packed in enumerate(exchange(parts)):
                out_ref[index * CHUNKS + chunk, half] = packed.reshape(3, SUB, LANES).astype(LOW)
        return carry

    lax.fori_loop(0, steps, step, 0, unroll=steps)


def collect_kernel(core, triples_ref, grads_ref, total_ref, grad_ref):
    attrs = total_ref.shape[0]
    triples = triples_ref[...]
    grad_ref[...] = grads_ref[:, core].astype(F32).reshape(grad_ref.shape)
    total = jnp.zeros(total_ref.shape, F32)
    for which in range(3):
        parts = []
        for rest in range(SUB):
            tiles = [grad_ref[rows, :] for rows, unused in tile_rows(which, rest, 3 * SUB)]
            parts.append(jnp.concatenate(tiles, axis=0))
        grads = jnp.concatenate(parts, axis=1).astype(LOW)
        total += jnp.dot(one_hot(triples, which, attrs), grads, preferred_element_type=F32)
    total_ref[...] = total.astype(total_ref.dtype)


def join_kernel(own_ref, other_ref, send_ref):
    groups, attrs = send_ref.shape[0], send_ref.shape[1]
    total = own_ref[...] + other_ref[...].astype(F32)
    for index in range(groups):
        send_ref[index] = total[index * attrs : (index + 1) * attrs, :].astype(LOW)


def adam_kernel(
    parts_ref, probs_ref, logits_ref, first_ref, second_ref, out_logits_ref, out_first_ref, out_second_ref, grad_ref
):
    groups, attrs = parts_ref.shape[0], parts_ref.shape[1]
    halves = groups // CHUNKS
    chunks = []
    for chunk in range(CHUNKS):
        total = parts_ref[chunk * halves].astype(F32)
        for half in range(1, halves):
            total += parts_ref[chunk * halves + half].astype(F32)
        chunks.append(total)
    row_grad = [None] * V
    for rest in range(SUB):
        blocks = [chunk[:, rest * LANES : (rest + 1) * LANES] for chunk in chunks]
        for part, block in enumerate(exchange(blocks)):
            row_grad[part * SUB + rest] = block
    inner = jnp.zeros((attrs, LANES), F32)
    for value in range(V):
        inner += probs_ref[value] * row_grad[value]
    for value in range(V):
        grad_ref[pl.ds(value, attrs, stride=V), :] = 512.0 * probs_ref[value] * (row_grad[value] - inner)
    grad = grad_ref[...].T
    new_first = 0.9 * first_ref[...] + 0.1 * grad
    new_second = 0.999 * second_ref[...] + 0.001 * grad * grad
    step = new_first * (0.5 / (1.0 - 0.9**ADAM_STEP))
    second_hat = new_second * (1.0 / (1.0 - 0.999**ADAM_STEP))
    out_logits_ref[...] = logits_ref[...] - step / (jnp.sqrt(second_hat) + 1e-08)
    out_first_ref[...] = new_first
    out_second_ref[...] = new_second


def swap(value, axes):
    return lax.all_to_all(value, axes, 0, 0, tiled=True)


def cross(value, axis):
    return lax.ppermute(value, axis, [(0, 1), (1, 0)])


def answers(src):
    shape = jax.ShapeDtypeStruct
    shards = src.shape[0] // CHUNKS * CORES
    tall, wide = V * V // MODS, V * MODS
    return call(
        answer_kernel,
        (
            shape((wide, tall), F32),
            shape((wide, tall), LOW),
            shape((shards, 3, V, LANES), LOW),
            shape((shards // 2, MODS, tall, 2 * LANES), LOW),
        ),
        (src,),
        [VMEM],
    )


def backward(scale, table, pairs, base, other):
    shards = table.shape[0]
    tall, wide = V * V // MODS, V * MODS
    return call(
        lambda *refs: backward_kernel(scale, *refs),
        jax.ShapeDtypeStruct((shards // CORES * CHUNKS, CORES, 3, SUB, LANES), LOW),
        (table, pairs, base, other),
        [VMEM] * 4,
        [
            pltpu.VMEM((wide, tall), LOW),
            pltpu.VMEM((MODS, tall, wide), LOW),
            pltpu.VMEM((V, 2 * LANES), F32),
            pltpu.VMEM((2, 8 * V, LANES), F32),
        ],
    )


def shards(logits, first_moment, second_moment, targets, triples):
    rows, cols = logits.shape
    margs, cells = targets.shape
    attrs = cols // V
    groups = lax.axis_size(MARG_AXES)
    scale = cells / (rows * lax.axis_size(ROW_AXES))
    shape = jax.ShapeDtypeStruct
    tall, wide = V * V // MODS, V * MODS
    place = lax.axis_index(PLACE_AXES).astype(jnp.int32).reshape(1)
    side = lax.axis_index("h").astype(jnp.int32).reshape(1)
    probs, copies = call(
        relax_kernel,
        (shape((V, attrs, rows), F32), shape((groups, attrs, (SUB + 1) * LANES), LOW)),
        (side, place, stay(triples.T), stay(logits)),
        [SMEM, SMEM, ANY, ANY],
        [
            pltpu.VMEM((SUB, LANES), F32),
            pltpu.VMEM((3, margs), jnp.int32),
            pltpu.VMEM((rows, cols), F32),
            pltpu.VMEM((cols, rows), F32),
            pltpu.SemaphoreType.DMA((2,)),
        ],
    )
    full = swap(copies, MARG_AXES)
    places = margs // CORES * CHUNKS
    lines = [pltpu.VMEM((places * 3 * SUB, LANES), F32)]
    other_full = cross(full, "c")
    mine, attributes = call(
        select_kernel,
        (shape((places, 3, SUB, LANES), LOW), shape((SUB, LANES), F32)),
        (full,),
        [VMEM],
        lines,
    )
    picked = call(
        merge_kernel,
        shape((places, CORES, 3, SUB, LANES), LOW),
        (attributes, mine, other_full),
        [VMEM] * 3,
        lines,
    )
    own, send, table, pairs = answers(swap(picked, SHARE_AXES))
    other = cross(send, "u")
    base = call(
        lambda *refs: base_kernel(scale, *refs),
        shape((wide, tall), F32),
        (place, own, stay(targets)),
        [SMEM, VMEM, ANY],
        [pltpu.VMEM((8, cells), F32), pltpu.VMEM((tall, wide), F32), pltpu.SemaphoreType.DMA],
    )
    returned = swap(backward(scale, table, pairs, base, other), SHARE_AXES)
    given, kept = [
        call(
            lambda *refs, core=core: collect_kernel(core, *refs),
            shape((groups * attrs, SUB * LANES), kind),
            (attributes, returned),
            [VMEM, VMEM],
            lines,
        )
        for core, kind in ((1, LOW), (0, F32))
    ]
    totals = call(
        join_kernel, shape((groups, attrs, SUB * LANES), LOW), (kept, cross(given, "c")), [VMEM, VMEM]
    )
    return call(
        adam_kernel,
        (shape((rows, cols), F32),) * 3,
        (swap(totals, MARG_AXES), probs, logits, first_moment, second_moment),
        [VMEM] * 5,
        [pltpu.VMEM((cols, rows), F32)],
    )


def solution(mesh):
    fine = Mesh(mesh.devices.reshape(PARTS), NAMES)
    table = P(ROW_AXES, MARG_AXES)
    listed = P(MARG_AXES, None)
    return jax.shard_map(
        shards,
        mesh=fine,
        in_specs=(table, table, table, listed, listed),
        out_specs=(table, table, table),
        check_vma=False,
    )
```

```python
import jax
import jax.numpy as jnp
from jax import lax
from jax.experimental import pallas as pl
from jax.experimental.pallas import tpu as pltpu
from jax.sharding import Mesh, PartitionSpec as P

V = 32
ADAM_STEP = 4
PARTS = (4, 2, 2, 2, 4, 2)
NAMES = ("x", "u", "w", "c", "y", "h")
ROW_AXES = ("x", "u", "w", "c")
MARG_AXES = ("y", "h")
PLACE_AXES = ("c", "x", "w")
SHARE_AXES = ("x", "w", "y")
CORES = 2
CHUNKS = 4
CHUNK = 32
LANES = CHUNKS * CHUNK
SUB = V // CHUNKS
MODS = 4
MARGS = 8
VMEM = pl.BlockSpec(memory_space=pltpu.VMEM)
SMEM = pl.BlockSpec(memory_space=pltpu.SMEM)
ANY = pl.BlockSpec(memory_space=pl.ANY)
LIMIT = 20 * 1024 * 1024
F32 = jnp.float32
LOW = jnp.bfloat16


def call(body, out_shape, operands, specs, scratch=()):
    return pl.pallas_call(
        body,
        out_shape=out_shape,
        in_specs=specs,
        out_specs=jax.tree.map(lambda unused: VMEM, out_shape),
        scratch_shapes=scratch,
        compiler_params=pltpu.CompilerParams(vmem_limit_bytes=LIMIT),
    )(*operands)


def exchange(blocks):
    lane = lax.broadcasted_iota(jnp.int32, blocks[0].shape, 1)
    blocks = list(blocks)
    for width, pairs in ((2 * CHUNK, ((0, 2), (1, 3))), (CHUNK, ((0, 1), (2, 3)))):
        low_part = (lane // width) % 2 == 0
        for a, b in pairs:
            left, right = blocks[a], blocks[b]
            blocks[a] = jnp.where(low_part, left, pltpu.roll(right, width, 1))
            blocks[b] = jnp.where(low_part, pltpu.roll(left, LANES - width, 1), right)
    return blocks


def stay(value):
    return pltpu.with_memory_space_constraint(value, pltpu.HBM)


def relax_kernel(
    side_ref,
    place_ref,
    triples_hbm,
    logits_hbm,
    probs_ref,
    send_ref,
    tile_ref,
    triples_ref,
    logits_ref,
    flipped_ref,
    sems,
):
    logits_copy = pltpu.make_async_copy(logits_hbm, logits_ref, sems.at[0])
    triples_copy = pltpu.make_async_copy(triples_hbm, triples_ref, sems.at[1])
    logits_copy.start()
    triples_copy.start()
    logits_copy.wait()
    flipped_ref[...] = logits_ref[...].T
    attrs = probs_ref.shape[1]
    halves = send_ref.shape[0] // CHUNKS
    values = [flipped_ref[pl.ds(value, attrs, stride=V), :] for value in range(V)]
    top = values[0]
    for value in values[1:]:
        top = jnp.maximum(top, value)
    expos = [jnp.exp(value - top) for value in values]
    total = expos[0]
    for expo in expos[1:]:
        total = total + expo
    probs = [expo / total for expo in expos]
    for value in range(V):
        probs_ref[value] = probs[value]
    for rest in range(SUB):
        for chunk, packed in enumerate(exchange([probs[part * SUB + rest] for part in range(CHUNKS)])):
            low = packed.astype(LOW)
            for half in range(halves):
                send_ref[chunk * halves + half, :, rest * LANES : (rest + 1) * LANES] = low
    triples_copy.wait()
    tile_ref[...] = jnp.zeros(tile_ref.shape, F32)
    tile_ref[0:3, 0 : triples_ref.shape[1]] = triples_ref[...].astype(F32)
    both = tile_ref[...]
    first_core = jnp.where(place_ref[0] < MARGS, 1.0, 0.0)
    kept = both * first_core + pltpu.roll(both, LANES - MARGS, 1) * (1.0 - first_core)
    kept = jnp.where(lax.broadcasted_iota(jnp.int32, kept.shape, 1) < MARGS, kept, 0.0)
    for half in range(halves):
        tile = (kept * jnp.where(side_ref[0] == half, 1.0, 0.0)).astype(LOW)
        for chunk in range(CHUNKS):
            send_ref[chunk * halves + half, :, SUB * LANES :] = tile


def one_hot(triples, count):
    width = CHUNKS * MARGS
    row = jnp.concatenate([triples[which : which + 1, 0:width] for which in range(3)], axis=1)
    row = jnp.broadcast_to(row, (count, 3 * width))
    attr = lax.broadcasted_iota(jnp.int32, (count, 3 * width), 0).astype(F32)
    return jnp.where(row == attr, 1.0, 0.0).astype(LOW)


def tile_rows(which, rest, gap):
    for chunk in range(CHUNKS):
        rows = pl.ds(chunk * gap + which * SUB + rest, MARGS, stride=CHUNKS * gap)
        yield rows, chunk * MARGS


def pick(triples, table_ref, picked_ref):
    groups, attrs = table_ref.shape[0], table_ref.shape[1]
    parts = [table_ref[index].astype(F32)[:, 0 : SUB * LANES] for index in range(groups)]
    table = jnp.concatenate(parts, axis=0).astype(LOW)
    mine = one_hot(triples, groups * attrs)
    picked = lax.dot_general(mine, table, (((0,), (0,)), ((), ())), preferred_element_type=F32)
    for which in range(3):
        for rest in range(SUB):
            for rows, place in tile_rows(which, rest, 3 * SUB):
                start = which * CHUNKS * MARGS + place
                picked_ref[rows, :] = picked[start : start + MARGS, rest * LANES : (rest + 1) * LANES]
    return picked_ref[...].reshape(CHUNKS * MARGS, 3, SUB, LANES).astype(LOW)


def select_kernel(full_ref, mine_ref, triples_ref, picked_ref):
    halves = full_ref.shape[0] // CHUNKS
    triples = jnp.zeros(triples_ref.shape, F32)
    for chunk in range(CHUNKS):
        tile = jnp.zeros(triples_ref.shape, F32)
        for half in range(halves):
            tile += full_ref[chunk * halves + half, :, SUB * LANES :].astype(F32)
        triples += pltpu.roll(tile, chunk * MARGS, 1) if chunk else tile
    triples_ref[...] = triples
    mine_ref[...] = pick(triples, full_ref, picked_ref)


def merge_kernel(triples_ref, mine_ref, other_ref, send_ref, picked_ref):
    theirs = pick(triples_ref[...], other_ref, picked_ref)
    for place in range(send_ref.shape[0]):
        send_ref[place, 0] = mine_ref[place]
        send_ref[place, 1] = theirs[place]


def unpack(src_ref, place, core):
    packed = [src_ref[place * CHUNKS + chunk, core].astype(F32).reshape(3 * SUB, LANES) for chunk in range(CHUNKS)]
    parts = exchange(packed)
    return [
        jnp.concatenate([part[which * SUB : (which + 1) * SUB, :] for part in parts], axis=0) for which in range(3)
    ]


def answer_kernel(src_ref, own_ref, send_ref, table_ref, pairs_ref):
    shards = table_ref.shape[0]

    def fill(step):
        for part in range(2):
            shard = 2 * step + part
            first, second, third = [value.astype(LOW) for value in unpack(src_ref, step, part)]
            table_ref[shard, 0] = first
            table_ref[shard, 1] = second
            table_ref[shard, 2] = third
            for value in range(V):
                row = jnp.broadcast_to(second[value : value + 1, :], first.shape)
                mod, rest = value % MODS, value // MODS
                pairs_ref[step, mod, rest * V : (rest + 1) * V, part * LANES : (part + 1) * LANES] = first * row

    def add(step):
        third = jnp.concatenate([table_ref[2 * step, 2], table_ref[2 * step + 1, 2]], axis=1)
        for mod in range(MODS):
            own_ref[mod * V : (mod + 1) * V, :] += lax.dot_general(
                third, pairs_ref[step, mod], (((1,), (1,)), ((), ())), preferred_element_type=F32
            )

    own_ref[...] = jnp.zeros(own_ref.shape, F32)
    fill(0)

    def both(step, carry):
        add(step - 1)
        fill(step)
        return carry

    lax.fori_loop(1, shards // 2, both, 0, unroll=shards // 2 - 1)
    add(shards // 2 - 1)
    send_ref[...] = own_ref[...].astype(LOW)


def base_kernel(scale, place_ref, own_ref, targets_any, base_ref, block_ref, target_ref, sem):
    place = place_ref[0]
    start = pl.multiple_of(place // 8 * 8, 8)
    copy = pltpu.make_async_copy(targets_any.at[pl.ds(start, 8), :], block_ref, sem)
    copy.start()
    copy.wait()
    mine = lax.broadcasted_iota(jnp.int32, (8, LANES), 0) == lax.rem(place, 8)
    for rest in range(SUB):
        for value in range(V):
            tile = block_ref[:, pl.ds((value * SUB + rest) * LANES, LANES)]
            row = jnp.sum(jnp.where(mine, tile, 0.0), axis=0, keepdims=True)
            target_ref[pl.ds(rest * V + value, 1), :] = row
    base_ref[...] = scale * own_ref[...] - target_ref[...].T


def backward_kernel(scale, table_ref, pairs_ref, base_ref, other_ref, out_ref, low_ref, mask_ref, row_ref, sum_ref):
    steps = pairs_ref.shape[0]
    wide = 2 * LANES
    resid = base_ref[...] + scale * other_ref[...].astype(F32)
    low_ref[...] = resid.astype(LOW)
    flipped = resid.T
    lane_mod = lax.broadcasted_iota(jnp.int32, flipped.shape, 1) // V
    for mod in range(MODS):
        mask_ref[mod] = jnp.where(lane_mod == mod, flipped, 0.0).astype(LOW)

    def step(index, carry):
        pair = [
            jnp.concatenate([table_ref[2 * index, which], table_ref[2 * index + 1, which]], axis=1)
            for which in range(3)
        ]
        first = pair[0].astype(F32)
        row_ref[...] = pair[1].astype(F32)
        stacked = jnp.concatenate([pair[2]] * MODS, axis=0)
        third_grad = jnp.zeros((V, wide), F32)
        first_grad = jnp.zeros((V, wide), F32)
        for mod in range(MODS):
            third_grad += jnp.dot(
                low_ref[mod * V : (mod + 1) * V, :], pairs_ref[index, mod], preferred_element_type=F32
            )
            cross = jnp.dot(mask_ref[mod], stacked, preferred_element_type=F32)
            for rest in range(SUB):
                value = rest * MODS + mod
                block = cross[rest * V : (rest + 1) * V, :]
                first_grad += block * row_ref[pl.ds(value, 1), :]
                product = block * first
                partial = product[0:8]
                for part in range(1, V // 8):
                    partial += product[8 * part : 8 * part + 8]
                for half in range(2):
                    sum_ref[half, value * 8 : value * 8 + 8, :] = partial[:, half * LANES : (half + 1) * LANES]
        mean = jnp.sum(first * first_grad, axis=0, keepdims=True)
        for half in range(2):
            lanes = slice(half * LANES, (half + 1) * LANES)
            second_grad = jnp.zeros((V, LANES), F32)
            for part in range(8):
                second_grad += sum_ref[half, pl.ds(part, V, stride=8), :]
            centre = jnp.broadcast_to(mean[:, lanes], (V, LANES))
            grads = [grad - centre for grad in (first_grad[:, lanes], second_grad, third_grad[:, lanes])]
            parts = [
                jnp.concatenate([grad[part * SUB : (part + 1) * SUB, :] for grad in grads], axis=0)
                for part in range(CHUNKS)
            ]
            for chunk, packed in enumerate(exchange(parts)):
                out_ref[index * CHUNKS + chunk, half] = packed.reshape(3, SUB, LANES).astype(LOW)
        return carry

    lax.fori_loop(0, steps, step, 0, unroll=steps)


def collect_kernel(core, triples_ref, grads_ref, total_ref, grad_ref):
    attrs = total_ref.shape[0]
    triples = triples_ref[...]
    grad_ref[...] = grads_ref[:, core].astype(F32).reshape(grad_ref.shape)
    parts = []
    for rest in range(SUB):
        tiles = [grad_ref[rows, :] for which in range(3) for rows, unused in tile_rows(which, rest, 3 * SUB)]
        parts.append(jnp.concatenate(tiles, axis=0))
    grads = jnp.concatenate(parts, axis=1).astype(LOW)
    total = jnp.dot(one_hot(triples, attrs), grads, preferred_element_type=F32)
    total_ref[...] = total.astype(total_ref.dtype)


def join_kernel(own_ref, other_ref, send_ref):
    groups, attrs = send_ref.shape[0], send_ref.shape[1]
    total = own_ref[...] + other_ref[...].astype(F32)
    for index in range(groups):
        send_ref[index] = total[index * attrs : (index + 1) * attrs, :].astype(LOW)


def adam_kernel(
    parts_ref, probs_ref, logits_ref, first_ref, second_ref, out_logits_ref, out_first_ref, out_second_ref, grad_ref
):
    groups, attrs = parts_ref.shape[0], parts_ref.shape[1]
    halves = groups // CHUNKS
    chunks = []
    for chunk in range(CHUNKS):
        total = parts_ref[chunk * halves].astype(F32)
        for half in range(1, halves):
            total += parts_ref[chunk * halves + half].astype(F32)
        chunks.append(total)
    row_grad = [None] * V
    for rest in range(SUB):
        blocks = [chunk[:, rest * LANES : (rest + 1) * LANES] for chunk in chunks]
        for part, block in enumerate(exchange(blocks)):
            row_grad[part * SUB + rest] = block
    inner = jnp.zeros((attrs, LANES), F32)
    for value in range(V):
        inner += probs_ref[value] * row_grad[value]
    for value in range(V):
        grad_ref[pl.ds(value, attrs, stride=V), :] = 512.0 * probs_ref[value] * (row_grad[value] - inner)
    grad = grad_ref[...].T
    new_first = 0.9 * first_ref[...] + 0.1 * grad
    new_second = 0.999 * second_ref[...] + 0.001 * grad * grad
    first_hat = new_first / (1.0 - 0.9**ADAM_STEP)
    second_hat = new_second / (1.0 - 0.999**ADAM_STEP)
    out_logits_ref[...] = logits_ref[...] - 0.5 * first_hat / (jnp.sqrt(second_hat) + 1e-08)
    out_first_ref[...] = new_first
    out_second_ref[...] = new_second


def swap(value, axes):
    return lax.all_to_all(value, axes, 0, 0, tiled=True)


def cross(value, axis):
    return lax.ppermute(value, axis, [(0, 1), (1, 0)])


def answers(src):
    shape = jax.ShapeDtypeStruct
    shards = src.shape[0] // CHUNKS * CORES
    tall, wide = V * V // MODS, V * MODS
    return call(
        answer_kernel,
        (
            shape((wide, tall), F32),
            shape((wide, tall), LOW),
            shape((shards, 3, V, LANES), LOW),
            shape((shards // 2, MODS, tall, 2 * LANES), LOW),
        ),
        (src,),
        [VMEM],
    )


def backward(scale, table, pairs, base, other):
    shards = table.shape[0]
    tall, wide = V * V // MODS, V * MODS
    return call(
        lambda *refs: backward_kernel(scale, *refs),
        jax.ShapeDtypeStruct((shards // CORES * CHUNKS, CORES, 3, SUB, LANES), LOW),
        (table, pairs, base, other),
        [VMEM] * 4,
        [
            pltpu.VMEM((wide, tall), LOW),
            pltpu.VMEM((MODS, tall, wide), LOW),
            pltpu.VMEM((V, 2 * LANES), F32),
            pltpu.VMEM((2, 8 * V, LANES), F32),
        ],
    )


def shards(logits, first_moment, second_moment, targets, triples):
    rows, cols = logits.shape
    margs, cells = targets.shape
    attrs = cols // V
    groups = lax.axis_size(MARG_AXES)
    scale = cells / (rows * lax.axis_size(ROW_AXES))
    shape = jax.ShapeDtypeStruct
    tall, wide = V * V // MODS, V * MODS
    place = lax.axis_index(PLACE_AXES).astype(jnp.int32).reshape(1)
    side = lax.axis_index("h").astype(jnp.int32).reshape(1)
    probs, copies = call(
        relax_kernel,
        (shape((V, attrs, rows), F32), shape((groups, attrs, (SUB + 1) * LANES), LOW)),
        (side, place, stay(triples.T), stay(logits)),
        [SMEM, SMEM, ANY, ANY],
        [
            pltpu.VMEM((SUB, LANES), F32),
            pltpu.VMEM((3, margs), jnp.int32),
            pltpu.VMEM((rows, cols), F32),
            pltpu.VMEM((cols, rows), F32),
            pltpu.SemaphoreType.DMA((2,)),
        ],
    )
    full = swap(copies, MARG_AXES)
    places = margs // CORES * CHUNKS
    lines = [pltpu.VMEM((places * 3 * SUB, LANES), F32)]
    other_full = cross(full, "c")
    mine, attributes = call(
        select_kernel,
        (shape((places, 3, SUB, LANES), LOW), shape((SUB, LANES), F32)),
        (full,),
        [VMEM],
        lines,
    )
    picked = call(
        merge_kernel,
        shape((places, CORES, 3, SUB, LANES), LOW),
        (attributes, mine, other_full),
        [VMEM] * 3,
        lines,
    )
    own, send, table, pairs = answers(swap(picked, SHARE_AXES))
    other = cross(send, "u")
    base = call(
        lambda *refs: base_kernel(scale, *refs),
        shape((wide, tall), F32),
        (place, own, stay(targets)),
        [SMEM, VMEM, ANY],
        [pltpu.VMEM((8, cells), F32), pltpu.VMEM((tall, wide), F32), pltpu.SemaphoreType.DMA],
    )
    returned = swap(backward(scale, table, pairs, base, other), SHARE_AXES)
    given, kept = [
        call(
            lambda *refs, core=core: collect_kernel(core, *refs),
            shape((groups * attrs, SUB * LANES), kind),
            (attributes, returned),
            [VMEM, VMEM],
            lines,
        )
        for core, kind in ((1, LOW), (0, F32))
    ]
    totals = call(
        join_kernel, shape((groups, attrs, SUB * LANES), LOW), (kept, cross(given, "c")), [VMEM, VMEM]
    )
    return call(
        adam_kernel,
        (shape((rows, cols), F32),) * 3,
        (swap(totals, MARG_AXES), probs, logits, first_moment, second_moment),
        [VMEM] * 5,
        [pltpu.VMEM((cols, rows), F32)],
    )


def solution(mesh):
    fine = Mesh(mesh.devices.reshape(PARTS), NAMES)
    table = P(ROW_AXES, MARG_AXES)
    listed = P(MARG_AXES, None)
    return jax.shard_map(
        shards,
        mesh=fine,
        in_specs=(table, table, table, listed, listed),
        out_specs=(table, table, table),
        check_vma=False,
    )
```
